128 devices in a mesh: dp: 64 (over x_hi, z, y, core), fsdp: 2 (over x_lo).
Axes of the slice: x: 4 (x_hi: 2, x_lo: 2; x = x_hi * 2 + x_lo), y: 4, z: 4, core: 2. Of those that a mesh axis runs over, the one named last changes fastest.
Arguments:
- layer_input: bfloat16 [65536, 768], P(('dp', 'fsdp')), may hold values from -6 to 6
- prior_logits: bfloat16 [12, 65536, 512], P(None, ('dp', 'fsdp')), may hold values from -4 to 4
- bucket_counts: int32 [128, 4], P(('dp', 'fsdp')), may hold values from 0 to 4, as said below
- output_cotangent: bfloat16 [65536, 768], P(('dp', 'fsdp')), may hold values from -24 to 24
- logits_cotangent: bfloat16 [12, 65536, 512], P(None, ('dp', 'fsdp')), may hold values from -1.796875 to 1.796875
- query_kernel: bfloat16 [768, 768], P(None, ('dp', 'fsdp')), may hold values from -0.21875 to 0.21875
- query_offset: bfloat16 [768], P(('dp', 'fsdp')), may hold values from -3 to 3
- key_kernel: bfloat16 [768, 768], P(None, ('dp', 'fsdp')), may hold values from -0.21875 to 0.21875
- value_kernel: bfloat16 [768, 768], P(None, ('dp', 'fsdp')), may hold values from -0.21875 to 0.21875
- value_offset: bfloat16 [768], P(('dp', 'fsdp')), may hold values from -3 to 3
- output_kernel: bfloat16 [768, 768], P(None, ('dp', 'fsdp')), may hold values from -1.5 to 1.5
- output_offset: bfloat16 [768], P(('dp', 'fsdp')), may hold values from -1.796875 to 1.796875
- first_gain: bfloat16 [768], P(('dp', 'fsdp')), may hold values from 0.5 to 1.5
- first_shift: bfloat16 [768], P(('dp', 'fsdp')), may hold values from -1.796875 to 1.796875
- inner_kernel: bfloat16 [768, 3072], P(None, ('dp', 'fsdp')), may hold values from -0.21875 to 0.21875
- inner_offset: bfloat16 [3072], P(('dp', 'fsdp')), may hold values from -3 to 3
- outer_kernel: bfloat16 [3072, 768], P(None, ('dp', 'fsdp')), may hold values from -0.109375 to 0.109375
- outer_offset: bfloat16 [768], P(('dp', 'fsdp')), may hold values from -1.796875 to 1.796875
- second_gain: bfloat16 [768], P(('dp', 'fsdp')), may hold values from 0.5 to 1.5
- second_shift: bfloat16 [768], P(('dp', 'fsdp')), may hold values from -1.796875 to 1.796875
Outputs:
- layer_output: bfloat16 [65536, 768], P(('dp', 'fsdp'))
- raw_logits: bfloat16 [12, 65536, 512], P(None, ('dp', 'fsdp'))
- input_slope: bfloat16 [65536, 768], P(('dp', 'fsdp'))
- logits_slope: bfloat16 [12, 65536, 512], P(None, ('dp', 'fsdp'))
- query_kernel_slope: float32 [768, 768], P(None, ('dp', 'fsdp'))
- query_offset_slope: float32 [768], P(('dp', 'fsdp'))
- key_kernel_slope: float32 [768, 768], P(None, ('dp', 'fsdp'))
- value_kernel_slope: float32 [768, 768], P(None, ('dp', 'fsdp'))
- value_offset_slope: float32 [768], P(('dp', 'fsdp'))
- output_kernel_slope: float32 [768, 768], P(None, ('dp', 'fsdp'))
- output_offset_slope: float32 [768], P(('dp', 'fsdp'))
- first_gain_slope: float32 [768], P(('dp', 'fsdp'))
- first_shift_slope: float32 [768], P(('dp', 'fsdp'))
- inner_kernel_slope: float32 [768, 3072], P(None, ('dp', 'fsdp'))
- inner_offset_slope: float32 [3072], P(('dp', 'fsdp'))
- outer_kernel_slope: float32 [3072, 768], P(None, ('dp', 'fsdp'))
- outer_offset_slope: float32 [768], P(('dp', 'fsdp'))
- second_gain_slope: float32 [768], P(('dp', 'fsdp'))
- second_shift_slope: float32 [768], P(('dp', 'fsdp'))
The draws below stay inside these ranges and needn't reach their ends.
Inputs may be any that keep to these rules, and one draw needn't show every extreme that they name: `bucket_counts`: row d gives the counts of sequences of 128, 256, 384 and 512 tokens of block d; they fill its 512 rows exactly. Some block holds four sequences of 128 tokens.
All inputs are finite; a program needn't handle non-finite values.
Results may differ from the reference program's by a relative error of at most 0.013.
Values may be sent and summed in bfloat16 or wider, within the bound.
No kernel may reach another device: no remote copies, remote signals or barrier semaphores. Data moves between devices by JAX's collectives and lax.ppermute only.
A program may use at most 192 MiB of HBM per device.

```python
import jax
import jax.numpy as jnp
from jax import lax

D = 768
H = 12
HEAD = 64
FF = 3072
UNIT = 128
DEV_UNITS = 4
TOK_DEV = 512
TOKENS = 65536
N_DP = 64
N_FSDP = 2


def draw_bucket_counts(key, part):
    key = jax.random.fold_in(key, 11)
    first_key, second_key = jax.random.split(key)
    blocks = N_DP * N_FSDP
    patterns = jnp.array([[0, 0, 0, 1], [1, 0, 1, 0], [0, 2, 0, 0], [2, 1, 0, 0], [4, 0, 0, 0]], dtype=jnp.int32)
    picks = jax.random.randint(first_key, (blocks,), 0, 5)
    chosen = jax.random.randint(second_key, (), 0, blocks)
    picks = jnp.where(jnp.arange(blocks) == chosen, 4, picks)
    return patterns[picks]


def with_spikes(values, own_key, source, target, parts, factor):
    def block_of(dim):
        return (jnp.arange(values.shape[dim]) // (values.shape[dim] // parts)).reshape((-1,) + (1,) * (values.ndim - 1 - dim))

    near = jax.random.permutation(own_key, parts)[block_of(target)]
    other_side = (block_of(target) + parts // 2) % parts
    return jnp.where((block_of(source) == near) | (block_of(source) == other_side), factor * values, values)


def block_levels(stream_key, shape, shards, smallest, largest):
    gain = 1.0
    for dim, blocks in shards:
        heights = jax.random.uniform(jax.random.fold_in(jax.random.fold_in(stream_key, 6), dim), (blocks,), jnp.float32, smallest / len(shards), largest / len(shards))
        gain = gain * jnp.repeat(jnp.exp(heights), shape[dim] // blocks).reshape((-1,) + (1,) * (len(shape) - 1 - dim))
    return gain


def normal_values(stream_key, shape, scale, most, cuts=(), held_as=jnp.bfloat16):
    entries = jax.random.normal(stream_key, shape, jnp.float32) * scale
    if len(cuts) > 0:
        entries = block_levels(stream_key, shape, cuts, -0.22, 0.18) * entries
    return jnp.clip(entries, min=-most, max=most).astype(held_as)


def bell_draw_with(own_key, shape, scale, most, shards, heavy, held_as=jnp.bfloat16):
    values = scale * jax.random.normal(own_key, shape, jnp.float32)
    if shards:
        values = values * block_levels(own_key, shape, shards, -0.22, 0.18)
    return jnp.clip(with_spikes(values, jax.random.fold_in(own_key, 3), *heavy), -most, most).astype(held_as)


def setup_inputs(seed: int = 0) -> dict:
    arg_keys = jax.random.split(jax.random.key(seed), 21)
    return {
        "layer_input": normal_values(arg_keys[0], (TOKENS, D), 1.0, 6.0, ((0, 128),)),
        "prior_logits": normal_values(arg_keys[1], (H, TOKENS, TOK_DEV), 1.0, 4.0, ((1, 128),)),
        "bucket_counts": draw_bucket_counts(jax.random.fold_in(arg_keys[20], 71), 0),
        "output_cotangent": bell_draw_with(arg_keys[3], (TOKENS, D), 1.0, 24.0, ((0, 128),), (0, 1, 128, 5.5)),
        "logits_cotangent": normal_values(arg_keys[4], (H, TOKENS, TOK_DEV), 0.3, 1.796875, ((1, 128),)),
        "query_kernel": normal_values(arg_keys[5], (D, D), D ** -0.5, 0.21875, ((1, 128),)),
        "query_offset": normal_values(arg_keys[6], (D,), 0.5, 3.0, ((0, 128),)),
        "key_kernel": normal_values(arg_keys[7], (D, D), D ** -0.5, 0.21875, ((1, 128),)),
        "value_kernel": normal_values(arg_keys[8], (D, D), D ** -0.5, 0.21875, ((1, 128),)),
        "value_offset": normal_values(arg_keys[9], (D,), 0.5, 3.0, ((0, 128),)),
        "output_kernel": normal_values(arg_keys[10], (D, D), (D // 48) ** -0.5, 1.5, ((1, 128),)),
        "output_offset": normal_values(arg_keys[11], (D,), 0.3, 1.796875, ((0, 128),)),
        "first_gain": jnp.clip(1.0 + 0.1 * jax.random.normal(arg_keys[12], (D,), jnp.float32), 0.5, 1.5).astype(jnp.bfloat16),
        "first_shift": normal_values(arg_keys[13], (D,), 0.3, 1.796875, ((0, 128),)),
        "inner_kernel": normal_values(arg_keys[14], (D, FF), D ** -0.5, 0.21875, ((1, 128),)),
        "inner_offset": normal_values(arg_keys[15], (FF,), 0.5, 3.0, ((0, 128),)),
        "outer_kernel": normal_values(arg_keys[16], (FF, D), FF ** -0.5, 0.109375, ((1, 128),)),
        "outer_offset": normal_values(arg_keys[17], (D,), 0.3, 1.796875, ((0, 128),)),
        "second_gain": jnp.clip(1.0 + 0.1 * jax.random.normal(arg_keys[18], (D,), jnp.float32), 0.5, 1.5).astype(jnp.bfloat16),
        "second_shift": normal_values(arg_keys[19], (D,), 0.3, 1.796875, ((0, 128),)),
    }


@jax.custom_vjp
def low(v):
    return lax.optimization_barrier(v.astype(jnp.bfloat16)).astype(jnp.float32)

@jax.custom_vjp
def low_back(v):
    return v

def low_keep(v):
    return (low(v), None)

def low_pass(kept, grad):
    return (grad,)

def back_keep(v):
    return (v, None)

def back_low(kept, grad):
    return (low(grad),)
low.defvjp(low_keep, low_pass)
low_back.defvjp(back_keep, back_low)
EPSILON = 1e-12
HIGHEST = lax.Precision.HIGHEST

def segment_rows(counts_row):
    lengths = jnp.arange(1, 5, dtype=jnp.int32)
    covered = counts_row.astype(jnp.int32) * lengths
    offsets = jnp.cumsum(covered).astype(jnp.int32) - covered
    unit_index = jnp.arange(DEV_UNITS, dtype=jnp.int32)
    relative = unit_index[:, None] - offsets[None, :]
    starting = (relative >= 0) & (relative < covered[None, :]) & (relative % lengths[None, :] == 0)
    unit_segment = jnp.cumsum(jnp.any(starting, axis=1).astype(jnp.int32)).astype(jnp.int32) - 1
    return jnp.repeat(unit_segment, UNIT)

def layer_norm(values, scaling, offset):
    centred = values - lax.optimization_barrier(jnp.mean(values, axis=-1, keepdims=True))
    spread = lax.optimization_barrier(jnp.mean(centred * centred, axis=-1, keepdims=True))
    return centred * lax.rsqrt(spread + EPSILON) * scaling + offset

def attend_block(block):
    query_block, key_block, value_block, prior_block, allowed = block
    scores = jnp.einsum('qhd,khd->hqk', query_block, key_block, precision=HIGHEST) * HEAD ** (-0.5)
    scores = low_back(scores) + prior_block
    probs = jax.nn.softmax(jnp.where(allowed[None], scores, -1e+30), axis=-1)
    mixed = jnp.einsum('hqk,khd->qhd', low(probs), value_block, precision=HIGHEST)
    return (mixed.reshape(TOK_DEV, D), jnp.where(allowed[None], scores, 0.0))

def forward(inputs, prior, params, allowed):
    query_kernel, query_offset, key_kernel, value_kernel, value_offset, output_kernel, output_offset, first_gain, first_shift, inner_kernel, inner_offset, outer_kernel, outer_offset, second_gain, second_shift = params
    blocks = N_DP * N_FSDP
    queries = low(low_back(jnp.dot(inputs, query_kernel, precision=HIGHEST) + query_offset))
    key_rows = low(low_back(jnp.dot(inputs, key_kernel, precision=HIGHEST)))
    value_rows = low(low_back(jnp.dot(inputs, value_kernel, precision=HIGHEST) + value_offset))

    def shaped(values):
        return values.reshape(blocks, TOK_DEV, H, HEAD)
    prior_blocks = prior.reshape(H, blocks, TOK_DEV, TOK_DEV).transpose(1, 0, 2, 3)
    mixed, scores = lax.map(jax.checkpoint(attend_block), (shaped(queries), shaped(key_rows), shaped(value_rows), prior_blocks, allowed))
    mixed = low(low_back(mixed.reshape(blocks * TOK_DEV, D)))
    attended = low_back(jnp.dot(mixed, output_kernel, precision=HIGHEST) + output_offset)
    normed = low(layer_norm(inputs + attended, first_gain, first_shift))
    inner = low_back(jnp.dot(normed, inner_kernel, precision=HIGHEST) + inner_offset)
    active = low(jax.nn.gelu(inner, approximate=False))
    outer = low_back(jnp.dot(active, outer_kernel, precision=HIGHEST) + outer_offset)
    result = layer_norm(normed + outer, second_gain, second_shift)
    raw_all = scores.transpose(1, 0, 2, 3).reshape(H, blocks * TOK_DEV, TOK_DEV)
    return (result, raw_all)

def reference(layer_input, prior_logits, bucket_counts, output_cotangent, logits_cotangent, query_kernel, query_offset, key_kernel, value_kernel, value_offset, output_kernel, output_offset, first_gain, first_shift, inner_kernel, inner_offset, outer_kernel, outer_offset, second_gain, second_shift):
    segments = jax.vmap(segment_rows)(bucket_counts)
    allowed = segments[:, :, None] == segments[:, None, :]
    params = (query_kernel, query_offset, key_kernel, value_kernel, value_offset, output_kernel, output_offset, first_gain, first_shift, inner_kernel, inner_offset, outer_kernel, outer_offset, second_gain, second_shift)
    floats = tuple((p.astype(jnp.float32) for p in params))
    inputs = layer_input.astype(jnp.float32)
    prior = prior_logits.astype(jnp.float32)

    def wrapped(inputs, prior, floats):
        return forward(inputs, prior, floats, allowed)
    (result, raw_all), pullback = jax.vjp(wrapped, inputs, prior, floats)
    input_slope, prior_slope, slopes = pullback((output_cotangent.astype(jnp.float32), logits_cotangent.astype(jnp.float32)))
    return (result.astype(jnp.bfloat16), raw_all.astype(jnp.bfloat16), input_slope.astype(jnp.bfloat16), prior_slope.astype(jnp.bfloat16), slopes[0], slopes[1], slopes[2], slopes[3], slopes[4], slopes[5], slopes[6], slopes[7], slopes[8], slopes[9], slopes[10], slopes[11], slopes[12], slopes[13], slopes[14])
```

```python
import jax
import jax.numpy as jnp
from jax import lax
from jax.experimental import pallas as pl
from jax.experimental.pallas import tpu as pltpu
from jax.sharding import Mesh
from jax.sharding import PartitionSpec as P

D = 768
H = 12
HEAD = 64
FF = 3072
UNIT = 128
DEV_UNITS = 4
EPSILON = 1e-12

AXES = ("xh", "z", "y", "c", "xl")
SIZES = (2, 4, 4, 2, 2)
GROUPS = 32
ROWS = 24
MASKS = ((1, 3), (3, 1))
STEPS_A = (("x", 0), ("z", 0), ("z", 1), ("y", 0), ("y", 1))
STEPS_B = (("x", 0), ("y", 0), ("y", 1), ("z", 0), ("z", 1))
BF16 = jnp.bfloat16
F32 = jnp.float32


def exchange(values, step):
    axis, turn = step
    if axis == "x":
        return lax.ppermute(values, ("xh", "xl"), [(i, 3 - i) for i in range(4)])
    pairs = []
    for i in range(4):
        for core in range(2):
            pairs.append((i * 2 + core, (i ^ MASKS[core][turn]) * 2 + core))
    return lax.ppermute(values, (axis, "c"), pairs)


def swap(values, axis):
    return lax.ppermute(values, axis, [(0, 1), (1, 0)])


def position_groups(steps, core):
    position = jnp.arange(GROUPS, dtype=jnp.int32)
    place = {
        "x": jnp.full((GROUPS,), lax.axis_index("xh"), jnp.int32),
        "y": jnp.full((GROUPS,), lax.axis_index("y"), jnp.int32),
        "z": jnp.full((GROUPS,), lax.axis_index("z"), jnp.int32),
    }
    for bit, (axis, turn) in enumerate(steps):
        if axis == "x":
            mask = 1
        else:
            mask = jnp.where(core == 0, MASKS[0][turn], MASKS[1][turn])
        place[axis] = place[axis] ^ (((position >> bit) & 1) * mask)
    return (place["x"] * 4 + place["z"]) * 4 + place["y"]


def gather_part(block, steps):
    held = block
    for step in steps[:-1]:
        held = jnp.concatenate([held, exchange(held, step)], axis=0)
    return held, exchange(held, steps[-1])


def reduce_part(total, steps):
    for step in reversed(steps):
        half = total.shape[0] // 2
        arrived = exchange(total[half:], step)
        total = (total[:half].astype(F32) + arrived.astype(F32)).astype(BF16)
    return total


ANY = pl.BlockSpec(memory_space=pl.ANY)
VMEM = pl.BlockSpec(memory_space=pltpu.VMEM)
SMEM = pl.BlockSpec(memory_space=pltpu.SMEM)
TOKENS = 512
PAIR = 2 * HEAD
LIMIT = 58 * 1024 * 1024


def dot_nt(rows, matrix):
    return lax.dot_general(rows, matrix, (((1,), (1,)), ((), ())), preferred_element_type=F32)


def dot_nn(rows, matrix):
    return lax.dot_general(rows, matrix, (((1,), (0,)), ((), ())), preferred_element_type=F32)


def dot_tn(rows, matrix):
    return lax.dot_general(rows, matrix, (((0,), (0,)), ((), ())), preferred_element_type=F32)


def fetch(table, core, own, other, targets, sems):
    def place(parts, half, row):
        for part in range(2):
            if (half, part) not in targets:
                continue
            where, sem = targets[half, part]
            for second in range(2):
                source = parts[2 * part + second]

                def body(i, carry):
                    group = table[row + part, i + 16 * second]
                    pltpu.make_async_copy(source.at[i], where(group), sems.at[sem]).start()
                    return carry

                lax.fori_loop(0, 16, body, 0)

    @pl.when(core[0] == 0)
    def _():
        place(own, 0, 0)
        place(other, 1, 2)

    @pl.when(core[0] != 0)
    def _():
        place(own, 1, 0)
        place(other, 0, 2)


def settle(ref, sem):
    pltpu.make_async_copy(ref, ref, sem).wait()


def straighten(raw, skip, store):
    for i in range(4):
        block = raw[8 * i : 8 * i + 8].astype(F32)[:, skip : skip + ROWS]
        store(i, block.reshape(8 * ROWS, D).astype(BF16))


def attend_kernel(
    table, core, counts, x_ref, prior_ref, *refs
):
    own, other = refs[0:4], refs[4:8]
    raw_ref, probs_ref, q_ref, k_ref, v_ref, mixed_ref, wq_ref, wk_ref, wv_ref, vec_ref = refs[8:18]
    raw_q, raw_k, raw_v, sems = refs[18:22]
    step = pl.program_id(0)

    @pl.when(step == 0)
    def _():
        targets = {
            (0, 0): (lambda g: raw_q.at[g], 0),
            (0, 1): (lambda g: raw_k.at[g], 1),
            (1, 0): (lambda g: raw_v.at[g], 2),
        }
        fetch(table, core, own, other, targets, sems)

        def keep(ref):
            def store(i, rows):
                ref[192 * i : 192 * (i + 1), :] = rows

            return store

        settle(raw_k, sems.at[1])
        small = raw_k[...].astype(F32)[:, ROWS : ROWS + 8, 0:256]
        row = lax.broadcasted_iota(jnp.int32, (128, D), 0)
        lane = lax.broadcasted_iota(jnp.int32, (128, D), 1)
        spread = (lane % ROWS == row).astype(BF16)
        wide = dot_nn(small[:, :, 0:128].reshape(256, 128).astype(BF16), spread).reshape(32, 8, D)
        group = lax.broadcasted_iota(jnp.int32, (32, 8, D), 0)
        lane3 = lax.broadcasted_iota(jnp.int32, (32, 8, D), 2)
        vec_ref[0:8, :] = jnp.sum(jnp.where(lane3 // ROWS == group, wide, 0.0), axis=0)
        spread = ((lane % 96 == row) & (row < 96)).astype(BF16)
        wide = dot_nn(small[:, :, 128:256].reshape(256, 128).astype(BF16), spread).reshape(4, 8, 8, D)
        second = lax.broadcasted_iota(jnp.int32, (4, 8, 8, D), 1)
        place = lax.broadcasted_iota(jnp.int32, (4, 8, 8, D), 2)
        lane4 = lax.broadcasted_iota(jnp.int32, (4, 8, 8, D), 3)
        chosen = jnp.where((lane4 // 96 == second) & (place == 0), wide, 0.0)
        inner_rows = jnp.sum(chosen, axis=1)
        for i in range(4):
            vec_ref[8 + i : 9 + i, :] = inner_rows[i, 0:1, :]
        vec_ref[12:16, :] = jnp.zeros((4, D), F32)

        straighten(raw_k, 0, keep(wk_ref))
        settle(raw_q, sems.at[0])
        straighten(raw_q, 0, keep(wq_ref))
        settle(raw_v, sems.at[2])
        straighten(raw_v, 0, keep(wv_ref))
        x = x_ref[...]
        q_ref[...] = (dot_nt(x, wq_ref[...]) + vec_ref[0:1, :]).astype(BF16)
        k_ref[...] = dot_nt(x, wk_ref[...]).astype(BF16)
        v_ref[...] = (dot_nt(x, wv_ref[...]) + vec_ref[1:2, :]).astype(BF16)

    columns = pl.ds(pl.multiple_of(step * PAIR, PAIR), PAIR)
    query = q_ref[:, columns] * jnp.asarray(HEAD ** (-0.5), BF16)
    key = k_ref[:, columns]
    value = v_ref[:, columns]
    low_lane = lax.broadcasted_iota(jnp.int32, (TOKENS, PAIR), 1) < HEAD
    segments = unit_segments(counts)
    results = []
    for head in range(2):
        chosen = low_lane if head == 0 else ~low_lane
        masked = jnp.where(chosen, query, jnp.zeros_like(query))
        parts = []
        for block in range(DEV_UNITS):
            rows = slice(block * UNIT, (block + 1) * UNIT)
            allowed = allowed_lanes(segments, block)
            scores = dot_nt(masked[rows], key) + prior_ref[head, rows, :].astype(F32)
            raw_ref[head, rows, :] = jnp.where(allowed, scores, 0.0).astype(BF16)
            scores = jnp.where(allowed, scores, -1e30)
            grown = jnp.exp(scores - jnp.max(scores, axis=-1, keepdims=True))
            total = jnp.sum(grown, axis=-1, keepdims=True)
            probs = (grown * (1.0 / total)).astype(BF16)
            probs_ref[head, rows, :] = probs
            parts.append(dot_nn(probs, value))
        results.append(jnp.concatenate(parts, axis=0))
    mixed_ref[...] = jnp.where(low_lane, results[0], results[1]).astype(BF16)


def unit_segments(counts):
    start = [counts[0, 0], counts[0, 0] + 2 * counts[0, 1]]
    start.append(start[1] + 3 * counts[0, 2])
    segments = []
    current = jnp.int32(-1)
    for unit in range(DEV_UNITS):
        first = unit < start[0]
        second = (unit >= start[0]) & (unit < start[1]) & ((unit - start[0]) % 2 == 0)
        third = (unit >= start[1]) & (unit < start[2]) & ((unit - start[1]) % 3 == 0)
        fourth = (unit >= start[2]) & ((unit - start[2]) % 4 == 0)
        current = current + jnp.where(first | second | third | fourth, 1, 0)
        segments.append(current)
    return segments


def allowed_lanes(segments, block):
    unit = lax.broadcasted_iota(jnp.int32, (1, TOKENS), 1) // UNIT
    same = jnp.zeros((1, TOKENS), jnp.int32)
    for other in range(DEV_UNITS):
        same = jnp.where(unit == other, jnp.where(segments[other] == segments[block], 1, 0), same)
    return same > 0


def attend(table, core, counts, layer_input, prior_logits, own, other):
    whole = pl.BlockSpec((TOKENS, D), lambda i, *_: (0, 0))
    square = pl.BlockSpec((D, D), lambda i, *_: (0, 0))
    logits = pl.BlockSpec((2, TOKENS, TOKENS), lambda i, *_: (i, 0, 0))
    rows_shape = jax.ShapeDtypeStruct((TOKENS, D), BF16)
    logits_shape = jax.ShapeDtypeStruct((H, TOKENS, TOKENS), BF16)
    square_shape = jax.ShapeDtypeStruct((D, D), BF16)
    return pl.pallas_call(
        attend_kernel,
        grid_spec=pltpu.PrefetchScalarGridSpec(
            num_scalar_prefetch=3,
            grid=(H // 2,),
            in_specs=[whole, logits] + [ANY] * 8,
            out_specs=[
                logits,
                logits,
                whole,
                whole,
                whole,
                pl.BlockSpec((TOKENS, PAIR), lambda i, *_: (0, i)),
                square,
                square,
                square,
                pl.BlockSpec((16, D), lambda i, *_: (0, 0)),
            ],
            scratch_shapes=[
                pltpu.VMEM((GROUPS, ROWS, D), BF16),
                pltpu.VMEM((GROUPS, 32, D), BF16),
                pltpu.VMEM((GROUPS, ROWS, D), BF16),
                pltpu.SemaphoreType.DMA((3,)),
            ],
        ),
        out_shape=(
            logits_shape,
            logits_shape,
            rows_shape,
            rows_shape,
            rows_shape,
            rows_shape,
            square_shape,
            square_shape,
            square_shape,
            jax.ShapeDtypeStruct((16, D), F32),
        ),
        compiler_params=pltpu.CompilerParams(vmem_limit_bytes=LIMIT),
        cost_estimate=pl.CostEstimate(flops=5 * 10**9, bytes_accessed=30 * 10**6, transcendentals=3145728),
        name="attend",
    )(table, core, counts, layer_input, prior_logits, *own, *other)


def mean_of(values):
    return jnp.sum(values, axis=-1, keepdims=True) * (1.0 / D)


def normalise(values):
    centred = values - mean_of(values)
    scale = lax.rsqrt(mean_of(centred * centred) + EPSILON)
    return centred * scale, scale


def norm_back(slope, normal, scale):
    return scale * (slope - mean_of(slope) - normal * mean_of(slope * normal))


def fold(values):
    return jnp.sum(values.reshape(values.shape[0] // 8, 8, D), axis=0)


CHUNK = 128


def middle_kernel(table, core, x_ref, mixed_ref, cot_ref, vec_ref, *refs):
    own_b, other_b = refs[0:2], refs[2:4]
    own, other = refs[4:8], refs[8:12]
    y_ref, first_ref, mixed_low_ref, og_ref, vg_ref = refs[12:17]
    outs = refs[17:21]
    (
        raw_o,
        wo,
        w_in,
        raw_a,
        raw_b,
        w_out,
        active,
        curve,
        normed,
        normal,
        scales,
        total,
        low,
        low_t,
        d_in,
        d_out,
        sums,
        sems,
    ) = refs[21:39]

    fetch(table, core, (None, None) + own_b, (None, None) + other_b, {(1, 1): (lambda g: raw_o.at[g], 0)}, sems)
    targets = {
        (0, 0): (lambda g: w_in.at[g, pl.ds(0, 48)], 1),
        (0, 1): (lambda g: w_in.at[g, pl.ds(48, 48)], 1),
        (1, 0): (lambda g: raw_a.at[g], 2),
        (1, 1): (lambda g: raw_b.at[g], 3),
    }
    fetch(table, core, own, other, targets, sems)

    def keep_wo(i, rows):
        wo[192 * i : 192 * (i + 1), :] = rows

    settle(raw_o, sems.at[0])
    straighten(raw_o, 0, keep_wo)
    total[...] = dot_nt(mixed_ref[...], wo[...])

    def first_norm(i, carry):
        rows = pl.ds(pl.multiple_of(i * CHUNK, CHUNK), CHUNK)
        values, scale = normalise(x_ref[rows, :].astype(F32) + (total[rows, :] + vec_ref[2:3, :]))
        normal[rows, :] = values
        scales[rows, :] = scale
        normed[rows, :] = (values * vec_ref[3:4, :] + vec_ref[4:5, :]).astype(BF16)
        return carry

    lax.fori_loop(0, TOKENS // CHUNK, first_norm, 0)

    settle(w_in, sems.at[1])
    for part in range(4):
        matrix = w_in.at[pl.ds(part * 8, 8)]
        for j in range(2):
            weights = matrix[4 * j : 4 * j + 4].reshape(384, D)
            columns = slice(part * D + 384 * j, part * D + 384 * (j + 1))
            inner = dot_nt(normed[...], weights) + vec_ref[8 + part : 9 + part, 384 * j : 384 * (j + 1)]
            bell = 0.5 * (1.0 + lax.erf(inner * (0.5**0.5)))
            active[:, columns] = (inner * bell).astype(BF16)
            slope = bell + inner * jnp.exp(inner * inner * -0.5) * 0.3989422804014327
            curve[:, columns] = slope.astype(BF16)

    settle(raw_a, sems.at[2])
    settle(raw_b, sems.at[3])
    for part in range(4):

        def keep_out(i, rows):
            w_out[192 * i : 192 * (i + 1), part * D : (part + 1) * D] = rows

        straighten(raw_a if part < 2 else raw_b, ROWS * (part % 2), keep_out)
    for j in range(3):
        total[:, 256 * j : 256 * (j + 1)] = dot_nt(active[...], w_out[256 * j : 256 * (j + 1), :])

    sums[...] = jnp.zeros_like(sums)

    def second_norm(i, carry):
        rows = pl.ds(pl.multiple_of(i * CHUNK, CHUNK), CHUNK)
        values, scale = normalise(normed[rows, :].astype(F32) + (total[rows, :] + vec_ref[5:6, :]))
        y_ref[rows, :] = (values * vec_ref[6:7, :] + vec_ref[7:8, :]).astype(BF16)
        given = cot_ref[rows, :].astype(F32)
        sums[0] += fold(given * values)
        sums[1] += fold(given)
        slope = norm_back(given * vec_ref[6:7, :], values, scale)
        total[rows, :] = slope
        low[rows, :] = slope.astype(BF16)
        return carry

    lax.fori_loop(0, TOKENS // CHUNK, second_norm, 0)
    vg_ref[...] = jnp.zeros_like(vg_ref)
    ones = jnp.ones((8, TOKENS), BF16)
    vg_ref[6:7, :] = jnp.sum(sums[0], axis=0, keepdims=True)
    vg_ref[7:8, :] = jnp.sum(sums[1], axis=0, keepdims=True)
    vg_ref[5:6, :] = dot_nn(ones, low[...])[0:1]
    low_t[...] = low[...].T

    for part in range(4):
        for j in range(2):
            columns = slice(part * D + 384 * j, part * D + 384 * (j + 1))
            grown = dot_nn(low_t[...], active[:, columns])
            d_out[part, :, :, 384 * j : 384 * (j + 1)] = grown.reshape(GROUPS, ROWS, 384).astype(BF16)
            slope = dot_nn(low[...], w_out[:, columns])
            curve[:, columns] = (slope * curve[:, columns].astype(F32)).astype(BF16)

    for part in range(4):
        columns = slice(part * D, (part + 1) * D)
        grown = dot_tn(curve[:, columns], normed[...])
        d_in[8 * part : 8 * part + 8] = grown.reshape(8, 4, ROWS, D).astype(BF16)
        vg_ref[8 + part : 9 + part, :] = dot_nn(ones, curve[:, columns])[0:1]

    def send(parts, half, row, sem):
        for part in range(2):
            target = parts[part]

            def body(i, carry):
                group = table[row + part, i]
                if half == 0:
                    pltpu.make_async_copy(
                        d_in.at[group, pl.ds(2 * part, 2)], target.at[i], sems.at[sem + part]
                    ).start()
                else:
                    for k in range(2):
                        pltpu.make_async_copy(
                            d_out.at[2 * part + k, group], target.at[i, k], sems.at[sem + part]
                        ).start()
                return carry

            lax.fori_loop(0, GROUPS, body, 0)

    @pl.when(core[0] == 0)
    def _():
        send(outs[0:2], 0, 0, 4)
        send(outs[2:4], 1, 2, 6)

    @pl.when(core[0] != 0)
    def _():
        send(outs[0:2], 1, 0, 4)
        send(outs[2:4], 0, 2, 6)

    matrix = w_in[...].reshape(FF, D)
    for j in range(3):
        columns = slice(256 * j, 256 * (j + 1))
        total[:, columns] += dot_nn(curve[...], matrix[:, columns])

    sums[...] = jnp.zeros_like(sums)

    def first_back(i, carry):
        rows = pl.ds(pl.multiple_of(i * CHUNK, CHUNK), CHUNK)
        given = total[rows, :]
        values = normal[rows, :]
        sums[0] += fold(given * values)
        sums[1] += fold(given)
        slope = norm_back(given * vec_ref[3:4, :], values, scales[rows, :])
        first_ref[rows, :] = slope
        low[rows, :] = slope.astype(BF16)
        return carry

    lax.fori_loop(0, TOKENS // CHUNK, first_back, 0)
    vg_ref[3:4, :] = jnp.sum(sums[0], axis=0, keepdims=True)
    vg_ref[4:5, :] = jnp.sum(sums[1], axis=0, keepdims=True)
    vg_ref[2:3, :] = dot_nn(ones, low[...])[0:1]
    mixed_low_ref[...] = dot_nn(low[...], wo[...]).astype(BF16)
    grown = dot_tn(low[...], mixed_ref[...]).reshape(GROUPS, ROWS, D)
    og_ref[...] = jnp.concatenate([grown, jnp.zeros((GROUPS, 8, D), F32)], axis=1).astype(BF16)
    for i in range(4):
        settle(outs[i], sems.at[4 + i])


def middle(table, core, layer_input, mixed, cotangent, vectors, own_b, other_b, own, other):
    part = jax.ShapeDtypeStruct((GROUPS, 2, ROWS, D), BF16)
    return pl.pallas_call(
        middle_kernel,
        in_specs=[SMEM, SMEM, VMEM, VMEM, VMEM, VMEM] + [ANY] * 12,
        out_specs=[VMEM] * 5 + [ANY] * 4,
        out_shape=(
            jax.ShapeDtypeStruct((TOKENS, D), BF16),
            jax.ShapeDtypeStruct((TOKENS, D), F32),
            jax.ShapeDtypeStruct((TOKENS, D), BF16),
            jax.ShapeDtypeStruct((GROUPS, 32, D), BF16),
            jax.ShapeDtypeStruct((16, D), F32),
            part,
            part,
            part,
            part,
        ),
        scratch_shapes=[
            pltpu.VMEM((GROUPS, 32, D), BF16),
            pltpu.VMEM((D, D), BF16),
            pltpu.VMEM((GROUPS, 96, D), BF16),
            pltpu.VMEM((GROUPS, 48, D), BF16),
            pltpu.VMEM((GROUPS, 48, D), BF16),
            pltpu.VMEM((D, FF), BF16),
            pltpu.VMEM((TOKENS, FF), BF16),
            pltpu.VMEM((TOKENS, FF), BF16),
            pltpu.VMEM((TOKENS, D), BF16),
            pltpu.VMEM((TOKENS, D), F32),
            pltpu.VMEM((TOKENS, 1), F32),
            pltpu.VMEM((TOKENS, D), F32),
            pltpu.VMEM((TOKENS, D), BF16),
            pltpu.VMEM((D, TOKENS), BF16),
            pltpu.VMEM((GROUPS, 4, ROWS, D), BF16),
            pltpu.VMEM((4, GROUPS, ROWS, D), BF16),
            pltpu.VMEM((2, 8, D), F32),
            pltpu.SemaphoreType.DMA((8,)),
        ],
        compiler_params=pltpu.CompilerParams(vmem_limit_bytes=LIMIT),
        cost_estimate=pl.CostEstimate(flops=16 * 10**9, bytes_accessed=30 * 10**6, transcendentals=3145728),
        name="middle",
    )(table, core, layer_input, mixed, cotangent, vectors, *own_b, *other_b, *own, *other)


def attend_back_kernel(
    counts, q_ref, k_ref, v_ref, mixed_ref, slope_ref, probs_ref, cot_ref, out_ref, dq_ref, dk_ref, dv_ref
):
    low_lane = lax.broadcasted_iota(jnp.int32, (TOKENS, PAIR), 1) < HEAD
    segments = unit_segments(counts)
    scale = jnp.asarray(HEAD ** (-0.5), BF16)
    slope = slope_ref[...]
    query_t = (q_ref[...] * scale).T
    slope_t = slope.T
    key = k_ref[...] * scale
    value = v_ref[...]
    product = slope.astype(F32) * mixed_ref[...].astype(F32)
    results = []
    for head in range(2):
        chosen = low_lane if head == 0 else ~low_lane
        masked = jnp.where(chosen, slope, jnp.zeros_like(slope))
        shared = jnp.sum(jnp.where(chosen, product, 0.0), axis=-1, keepdims=True)
        for block in range(DEV_UNITS):
            rows = slice(block * UNIT, (block + 1) * UNIT)
            allowed = allowed_lanes(segments, block)
            grown = dot_nt(masked[rows], value)
            grown = probs_ref[head, rows, :].astype(F32) * (grown - shared[rows])
            grown = grown + jnp.where(allowed, cot_ref[head, rows, :].astype(F32), 0.0)
            out_ref[head, rows, :] = grown.astype(BF16)
        logits = out_ref[head]
        heads = slice(head * HEAD, (head + 1) * HEAD)
        results.append(dot_nn(logits, key))
        dk_ref[heads, :] = dot_nn(query_t[heads], logits).astype(BF16)
        dv_ref[heads, :] = dot_nn(slope_t[heads], probs_ref[head]).astype(BF16)
    dq_ref[...] = jnp.where(low_lane, results[0], results[1]).astype(BF16)


def attend_back(counts, queries, keys, values, mixed, mixed_low, probs, logits_cotangent):
    columns = pl.BlockSpec((TOKENS, PAIR), lambda i, *_: (0, i))
    turned = pl.BlockSpec((PAIR, TOKENS), lambda i, *_: (i, 0))
    logits = pl.BlockSpec((2, TOKENS, TOKENS), lambda i, *_: (i, 0, 0))
    return pl.pallas_call(
        attend_back_kernel,
        grid_spec=pltpu.PrefetchScalarGridSpec(
            num_scalar_prefetch=1,
            grid=(H // 2,),
            in_specs=[columns] * 5 + [logits] * 2,
            out_specs=[logits, columns, turned, turned],
        ),
        out_shape=(
            jax.ShapeDtypeStruct((H, TOKENS, TOKENS), BF16),
            jax.ShapeDtypeStruct((TOKENS, D), BF16),
            jax.ShapeDtypeStruct((D, TOKENS), BF16),
            jax.ShapeDtypeStruct((D, TOKENS), BF16),
        ),
        compiler_params=pltpu.CompilerParams(vmem_limit_bytes=LIMIT),
        cost_estimate=pl.CostEstimate(flops=6 * 10**9, bytes_accessed=22 * 10**6, transcendentals=0),
        name="attend_back",
    )(counts, queries, keys, values, mixed, mixed_low, probs, logits_cotangent)


def slopes_kernel(table, core, x_ref, dq_ref, dk_ref, dv_ref, og_ref, vg_ref, *refs):
    outs = refs[0:4]
    d_q, d_k, d_v, sems = refs[4:8]
    x = x_ref[...]
    ones = jnp.ones((8, TOKENS), BF16)
    query_sum = dot_nn(ones, dq_ref[...])[0:1]
    value_sum = dot_nt(ones, dv_ref[...])[0:1]
    rows8 = lax.broadcasted_iota(jnp.int32, (8, D), 0)
    offsets = vg_ref[0:8, :]
    offsets = jnp.where(rows8 == 0, query_sum, jnp.where(rows8 == 1, value_sum, offsets))
    group = lax.broadcasted_iota(jnp.int32, (32, 8, D), 0)
    lane = lax.broadcasted_iota(jnp.int32, (32, 8, D), 2)
    chosen = jnp.where(lane // ROWS == group, offsets[None], 0.0)
    row = lax.broadcasted_iota(jnp.int32, (D, 128), 0)
    column = lax.broadcasted_iota(jnp.int32, (D, 128), 1)
    narrow = dot_nn(chosen.reshape(256, D).astype(BF16), (row % ROWS == column).astype(BF16))
    wide = jnp.broadcast_to(vg_ref[8:12, :][:, None, :], (4, 8, D))
    second = lax.broadcasted_iota(jnp.int32, (4, 8, D), 1)
    lane = lax.broadcasted_iota(jnp.int32, (4, 8, D), 2)
    chosen = jnp.where(lane // 96 == second, wide, 0.0).reshape(32, D)
    inner = dot_nn(chosen.astype(BF16), (row % 96 == column).astype(BF16))
    place = lax.broadcasted_iota(jnp.int32, (32, 8, 128), 1)
    inner = jnp.where(place == 0, inner[:, None, :], 0.0)
    small = jnp.concatenate(
        [narrow.reshape(32, 8, 128), inner, jnp.zeros((32, 8, D - 256), F32)], axis=2
    )
    d_k[...] = jnp.concatenate(
        [dot_nn(dk_ref[...], x).reshape(GROUPS, ROWS, D), small], axis=1
    ).astype(BF16)
    d_v[...] = dot_nn(dv_ref[...], x).reshape(GROUPS, ROWS, D).astype(BF16)
    d_q[...] = dot_tn(dq_ref[...], x).reshape(GROUPS, ROWS, D).astype(BF16)

    def send(parts, half, row, sem):
        sources = (d_q, d_k) if half == 0 else (d_v, og_ref)
        for part in range(2):

            def body(i, carry):
                pltpu.make_async_copy(
                    sources[part].at[table[row + part, i]], parts[part].at[i], sems.at[sem + part]
                ).start()
                return carry

            lax.fori_loop(0, GROUPS, body, 0)

    @pl.when(core[0] == 0)
    def _():
        send(outs[0:2], 0, 0, 0)
        send(outs[2:4], 1, 2, 2)

    @pl.when(core[0] != 0)
    def _():
        send(outs[0:2], 1, 0, 0)
        send(outs[2:4], 0, 2, 2)

    for i in range(4):
        settle(outs[i], sems.at[i])


def slopes(table, core, layer_input, dq, dk, dv, og, vg):
    part_a = jax.ShapeDtypeStruct((GROUPS, ROWS, D), BF16)
    part_b = jax.ShapeDtypeStruct((GROUPS, 32, D), BF16)
    return pl.pallas_call(
        slopes_kernel,
        in_specs=[SMEM, SMEM] + [VMEM] * 6,
        out_specs=[ANY] * 4,
        out_shape=(part_a, part_b, part_a, part_b),
        scratch_shapes=[
            pltpu.VMEM((GROUPS, ROWS, D), BF16),
            pltpu.VMEM((GROUPS, 32, D), BF16),
            pltpu.VMEM((GROUPS, ROWS, D), BF16),
            pltpu.SemaphoreType.DMA((4,)),
        ],
        compiler_params=pltpu.CompilerParams(vmem_limit_bytes=LIMIT),
        cost_estimate=pl.CostEstimate(flops=2 * 10**9, bytes_accessed=12 * 10**6, transcendentals=0),
        name="slopes",
    )(table, core, layer_input, dq, dk, dv, og, vg)


def gather_weights(kernels, vectors, inner_offset):
    core, low_x = lax.axis_index("c"), lax.axis_index("xl")
    mine = core * 2 + low_x
    query, key, value, output, inner, outer = kernels
    packed = jnp.concatenate(
        [query.T, key.T, value.T, output.T, inner.T, outer.T.reshape(24, D)], axis=0
    )
    small = jnp.pad(jnp.stack(vectors), ((0, 0), (0, 122)))
    small = jnp.concatenate([small, jnp.pad(inner_offset[None], ((0, 7), (0, 104)))], axis=1)
    packed = jnp.concatenate([packed, jnp.pad(small, ((0, 0), (0, D - 256)))], axis=0)
    pieces = jnp.stack(
        [
            packed,
            swap(packed, "xl"),
            swap(packed, "c"),
            lax.ppermute(packed, ("c", "xl"), [(i, 3 - i) for i in range(4)]),
        ]
    )
    natural = jnp.concatenate(
        [lax.dynamic_slice_in_dim(pieces, mine ^ i, 1, axis=0) for i in range(4)], axis=0
    )

    def wide(first):
        return natural[:, first : first + 6].reshape(ROWS, D)

    query, key, value, output = (wide(6 * i) for i in range(4))
    inner = natural[:, 24:48].reshape(96, D)
    outer = natural[:, 48:72].reshape(4, 6, 4, D).transpose(2, 0, 1, 3).reshape(96, D)
    offsets = natural[:, 72:80, 0:6].transpose(1, 0, 2).reshape(8, ROWS)
    offsets = jnp.pad(offsets, ((0, 0), (0, 128 - ROWS)))
    wide_offset = jnp.pad(natural[:, 72, 128:152].reshape(1, 96), ((0, 7), (0, 32)))
    small = jnp.concatenate([offsets, wide_offset, jnp.zeros((8, D - 256), BF16)], axis=1)
    first = core == 0
    part_a = jnp.where(first, query, value)
    part_b = jnp.concatenate([jnp.where(first, key, output), small], axis=0)
    chunk = jnp.where(first, inner, outer)
    near = gather_part(part_a[None], STEPS_A) + gather_part(part_b[None], STEPS_B)
    far = gather_part(chunk[None, 0:48], STEPS_A) + gather_part(chunk[None, 48:96], STEPS_B)
    return near, tuple(swap(part, "c") for part in near), far, tuple(swap(part, "c") for part in far)


def reduce_chunk(parts):
    keep_a, keep_b, send_a, send_b = parts
    total_a = (keep_a.astype(F32) + swap(send_a, "c").astype(F32)).astype(BF16)
    total_b = (keep_b.astype(F32) + swap(send_b, "c").astype(F32)).astype(BF16)
    total = jnp.concatenate(
        [
            reduce_part(total_a, STEPS_A)[0].reshape(-1, D),
            reduce_part(total_b, STEPS_B)[0].reshape(-1, D),
        ],
        axis=0,
    )
    own = total.astype(F32) + swap(total, "xl").astype(F32)
    other = swap(own, "c")
    first = lax.axis_index("c") == 0
    return jnp.where(first, own, other), jnp.where(first, other, own)


def body(
    layer_input,
    prior_logits,
    bucket_counts,
    output_cotangent,
    logits_cotangent,
    query_kernel,
    query_offset,
    key_kernel,
    value_kernel,
    value_offset,
    output_kernel,
    output_offset,
    first_gain,
    first_shift,
    inner_kernel,
    inner_offset,
    outer_kernel,
    outer_offset,
    second_gain,
    second_shift,
):
    core, low_x = lax.axis_index("c"), lax.axis_index("xl")
    mine = core * 2 + low_x
    table = jnp.stack(
        [
            position_groups(STEPS_A, core),
            position_groups(STEPS_B, core),
            position_groups(STEPS_A, 1 - core),
            position_groups(STEPS_B, 1 - core),
        ]
    )
    core_table = core.astype(jnp.int32).reshape(1)
    near, near_other, far, far_other = gather_weights(
        (query_kernel, key_kernel, value_kernel, output_kernel, inner_kernel, outer_kernel),
        (
            query_offset,
            value_offset,
            output_offset,
            first_gain,
            first_shift,
            outer_offset,
            second_gain,
            second_shift,
        ),
        inner_offset,
    )
    (raw_logits, probs, queries, keys, values, mixed, query_matrix, key_matrix, value_matrix, vectors) = attend(
        table, core_table, bucket_counts, layer_input, prior_logits, near, near_other
    )
    layer_output, first_slope, mixed_low, output_slope, vector_slopes, *ff_parts = middle(
        table,
        core_table,
        layer_input,
        mixed,
        output_cotangent,
        vectors,
        near[2:4],
        near_other[2:4],
        far,
        far_other,
    )
    ff_first, ff_second = reduce_chunk(ff_parts)
    logits_slope, dq, dk, dv = attend_back(
        bucket_counts, queries, keys, values, mixed, mixed_low, probs, logits_cotangent
    )
    tail_parts = slopes(table, core_table, layer_input, dq, dk, dv, output_slope, vector_slopes)
    tail_first, tail_second = reduce_chunk(tail_parts)
    input_slope = (
        first_slope + dot_nn(dq, query_matrix) + dot_tn(dk, key_matrix) + dot_tn(dv, value_matrix)
    ).astype(BF16)

    def owned(part, first):
        return lax.dynamic_slice_in_dim(part[first : first + ROWS], 6 * mine, 6, axis=0).T

    inner_owned = lax.dynamic_slice_in_dim(ff_first, ROWS * mine, ROWS, axis=0).T
    outer_owned = lax.dynamic_slice_in_dim(ff_second.reshape(4, ROWS, D), 6 * mine, 6, axis=1)
    outer_owned = outer_owned.transpose(1, 0, 2).reshape(6, FF).T
    small = tail_first[48:56]
    small_owned = lax.dynamic_slice(small, (0, 6 * mine), (8, 6))
    wide_owned = lax.dynamic_slice(small, (0, 128 + ROWS * mine), (1, ROWS))[0]
    return (
        layer_output,
        raw_logits,
        input_slope,
        logits_slope,
        owned(tail_first, 0),
        small_owned[0],
        owned(tail_first, 24),
        owned(tail_second, 0),
        small_owned[1],
        owned(tail_second, 24),
        small_owned[2],
        small_owned[3],
        small_owned[4],
        inner_owned,
        wide_owned,
        outer_owned,
        small_owned[5],
        small_owned[6],
        small_owned[7],
    )


def solution(mesh):
    fine = Mesh(mesh.devices.reshape(SIZES), AXES)
    rows = P(AXES, None)
    logits = P(None, AXES, None)
    columns = P(None, AXES)
    vector = P(AXES)
    return jax.shard_map(
        body,
        mesh=fine,
        in_specs=(
            rows,
            logits,
            rows,
            rows,
            logits,
            columns,
            vector,
            columns,
            columns,
            vector,
            columns,
            vector,
            vector,
            vector,
            columns,
            vector,
            columns,
            vector,
            vector,
            vector,
        ),
        out_specs=(
            rows,
            logits,
            rows,
            logits,
            columns,
            vector,
            columns,
            columns,
            vector,
            columns,
            vector,
            vector,
            vector,
            columns,
            vector,
            columns,
            vector,
            vector,
            vector,
        ),
        check_vma=False,
    )
```

```python
import jax
import jax.numpy as jnp
from jax import lax
from jax.experimental import pallas as pl
from jax.experimental.pallas import tpu as pltpu
from jax.sharding import Mesh
from jax.sharding import PartitionSpec as P

D = 768
H = 12
HEAD = 64
FF = 3072
UNIT = 128
DEV_UNITS = 4
EPSILON = 1e-12

AXES = ("xh", "z", "y", "c", "xl")
SIZES = (2, 4, 4, 2, 2)
GROUPS = 32
ROWS = 24
MASKS = ((1, 3), (3, 1))
STEPS_A = (("x", 0), ("z", 0), ("z", 1), ("y", 0), ("y", 1))
STEPS_B = (("x", 0), ("y", 0), ("y", 1), ("z", 0), ("z", 1))
BF16 = jnp.bfloat16
F32 = jnp.float32


def exchange(values, step):
    axis, turn = step
    if axis == "x":
        return lax.ppermute(values, ("xh", "xl"), [(i, 3 - i) for i in range(4)])
    pairs = []
    for i in range(4):
        for core in range(2):
            pairs.append((i * 2 + core, (i ^ MASKS[core][turn]) * 2 + core))
    return lax.ppermute(values, (axis, "c"), pairs)


def swap(values, axis):
    return lax.ppermute(values, axis, [(0, 1), (1, 0)])


def position_groups(steps, core):
    position = jnp.arange(GROUPS, dtype=jnp.int32)
    place = {
        "x": jnp.full((GROUPS,), lax.axis_index("xh"), jnp.int32),
        "y": jnp.full((GROUPS,), lax.axis_index("y"), jnp.int32),
        "z": jnp.full((GROUPS,), lax.axis_index("z"), jnp.int32),
    }
    for bit, (axis, turn) in enumerate(steps):
        if axis == "x":
            mask = 1
        else:
            mask = jnp.where(core == 0, MASKS[0][turn], MASKS[1][turn])
        place[axis] = place[axis] ^ (((position >> bit) & 1) * mask)
    return (place["x"] * 4 + place["z"]) * 4 + place["y"]


ANY = pl.BlockSpec(memory_space=pl.ANY)
VMEM = pl.BlockSpec(memory_space=pltpu.VMEM)
SMEM = pl.BlockSpec(memory_space=pltpu.SMEM)
TOKENS = 512
PAIR = 2 * HEAD
LIMIT = 58 * 1024 * 1024


def dot_nt(rows, matrix):
    return lax.dot_general(rows, matrix, (((1,), (1,)), ((), ())), preferred_element_type=F32)


def dot_nn(rows, matrix):
    return lax.dot_general(rows, matrix, (((1,), (0,)), ((), ())), preferred_element_type=F32)


def dot_tn(rows, matrix):
    return lax.dot_general(rows, matrix, (((0,), (0,)), ((), ())), preferred_element_type=F32)


def fetch(table, core, own, other, targets, sems):
    def place(parts, half, row):
        for part in range(2):
            if (half, part) not in targets:
                continue
            where, sem = targets[half, part]
            for second in range(2):
                source = parts[2 * part + second]

                def body(i, carry):
                    group = table[row + part, i + 16 * second]
                    pltpu.make_async_copy(source.at[i], where(group), sems.at[sem]).start()
                    return carry

                lax.fori_loop(0, 16, body, 0)

    @pl.when(core[0] == 0)
    def _():
        place(own, 0, 0)
        place(other, 1, 2)

    @pl.when(core[0] != 0)
    def _():
        place(own, 1, 0)
        place(other, 0, 2)


def settle(ref, sem):
    pltpu.make_async_copy(ref, ref, sem).wait()


def straighten(raw, skip, store):
    for i in range(4):
        block = raw[8 * i : 8 * i + 8].astype(F32)[:, skip : skip + ROWS]
        store(i, block.reshape(8 * ROWS, D).astype(BF16))


def project_kernel(table, core, x_ref, *refs):
    own, other = refs[0:4], refs[4:8]
    q_ref, k_ref, v_ref, wq_ref, wk_ref, wv_ref, vec_ref = refs[8:15]
    raw_q, raw_k, raw_v, sems = refs[15:19]
    targets = {
        (0, 0): (lambda g: raw_q.at[g], 0),
        (0, 1): (lambda g: raw_k.at[g], 1),
        (1, 0): (lambda g: raw_v.at[g], 2),
    }
    fetch(table, core, own, other, targets, sems)

    def keep(ref):
        def store(i, rows):
            ref[192 * i : 192 * (i + 1), :] = rows

        return store

    settle(raw_k, sems.at[1])
    small = raw_k[...].astype(F32)[:, ROWS : ROWS + 8, 0:256]
    row = lax.broadcasted_iota(jnp.int32, (128, D), 0)
    lane = lax.broadcasted_iota(jnp.int32, (128, D), 1)
    spread = (lane % ROWS == row).astype(BF16)
    wide = dot_nn(small[:, :, 0:128].reshape(256, 128).astype(BF16), spread).reshape(32, 8, D)
    group = lax.broadcasted_iota(jnp.int32, (32, 8, D), 0)
    lane3 = lax.broadcasted_iota(jnp.int32, (32, 8, D), 2)
    vec_ref[0:8, :] = jnp.sum(jnp.where(lane3 // ROWS == group, wide, 0.0), axis=0)
    spread = ((lane % 96 == row) & (row < 96)).astype(BF16)
    wide = dot_nn(small[:, :, 128:256].reshape(256, 128).astype(BF16), spread).reshape(4, 8, 8, D)
    second = lax.broadcasted_iota(jnp.int32, (4, 8, 8, D), 1)
    place = lax.broadcasted_iota(jnp.int32, (4, 8, 8, D), 2)
    lane4 = lax.broadcasted_iota(jnp.int32, (4, 8, 8, D), 3)
    chosen = jnp.where((lane4 // 96 == second) & (place == 0), wide, 0.0)
    inner_rows = jnp.sum(chosen, axis=1)
    for i in range(4):
        vec_ref[8 + i : 9 + i, :] = inner_rows[i, 0:1, :]
    vec_ref[12:16, :] = jnp.zeros((4, D), F32)

    x = x_ref[...]
    straighten(raw_k, 0, keep(wk_ref))
    k_ref[...] = dot_nt(x, wk_ref[...]).astype(BF16)
    settle(raw_q, sems.at[0])
    straighten(raw_q, 0, keep(wq_ref))
    q_ref[...] = (dot_nt(x, wq_ref[...]) + vec_ref[0:1, :]).astype(BF16)
    settle(raw_v, sems.at[2])
    straighten(raw_v, 0, keep(wv_ref))
    v_ref[...] = (dot_nt(x, wv_ref[...]) + vec_ref[1:2, :]).astype(BF16)


def project(table, core, layer_input, own, other):
    rows = jax.ShapeDtypeStruct((TOKENS, D), BF16)
    square = jax.ShapeDtypeStruct((D, D), BF16)
    return pl.pallas_call(
        project_kernel,
        in_specs=[SMEM, SMEM, VMEM] + [ANY] * 8,
        out_specs=[VMEM] * 7,
        out_shape=(rows, rows, rows, square, square, square, jax.ShapeDtypeStruct((16, D), F32)),
        scratch_shapes=[
            pltpu.VMEM((GROUPS, ROWS, D), BF16),
            pltpu.VMEM((GROUPS, 32, D), BF16),
            pltpu.VMEM((GROUPS, ROWS, D), BF16),
            pltpu.SemaphoreType.DMA((3,)),
        ],
        compiler_params=pltpu.CompilerParams(vmem_limit_bytes=LIMIT),
        cost_estimate=pl.CostEstimate(flops=2 * 10**9, bytes_accessed=12 * 10**6, transcendentals=0),
        name="project",
    )(table, core, layer_input, *own, *other)


def attend_kernel(counts, q_ref, k_ref, v_ref, prior_ref, *refs):
    raw_ref, probs_ref, mixed_ref = refs[-3:]
    query = q_ref[...] * jnp.asarray(HEAD ** (-0.5), BF16)
    key = k_ref[...]
    value = v_ref[...]
    low_lane = lax.broadcasted_iota(jnp.int32, (TOKENS, PAIR), 1) < HEAD
    segments = unit_segments(counts)
    results = []
    for head in range(2):
        chosen = low_lane if head == 0 else ~low_lane
        masked = jnp.where(chosen, query, jnp.zeros_like(query))
        products = dot_nt(masked, key)
        for block in range(DEV_UNITS):
            rows = slice(block * UNIT, (block + 1) * UNIT)
            allowed = allowed_lanes(segments, block)
            scores = products[rows] + prior_ref[head, rows, :].astype(F32)
            raw_ref[head, rows, :] = jnp.where(allowed, scores, 0.0).astype(BF16)
            scores = jnp.where(allowed, scores, -1e30)
            grown = jnp.exp(scores - jnp.max(scores, axis=-1, keepdims=True))
            total = jnp.sum(grown, axis=-1, keepdims=True)
            probs_ref[head, rows, :] = (grown * (1.0 / total)).astype(BF16)
        results.append(dot_nn(probs_ref[head], value))
    mixed_ref[...] = jnp.where(low_lane, results[0], results[1]).astype(BF16)


def attend(counts, queries, keys, values, prior_logits, first, last, held):
    columns = pl.BlockSpec((TOKENS, PAIR), lambda i, *_: (0, i + first))
    logits = pl.BlockSpec((2, TOKENS, TOKENS), lambda i, *_: (i + first, 0, 0))
    logits_shape = jax.ShapeDtypeStruct((H, TOKENS, TOKENS), BF16)
    pairs = last - first
    return pl.pallas_call(
        attend_kernel,
        grid_spec=pltpu.PrefetchScalarGridSpec(
            num_scalar_prefetch=1,
            grid=(pairs,),
            in_specs=[columns] * 3 + [logits] + [ANY] * len(held),
            out_specs=[logits, logits, columns],
        ),
        out_shape=(logits_shape, logits_shape, jax.ShapeDtypeStruct((TOKENS, D), BF16)),
        input_output_aliases={5 + i: i for i in range(len(held))},
        compiler_params=pltpu.CompilerParams(vmem_limit_bytes=LIMIT),
        cost_estimate=pl.CostEstimate(
            flops=pairs * 10**9, bytes_accessed=pairs * 5 * 10**6, transcendentals=pairs * 2**19
        ),
        name="attend_%d" % first,
    )(counts, queries, keys, values, prior_logits, *held)


def unit_segments(counts):
    start = [counts[0, 0], counts[0, 0] + 2 * counts[0, 1]]
    start.append(start[1] + 3 * counts[0, 2])
    segments = []
    current = jnp.int32(-1)
    for unit in range(DEV_UNITS):
        first = unit < start[0]
        second = (unit >= start[0]) & (unit < start[1]) & ((unit - start[0]) % 2 == 0)
        third = (unit >= start[1]) & (unit < start[2]) & ((unit - start[1]) % 3 == 0)
        fourth = (unit >= start[2]) & ((unit - start[2]) % 4 == 0)
        current = current + jnp.where(first | second | third | fourth, 1, 0)
        segments.append(current)
    return segments


def allowed_lanes(segments, block):
    unit = lax.broadcasted_iota(jnp.int32, (1, TOKENS), 1) // UNIT
    same = jnp.zeros((1, TOKENS), jnp.int32)
    for other in range(DEV_UNITS):
        same = jnp.where(unit == other, jnp.where(segments[other] == segments[block], 1, 0), same)
    return same > 0


def mean_of(values):
    return jnp.sum(values, axis=-1, keepdims=True) * (1.0 / D)


def normalise(values):
    centred = values - mean_of(values)
    scale = lax.rsqrt(mean_of(centred * centred) + EPSILON)
    return centred * scale, scale


def norm_back(slope, normal, scale):
    return scale * (slope - mean_of(slope) - normal * mean_of(slope * normal))


def fold(values):
    return jnp.sum(values.reshape(values.shape[0] // 8, 8, D), axis=0)


HALVES = (slice(0, 256), slice(256, 512))


def middle_kernel(table, core, x_ref, mixed_ref, cot_ref, vec_ref, *refs):
    own_b, other_b = refs[0:2], refs[2:4]
    own, other = refs[4:8], refs[8:12]
    y_ref, first_ref, mixed_low_ref, og_ref, vg_ref = refs[12:17]
    outs = refs[17:21]
    (
        raw_o,
        wo,
        w_in,
        raw_a,
        raw_b,
        w_out,
        active,
        curve,
        normed,
        normal,
        scales,
        total,
        low,
        low_t,
        d_in,
        d_out,
        sems,
    ) = refs[21:38]

    fetch(table, core, (None, None) + own_b, (None, None) + other_b, {(1, 1): (lambda g: raw_o.at[g], 0)}, sems)

    def inner_place(skip):
        return lambda g: w_in.at[pl.ds(pl.multiple_of(g * 96 + skip, 48), 48)]

    targets = {
        (0, 0): (inner_place(0), 1),
        (0, 1): (inner_place(48), 1),
        (1, 0): (lambda g: raw_a.at[g], 2),
        (1, 1): (lambda g: raw_b.at[g], 3),
    }
    fetch(table, core, own, other, targets, sems)

    def keep_wo(i, rows):
        wo[192 * i : 192 * (i + 1), :] = rows

    settle(raw_o, sems.at[0])
    straighten(raw_o, 0, keep_wo)
    for rows in HALVES:
        attended = dot_nt(mixed_ref[rows, :], wo[...]) + vec_ref[2:3, :]
        values, scale = normalise(x_ref[rows, :].astype(F32) + attended)
        normal[rows, :] = values
        scales[rows, :] = scale
        normed[rows, :] = (values * vec_ref[3:4, :] + vec_ref[4:5, :]).astype(BF16)

    def keep_out(part):
        def store(i, rows):
            w_out[192 * i : 192 * (i + 1), part * D : (part + 1) * D] = rows

        return store

    settle(w_in, sems.at[1])
    for j in range(12):
        columns = slice(256 * j, 256 * (j + 1))
        place = slice(256 * (j % 3), 256 * (j % 3 + 1))
        inner = dot_nt(normed[...], w_in[columns, :]) + vec_ref[8 + j // 3 : 9 + j // 3, place]
        bell = 0.5 * (1.0 + lax.erf(inner * (0.5**0.5)))
        active[:, columns] = (inner * bell).astype(BF16)
        slope = bell + inner * jnp.exp(inner * inner * -0.5) * 0.3989422804014327
        curve[:, columns] = slope.astype(BF16)
        if j == 3:
            settle(raw_a, sems.at[2])
            settle(raw_b, sems.at[3])
        if j in (4, 6, 8, 10):
            part = (j - 4) // 2
            straighten(raw_a if part < 2 else raw_b, ROWS * (part % 2), keep_out(part))

    gain_sum, shift_sum = 0.0, 0.0
    for rows in HALVES:
        for j in range(3):
            columns = slice(256 * j, 256 * (j + 1))
            total[rows, columns] = dot_nt(active[rows, :], w_out[columns, :])
        values, scale = normalise(normed[rows, :].astype(F32) + (total[rows, :] + vec_ref[5:6, :]))
        y_ref[rows, :] = (values * vec_ref[6:7, :] + vec_ref[7:8, :]).astype(BF16)
        given = cot_ref[rows, :].astype(F32)
        gain_sum += fold(given * values)
        shift_sum += fold(given)
        slope = norm_back(given * vec_ref[6:7, :], values, scale)
        total[rows, :] = slope
        low[rows, :] = slope.astype(BF16)

    vg_ref[...] = jnp.zeros_like(vg_ref)
    ones = jnp.ones((8, TOKENS), BF16)
    vg_ref[6:7, :] = jnp.sum(gain_sum, axis=0, keepdims=True)
    vg_ref[7:8, :] = jnp.sum(shift_sum, axis=0, keepdims=True)
    vg_ref[5:6, :] = dot_nn(ones, low[...])[0:1]
    low_t[...] = low[...].T

    for j in range(12):
        columns = slice(256 * j, 256 * (j + 1))
        place = slice(256 * (j % 3), 256 * (j % 3 + 1))
        grown = dot_nn(low_t[...], active[:, columns])
        d_out[j // 3, :, :, place] = grown.reshape(GROUPS, ROWS, 256).astype(BF16)
        slope = dot_nn(low[...], w_out[:, columns])
        curve[:, columns] = (slope * curve[:, columns].astype(F32)).astype(BF16)

    for part in range(4):
        columns = slice(part * D, (part + 1) * D)
        grown = dot_tn(curve[:, columns], normed[...])
        d_in[8 * part : 8 * part + 8] = grown.reshape(8, 4, ROWS, D).astype(BF16)
        vg_ref[8 + part : 9 + part, :] = dot_nn(ones, curve[:, columns])[0:1]

    def send(parts, half, row, sem):
        for part in range(2):
            target = parts[part]

            def body(i, carry):
                group = table[row + part, i]
                if half == 0:
                    pltpu.make_async_copy(
                        d_in.at[group, pl.ds(2 * part, 2)], target.at[i], sems.at[sem + part]
                    ).start()
                else:
                    for k in range(2):
                        pltpu.make_async_copy(
                            d_out.at[2 * part + k, group], target.at[i, k], sems.at[sem + part]
                        ).start()
                return carry

            lax.fori_loop(0, GROUPS, body, 0)

    @pl.when(core[0] == 0)
    def _():
        send(outs[0:2], 0, 0, 4)
        send(outs[2:4], 1, 2, 6)

    @pl.when(core[0] != 0)
    def _():
        send(outs[0:2], 1, 0, 4)
        send(outs[2:4], 0, 2, 6)

    gain_sum, shift_sum = 0.0, 0.0
    for rows in HALVES:
        for j in range(3):
            columns = slice(256 * j, 256 * (j + 1))
            total[rows, columns] += dot_nn(curve[rows, :], w_in[:, columns])
        given = total[rows, :]
        values = normal[rows, :]
        gain_sum += fold(given * values)
        shift_sum += fold(given)
        slope = norm_back(given * vec_ref[3:4, :], values, scales[rows, :])
        first_ref[rows, :] = slope
        low[rows, :] = slope.astype(BF16)
        mixed_low_ref[rows, :] = dot_nn(low[rows, :], wo[...]).astype(BF16)
    vg_ref[3:4, :] = jnp.sum(gain_sum, axis=0, keepdims=True)
    vg_ref[4:5, :] = jnp.sum(shift_sum, axis=0, keepdims=True)
    vg_ref[2:3, :] = dot_nn(ones, low[...])[0:1]
    grown = dot_tn(low[...], mixed_ref[...]).reshape(GROUPS, ROWS, D)
    og_ref[...] = jnp.concatenate([grown, jnp.zeros((GROUPS, 8, D), F32)], axis=1).astype(BF16)
    for i in range(4):
        settle(outs[i], sems.at[4 + i])


def middle(table, core, layer_input, mixed, cotangent, vectors, own_b, other_b, own, other):
    part = jax.ShapeDtypeStruct((GROUPS, 2, ROWS, D), BF16)
    return pl.pallas_call(
        middle_kernel,
        in_specs=[SMEM, SMEM, VMEM, VMEM, VMEM, VMEM] + [ANY] * 12,
        out_specs=[VMEM] * 5 + [ANY] * 4,
        out_shape=(
            jax.ShapeDtypeStruct((TOKENS, D), BF16),
            jax.ShapeDtypeStruct((TOKENS, D), F32),
            jax.ShapeDtypeStruct((TOKENS, D), BF16),
            jax.ShapeDtypeStruct((GROUPS, 32, D), BF16),
            jax.ShapeDtypeStruct((16, D), F32),
            part,
            part,
            part,
            part,
        ),
        scratch_shapes=[
            pltpu.VMEM((GROUPS, 32, D), BF16),
            pltpu.VMEM((D, D), BF16),
            pltpu.VMEM((FF, D), BF16),
            pltpu.VMEM((GROUPS, 48, D), BF16),
            pltpu.VMEM((GROUPS, 48, D), BF16),
            pltpu.VMEM((D, FF), BF16),
            pltpu.VMEM((TOKENS, FF), BF16),
            pltpu.VMEM((TOKENS, FF), BF16),
            pltpu.VMEM((TOKENS, D), BF16),
            pltpu.VMEM((TOKENS, D), F32),
            pltpu.VMEM((TOKENS, 1), F32),
            pltpu.VMEM((TOKENS, D), F32),
            pltpu.VMEM((TOKENS, D), BF16),
            pltpu.VMEM((D, TOKENS), BF16),
            pltpu.VMEM((GROUPS, 4, ROWS, D), BF16),
            pltpu.VMEM((4, GROUPS, ROWS, D), BF16),
            pltpu.SemaphoreType.DMA((8,)),
        ],
        compiler_params=pltpu.CompilerParams(vmem_limit_bytes=LIMIT),
        cost_estimate=pl.CostEstimate(flops=16 * 10**9, bytes_accessed=30 * 10**6, transcendentals=3145728),
        name="middle",
    )(table, core, layer_input, mixed, cotangent, vectors, *own_b, *other_b, *own, *other)


def pair_back(counts, q_ref, k_ref, v_ref, mixed_ref, slope_ref, probs_ref, cot_ref, out_ref):
    low_lane = lax.broadcasted_iota(jnp.int32, (TOKENS, PAIR), 1) < HEAD
    segments = unit_segments(counts)
    scale = jnp.asarray(HEAD ** (-0.5), BF16)
    slope = slope_ref[...]
    query = q_ref[...] * scale
    key = k_ref[...] * scale
    value = v_ref[...]
    product = slope.astype(F32) * mixed_ref[...].astype(F32)
    queries, keys, values = [], [], []
    for head in range(2):
        chosen = low_lane if head == 0 else ~low_lane
        masked = jnp.where(chosen, slope, jnp.zeros_like(slope))
        shared = jnp.sum(jnp.where(chosen, product, 0.0), axis=-1, keepdims=True)
        products = dot_nt(masked, value)
        for block in range(DEV_UNITS):
            rows = slice(block * UNIT, (block + 1) * UNIT)
            allowed = allowed_lanes(segments, block)
            grown = probs_ref[head, rows, :].astype(F32) * (products[rows] - shared[rows])
            grown = grown + jnp.where(allowed, cot_ref[head, rows, :].astype(F32), 0.0)
            out_ref[head, rows, :] = grown.astype(BF16)
        logits = out_ref[head]
        heads = slice(head * HEAD, (head + 1) * HEAD)
        queries.append(dot_nn(logits, key))
        keys.append(dot_tn(query[:, heads], logits))
        values.append(dot_tn(slope[:, heads], probs_ref[head]))
    return (
        jnp.where(low_lane, queries[0], queries[1]).astype(BF16),
        jnp.concatenate(keys, axis=0).astype(BF16),
        jnp.concatenate(values, axis=0).astype(BF16),
    )


def attend_back_kernel(counts, *refs):
    dq_ref, dk_ref, dv_ref = refs[8:11]
    dq_ref[...], dk_ref[...], dv_ref[...] = pair_back(counts, *refs[0:8])


FIRST = 2


def attend_back(counts, queries, keys, values, mixed, mixed_low, probs, logits_cotangent):
    columns = pl.BlockSpec((TOKENS, PAIR), lambda i, *_: (0, i))
    turned = pl.BlockSpec((PAIR, TOKENS), lambda i, *_: (i, 0))
    logits = pl.BlockSpec((2, TOKENS, TOKENS), lambda i, *_: (i, 0, 0))
    return pl.pallas_call(
        attend_back_kernel,
        grid_spec=pltpu.PrefetchScalarGridSpec(
            num_scalar_prefetch=1,
            grid=(FIRST,),
            in_specs=[columns] * 5 + [logits] * 2,
            out_specs=[logits, columns, turned, turned],
        ),
        out_shape=(
            jax.ShapeDtypeStruct((H, TOKENS, TOKENS), BF16),
            jax.ShapeDtypeStruct((TOKENS, PAIR * FIRST), BF16),
            jax.ShapeDtypeStruct((PAIR * FIRST, TOKENS), BF16),
            jax.ShapeDtypeStruct((PAIR * FIRST, TOKENS), BF16),
        ),
        compiler_params=pltpu.CompilerParams(vmem_limit_bytes=LIMIT),
        cost_estimate=pl.CostEstimate(flops=2 * 10**9, bytes_accessed=7 * 10**6, transcendentals=0),
        name="attend_back_first",
    )(counts, queries, keys, values, mixed, mixed_low, probs, logits_cotangent)


def rest_kernel(table, core, counts, *refs):
    x_ref, dq1_ref, dk1_ref, dv1_ref, og_ref, vg_ref = refs[7:13]
    out_ref, dq_ref, dk_ref, dv_ref = refs[14:18]
    outs = refs[18:22]
    grown_q, grown_k, grown_v, d_q, d_k, d_v, sems = refs[22:29]
    step = pl.program_id(0)
    x = x_ref[...]

    @pl.when(step == 0)
    def _():
        rows = slice(0, PAIR * FIRST)
        dq_ref[:, rows] = dq1_ref[...]
        dk_ref[rows, :] = dk1_ref[...]
        dv_ref[rows, :] = dv1_ref[...]
        grown_q[rows, :] = dot_tn(dq1_ref[...], x)
        grown_k[rows, :] = dot_nn(dk1_ref[...], x)
        grown_v[rows, :] = dot_nn(dv1_ref[...], x)

    dq, dk, dv = pair_back(counts, *refs[0:7], out_ref)
    rows = pl.ds(pl.multiple_of((step + FIRST) * PAIR, PAIR), PAIR)
    dq_ref[:, rows] = dq
    dk_ref[rows, :] = dk
    dv_ref[rows, :] = dv
    grown_q[rows, :] = dot_tn(dq, x)
    grown_k[rows, :] = dot_nn(dk, x)
    grown_v[rows, :] = dot_nn(dv, x)

    @pl.when(step == pl.num_programs(0) - 1)
    def _():
        ones = jnp.ones((8, TOKENS), BF16)
        query_sum = dot_nn(ones, dq_ref[...])[0:1]
        value_sum = dot_nt(ones, dv_ref[...])[0:1]
        rows8 = lax.broadcasted_iota(jnp.int32, (8, D), 0)
        offsets = vg_ref[0:8, :]
        offsets = jnp.where(rows8 == 0, query_sum, jnp.where(rows8 == 1, value_sum, offsets))
        group = lax.broadcasted_iota(jnp.int32, (32, 8, D), 0)
        lane = lax.broadcasted_iota(jnp.int32, (32, 8, D), 2)
        chosen = jnp.where(lane // ROWS == group, offsets[None], 0.0)
        row = lax.broadcasted_iota(jnp.int32, (D, 128), 0)
        column = lax.broadcasted_iota(jnp.int32, (D, 128), 1)
        narrow = dot_nn(chosen.reshape(256, D).astype(BF16), (row % ROWS == column).astype(BF16))
        wide = jnp.broadcast_to(vg_ref[8:12, :][:, None, :], (4, 8, D))
        second = lax.broadcasted_iota(jnp.int32, (4, 8, D), 1)
        lane = lax.broadcasted_iota(jnp.int32, (4, 8, D), 2)
        chosen = jnp.where(lane // 96 == second, wide, 0.0).reshape(32, D)
        inner = dot_nn(chosen.astype(BF16), (row % 96 == column).astype(BF16))
        place = lax.broadcasted_iota(jnp.int32, (32, 8, 128), 1)
        inner = jnp.where(place == 0, inner[:, None, :], 0.0)
        small = jnp.concatenate(
            [narrow.reshape(32, 8, 128), inner, jnp.zeros((32, 8, D - 256), F32)], axis=2
        )
        d_q[...] = grown_q[...].reshape(GROUPS, ROWS, D).astype(BF16)
        d_v[...] = grown_v[...].reshape(GROUPS, ROWS, D).astype(BF16)
        d_k[...] = jnp.concatenate([grown_k[...].reshape(GROUPS, ROWS, D), small], axis=1).astype(BF16)

        def send(parts, half, row, sem):
            sources = (d_q, d_k) if half == 0 else (d_v, og_ref)
            for part in range(2):

                def body(i, carry):
                    pltpu.make_async_copy(
                        sources[part].at[table[row + part, i]], parts[part].at[i], sems.at[sem + part]
                    ).start()
                    return carry

                lax.fori_loop(0, GROUPS, body, 0)

        @pl.when(core[0] == 0)
        def _():
            send(outs[2:4], 1, 2, 2)
            send(outs[0:2], 0, 0, 0)

        @pl.when(core[0] != 0)
        def _():
            send(outs[2:4], 0, 2, 2)
            send(outs[0:2], 1, 0, 0)

        for i in range(4):
            settle(outs[i], sems.at[i])


def rest(table, core, counts, queries, keys, values, mixed, mixed_low, probs, logits_cotangent, layer_input, held, og, vg):
    columns = pl.BlockSpec((TOKENS, PAIR), lambda i, *_: (0, i + FIRST))
    logits = pl.BlockSpec((2, TOKENS, TOKENS), lambda i, *_: (i + FIRST, 0, 0))

    def whole(shape):
        return pl.BlockSpec(shape, lambda i, *_: (0,) * len(shape))

    part_a = jax.ShapeDtypeStruct((GROUPS, ROWS, D), BF16)
    part_b = jax.ShapeDtypeStruct((GROUPS, 32, D), BF16)
    return pl.pallas_call(
        rest_kernel,
        grid_spec=pltpu.PrefetchScalarGridSpec(
            num_scalar_prefetch=3,
            grid=(H // 2 - FIRST,),
            in_specs=[columns] * 5
            + [logits] * 2
            + [
                whole((TOKENS, D)),
                whole((TOKENS, PAIR * FIRST)),
                whole((PAIR * FIRST, TOKENS)),
                whole((PAIR * FIRST, TOKENS)),
                whole((GROUPS, 32, D)),
                whole((16, D)),
                ANY,
            ],
            out_specs=[logits, whole((TOKENS, D)), whole((D, TOKENS)), whole((D, TOKENS))] + [ANY] * 4,
            scratch_shapes=[
                pltpu.VMEM((D, D), F32),
                pltpu.VMEM((D, D), F32),
                pltpu.VMEM((D, D), F32),
                pltpu.VMEM((GROUPS, ROWS, D), BF16),
                pltpu.VMEM((GROUPS, 32, D), BF16),
                pltpu.VMEM((GROUPS, ROWS, D), BF16),
                pltpu.SemaphoreType.DMA((4,)),
            ],
        ),
        out_shape=(
            jax.ShapeDtypeStruct((H, TOKENS, TOKENS), BF16),
            jax.ShapeDtypeStruct((TOKENS, D), BF16),
            jax.ShapeDtypeStruct((D, TOKENS), BF16),
            jax.ShapeDtypeStruct((D, TOKENS), BF16),
            part_a,
            part_b,
            part_a,
            part_b,
        ),
        input_output_aliases={16: 0},
        compiler_params=pltpu.CompilerParams(vmem_limit_bytes=LIMIT),
        cost_estimate=pl.CostEstimate(flops=6 * 10**9, bytes_accessed=25 * 10**6, transcendentals=0),
        name="attend_back_rest",
    )(
        table,
        core,
        counts,
        queries,
        keys,
        values,
        mixed,
        mixed_low,
        probs,
        logits_cotangent,
        layer_input,
        held[1],
        held[2],
        held[3],
        og,
        vg,
        held[0],
    )


def pack_kernel(core, *refs):
    query, key, value, output, inner, outer = refs[0:6]
    small = refs[6:15]
    mine_ref, other_ref, first, second = refs[15:19]
    first[...] = jnp.zeros_like(first)
    second[...] = jnp.zeros_like(second)
    first[0:6, :] = query[...].astype(F32)
    first[6:12, :] = key[...].astype(F32)
    first[12:36, :] = inner[...].astype(F32)
    for i, ref in enumerate(small):
        row, lane = 36 + i // 6, 128 * (i % 6)
        first[row : row + 1, lane : lane + ref.shape[1]] = ref[...].astype(F32)
    second[0:6, :] = value[...].astype(F32)
    second[6:12, :] = output[...].astype(F32)
    for i in range(4):
        second[12 + 6 * i : 18 + 6 * i, :] = outer[:, D * i : D * (i + 1)].astype(F32)

    @pl.when(core[0] == 0)
    def _():
        mine_ref[...] = first[...].astype(BF16)
        other_ref[...] = second[...].astype(BF16)

    @pl.when(core[0] != 0)
    def _():
        mine_ref[...] = second[...].astype(BF16)
        other_ref[...] = first[...].astype(BF16)


def pack(core, kernels, small):
    half = jax.ShapeDtypeStruct((40, D), BF16)
    return pl.pallas_call(
        pack_kernel,
        in_specs=[SMEM] + [VMEM] * 15,
        out_specs=[VMEM] * 2,
        out_shape=(half, half),
        scratch_shapes=[pltpu.VMEM((40, D), F32)] * 2,
        name="pack",
    )(core, *(kernel.T for kernel in kernels), *(v.reshape(1, -1) for v in small))


def finish_kernel(place, ff_own, ff_other, tail_own, tail_other, query, key, value, output, inner, outer, *small):
    def write(mine, ff_first, ff_second, tail_first, tail_second):
        rows = slice(6 * mine, 6 * mine + 6)
        for ref, part, skip in (
            (query, tail_first, 0),
            (key, tail_first, 24),
            (value, tail_second, 0),
            (output, tail_second, 24),
        ):
            ref[...] = part[skip + rows.start : skip + rows.stop, :]
        inner[...] = ff_first[24 * mine : 24 * mine + 24, :]
        for i in range(4):
            outer[:, D * i : D * (i + 1)] = ff_second[24 * i + rows.start : 24 * i + rows.stop, :]
        for i in range(8):
            small[i][...] = tail_first[48 + i : 49 + i, rows]
        small[8][...] = tail_first[48:49, 128 + 24 * mine : 152 + 24 * mine]

    for mine in range(4):

        @pl.when(place[0] == mine)
        def _():
            if mine < 2:
                write(mine, ff_own, ff_other, tail_own, tail_other)
            else:
                write(mine, ff_other, ff_own, tail_other, tail_own)


def finish(mine, ff_own, ff_other, tail_own, tail_other):
    narrow = jax.ShapeDtypeStruct((6, D), F32)
    outs = pl.pallas_call(
        finish_kernel,
        in_specs=[SMEM] + [VMEM] * 4,
        out_specs=[VMEM] * 15,
        out_shape=(
            narrow,
            narrow,
            narrow,
            narrow,
            jax.ShapeDtypeStruct((24, D), F32),
            jax.ShapeDtypeStruct((6, FF), F32),
        )
        + (jax.ShapeDtypeStruct((1, 6), F32),) * 8
        + (jax.ShapeDtypeStruct((1, 24), F32),),
        name="finish",
    )(mine.astype(jnp.int32).reshape(1), ff_own, ff_other, tail_own, tail_other)
    return tuple(out.T for out in outs[:6]) + tuple(out.reshape(-1) for out in outs[6:])


def gather_weights(core_table, kernels, vectors, inner_offset):
    core, low_x = lax.axis_index("c"), lax.axis_index("xl")
    mine = core * 2 + low_x
    own, other = pack(core_table, kernels, (*vectors, inner_offset))
    pieces = jnp.stack(
        [
            own,
            swap(own, "xl"),
            swap(other, "c"),
            lax.ppermute(other, ("c", "xl"), [(i, 3 - i) for i in range(4)]),
        ]
    )
    natural = jnp.concatenate(
        [lax.dynamic_slice_in_dim(pieces, mine ^ i, 1, axis=0) for i in range(4)], axis=0
    )
    first = core == 0
    near_a = natural[:, 0:6].reshape(ROWS, D)
    near_b = natural[:, 6:12].reshape(ROWS, D)
    inner = natural[:, 12:36].reshape(96, D)
    outer = natural[:, 12:36].reshape(4, 4, 6, D).transpose(1, 0, 2, 3).reshape(96, D)
    offsets = natural[:, 36:38].reshape(4, 12, 128)[:, 0:8, 0:6].transpose(1, 0, 2).reshape(8, ROWS)
    offsets = jnp.pad(offsets, ((0, 0), (0, 128 - ROWS)))
    wide_offset = jnp.pad(natural[:, 37, 256:280].reshape(1, 96), ((0, 7), (0, 32)))
    small = jnp.concatenate([offsets, wide_offset, jnp.zeros((8, D - 256), BF16)], axis=1)
    wide = jnp.where(first, inner, outer)
    block = jnp.concatenate([near_a, wide[0:48], near_b, small, wide[48:96]], axis=0)
    both = jnp.stack([block, exchange(block, STEPS_A[0])])
    part_a, part_b = both[:, 0:72], both[:, 72:152]
    for i in (1, 2):
        arrived_a, arrived_b = after((exchange(part_a, STEPS_A[i]), exchange(part_b, STEPS_B[i])))
        part_a = jnp.concatenate([part_a, arrived_a], axis=0)
        part_b = jnp.concatenate([part_b, arrived_b], axis=0)
    arrived_a, arrived_b = after((exchange(part_a, STEPS_A[3]), exchange(part_b, STEPS_B[3])))
    near_a = jnp.concatenate([part_a[:, 0:24], arrived_a[:, 0:24]], axis=0)
    near_b = jnp.concatenate([part_b[:, 0:32], arrived_b[:, 0:32]], axis=0)
    far_a = jnp.concatenate([part_a[:, 24:72], arrived_a[:, 24:72]], axis=0)
    far_b = jnp.concatenate([part_b[:, 32:80], arrived_b[:, 32:80]], axis=0)
    last_a, last_b = exchange(near_a, STEPS_A[4]), exchange(near_b, STEPS_B[4])
    far_a, far_b, last_a, last_b = after((far_a, far_b, last_a, last_b))
    near = (near_a, last_a, near_b, last_b)
    return near, tuple(swap(part, "c") for part in near), (far_a, far_b)


def after(values, *others):
    return lax.optimization_barrier((values, others))[0] if others else lax.optimization_barrier(values)


def add(first, second):
    return (first.astype(F32) + second.astype(F32)).astype(BF16)


def add3(first, second, third):
    return (first.astype(F32) + second.astype(F32) + third.astype(F32)).astype(BF16)


def split(*arrays):
    half = arrays[0].shape[0] // 2
    combine = add if len(arrays) == 2 else add3
    return combine(*(a[:half] for a in arrays)), combine(*(a[half:] for a in arrays))


def halve(total, step):
    return split(total[0], exchange(total[1], step))


def reduce_end(total_a, total_b):
    kept, sent = (
        jnp.concatenate([total_a[i].reshape(-1, D), total_b[i].reshape(-1, D)], axis=0) for i in range(2)
    )
    total = add(kept, exchange(sent, STEPS_A[0]))
    own = total.astype(F32) + swap(total, "xl").astype(F32)
    return own, swap(own, "c")


def body(
    layer_input,
    prior_logits,
    bucket_counts,
    output_cotangent,
    logits_cotangent,
    query_kernel,
    query_offset,
    key_kernel,
    value_kernel,
    value_offset,
    output_kernel,
    output_offset,
    first_gain,
    first_shift,
    inner_kernel,
    inner_offset,
    outer_kernel,
    outer_offset,
    second_gain,
    second_shift,
):
    core, low_x = lax.axis_index("c"), lax.axis_index("xl")
    mine = core * 2 + low_x
    table = jnp.stack(
        [
            position_groups(STEPS_A, core),
            position_groups(STEPS_B, core),
            position_groups(STEPS_A, 1 - core),
            position_groups(STEPS_B, 1 - core),
        ]
    )
    core_table = core.astype(jnp.int32).reshape(1)
    near, near_other, far = gather_weights(
        core_table,
        (query_kernel, key_kernel, value_kernel, output_kernel, inner_kernel, outer_kernel),
        (
            query_offset,
            value_offset,
            output_offset,
            first_gain,
            first_shift,
            outer_offset,
            second_gain,
            second_shift,
        ),
        inner_offset,
    )
    far_last = (exchange(far[0], STEPS_A[4]), exchange(far[1], STEPS_B[4]))
    far_other = [swap(far[0], "c"), None, swap(far[1], "c"), None]
    queries, keys, values, query_matrix, key_matrix, value_matrix, vectors = project(
        table, core_table, layer_input, near, near_other
    )
    held = attend(bucket_counts, queries, keys, values, prior_logits, 0, 3, ())
    far_last, held = after((far_last, held))
    far_other[1], far_other[3] = swap(far_last[0], "c"), swap(far_last[1], "c")
    raw_logits, probs, mixed = attend(bucket_counts, queries, keys, values, prior_logits, 3, 6, held)
    layer_output, first_slope, mixed_low, output_slope, vector_slopes, *ff = middle(
        table,
        core_table,
        layer_input,
        mixed,
        output_cotangent,
        vectors,
        near[2:4],
        near_other[2:4],
        (far[0], far_last[0], far[1], far_last[1]),
        far_other,
    )

    moved = [swap(ff[2], "c"), swap(ff[3], "c")]
    heads = (queries, keys, values, mixed, mixed_low, probs, logits_cotangent)
    held = attend_back(bucket_counts, *heads)
    moved, held = after((moved, held))
    half = GROUPS // 2
    sent_a, sent_b = add(ff[0][half:], moved[0][half:]), add(ff[1][half:], moved[1][half:])
    held, sent_a, sent_b = after((held, sent_a, sent_b))
    logits_slope, dq, dk, dv, *tail = rest(
        table, core_table, bucket_counts, *heads, layer_input, held, output_slope, vector_slopes
    )
    arrived_a, arrived_b = exchange(sent_a, STEPS_A[4]), exchange(sent_b, STEPS_B[4])
    arrived_a, arrived_b, tail = after((arrived_a, arrived_b, tuple(tail)))
    tail_moved = [swap(tail[2], "c"), swap(tail[3], "c")]
    tail_sent = [add(tail[i][half:], tail_moved[i][half:]) for i in range(2)]
    arrived_a, arrived_b, tail_sent = after((arrived_a, arrived_b, tail_sent))
    ff_a = split(ff[0][:half], moved[0][:half], arrived_a)
    ff_b = split(ff[1][:half], moved[1][:half], arrived_b)
    tail_a = split(tail[0][:half], tail_moved[0][:half], exchange(tail_sent[0], STEPS_A[4]))
    tail_b = split(tail[1][:half], tail_moved[1][:half], exchange(tail_sent[1], STEPS_B[4]))
    for i in (3, 2, 1):
        tail_a, tail_b = halve(tail_a, STEPS_A[i]), halve(tail_b, STEPS_B[i])
        ff_a, ff_b = halve(ff_a, STEPS_A[i]), halve(ff_b, STEPS_B[i])
    ff_sums = reduce_end(ff_a, ff_b)
    tail_sums = reduce_end(tail_a, tail_b)
    query_owned, key_owned, value_owned, output_owned, inner_owned, outer_owned, *small = finish(
        mine, *ff_sums, *tail_sums
    )
    input_slope = (
        first_slope + dot_nn(dq, query_matrix) + dot_tn(dk, key_matrix) + dot_tn(dv, value_matrix)
    ).astype(BF16)

    return (
        layer_output,
        raw_logits,
        input_slope,
        logits_slope,
        query_owned,
        small[0],
        key_owned,
        value_owned,
        small[1],
        output_owned,
        small[2],
        small[3],
        small[4],
        inner_owned,
        small[8],
        outer_owned,
        small[5],
        small[6],
        small[7],
    )


def solution(mesh):
    fine = Mesh(mesh.devices.reshape(SIZES), AXES)
    rows = P(AXES, None)
    logits = P(None, AXES, None)
    columns = P(None, AXES)
    vector = P(AXES)
    return jax.shard_map(
        body,
        mesh=fine,
        in_specs=(
            rows,
            logits,
            rows,
            rows,
            logits,
            columns,
            vector,
            columns,
            columns,
            vector,
            columns,
            vector,
            vector,
            vector,
            columns,
            vector,
            columns,
            vector,
            vector,
            vector,
        ),
        out_specs=(
            rows,
            logits,
            rows,
            logits,
            columns,
            vector,
            columns,
            columns,
            vector,
            columns,
            vector,
            vector,
            vector,
            columns,
            vector,
            columns,
            vector,
            vector,
            vector,
        ),
        check_vma=False,
    )
```

```python
import jax
import jax.numpy as jnp
from jax import lax
from jax.experimental import pallas as pl
from jax.experimental.pallas import tpu as pltpu
from jax.sharding import Mesh
from jax.sharding import PartitionSpec as P

D = 768
H = 12
HEAD = 64
FF = 3072
UNIT = 128
DEV_UNITS = 4
EPSILON = 1e-12

AXES = ("xh", "z", "y", "c", "xl")
SIZES = (2, 4, 4, 2, 2)
GROUPS = 32
ROWS = 24
MASKS = ((1, 3), (3, 1))
STEPS_A = (("x", 0), ("z", 0), ("z", 1), ("y", 0), ("y", 1))
STEPS_B = (("x", 0), ("y", 0), ("y", 1), ("z", 0), ("z", 1))
BF16 = jnp.bfloat16
F32 = jnp.float32


def exchange(values, step):
    axis, turn = step
    if axis == "x":
        return lax.ppermute(values, ("xh", "xl"), [(i, 3 - i) for i in range(4)])
    pairs = []
    for i in range(4):
        for core in range(2):
            pairs.append((i * 2 + core, (i ^ MASKS[core][turn]) * 2 + core))
    return lax.ppermute(values, (axis, "c"), pairs)


def swap(values, axis):
    return lax.ppermute(values, axis, [(0, 1), (1, 0)])


def position_groups(steps, core):
    position = jnp.arange(GROUPS, dtype=jnp.int32)
    place = {
        "x": jnp.full((GROUPS,), lax.axis_index("xh"), jnp.int32),
        "y": jnp.full((GROUPS,), lax.axis_index("y"), jnp.int32),
        "z": jnp.full((GROUPS,), lax.axis_index("z"), jnp.int32),
    }
    for bit, (axis, turn) in enumerate(steps):
        if axis == "x":
            mask = 1
        else:
            mask = jnp.where(core == 0, MASKS[0][turn], MASKS[1][turn])
        place[axis] = place[axis] ^ (((position >> bit) & 1) * mask)
    return (place["x"] * 4 + place["z"]) * 4 + place["y"]


ANY = pl.BlockSpec(memory_space=pl.ANY)
VMEM = pl.BlockSpec(memory_space=pltpu.VMEM)
SMEM = pl.BlockSpec(memory_space=pltpu.SMEM)
TOKENS = 512
PAIR = 2 * HEAD
LIMIT = 58 * 1024 * 1024


def dot_nt(rows, matrix):
    return lax.dot_general(rows, matrix, (((1,), (1,)), ((), ())), preferred_element_type=F32)


def dot_nn(rows, matrix):
    return lax.dot_general(rows, matrix, (((1,), (0,)), ((), ())), preferred_element_type=F32)


def dot_tn(rows, matrix):
    return lax.dot_general(rows, matrix, (((0,), (0,)), ((), ())), preferred_element_type=F32)


def fetch(table, core, own, other, targets, sems):
    def place(parts, half, row):
        for part in range(2):
            if (half, part) not in targets:
                continue
            where, sem = targets[half, part]
            for second in range(2):
                source = parts[2 * part + second]

                def body(i, carry):
                    group = table[row + part, i + 16 * second]
                    pltpu.make_async_copy(source.at[i], where(group), sems.at[sem]).start()
                    return carry

                lax.fori_loop(0, 16, body, 0)

    @pl.when(core[0] == 0)
    def _():
        place(own, 0, 0)
        place(other, 1, 2)

    @pl.when(core[0] != 0)
    def _():
        place(own, 1, 0)
        place(other, 0, 2)


def settle(ref, sem):
    pltpu.make_async_copy(ref, ref, sem).wait()


def straighten(raw, skip, store):
    for i in range(4):
        block = raw[8 * i : 8 * i + 8].astype(F32)[:, skip : skip + ROWS]
        store(i, block.reshape(8 * ROWS, D).astype(BF16))


def project_kernel(table, core, x_ref, *refs):
    own, other = refs[0:4], refs[4:8]
    q_ref, k_ref, v_ref, wq_ref, wk_ref, wv_ref, vec_ref = refs[8:15]
    raw_q, raw_k, raw_v, sems = refs[15:19]
    targets = {
        (0, 0): (lambda g: raw_q.at[g], 0),
        (0, 1): (lambda g: raw_k.at[g], 1),
        (1, 0): (lambda g: raw_v.at[g], 2),
    }
    fetch(table, core, own, other, targets, sems)

    def keep(ref):
        def store(i, rows):
            ref[192 * i : 192 * (i + 1), :] = rows

        return store

    settle(raw_k, sems.at[1])
    small = raw_k[...].astype(F32)[:, ROWS : ROWS + 8, 0:256]
    row = lax.broadcasted_iota(jnp.int32, (128, D), 0)
    lane = lax.broadcasted_iota(jnp.int32, (128, D), 1)
    spread = (lane % ROWS == row).astype(BF16)
    wide = dot_nn(small[:, :, 0:128].reshape(256, 128).astype(BF16), spread).reshape(32, 8, D)
    group = lax.broadcasted_iota(jnp.int32, (32, 8, D), 0)
    lane3 = lax.broadcasted_iota(jnp.int32, (32, 8, D), 2)
    vec_ref[0:8, :] = jnp.sum(jnp.where(lane3 // ROWS == group, wide, 0.0), axis=0)
    spread = ((lane % 96 == row) & (row < 96)).astype(BF16)
    wide = dot_nn(small[:, :, 128:256].reshape(256, 128).astype(BF16), spread).reshape(4, 8, 8, D)
    second = lax.broadcasted_iota(jnp.int32, (4, 8, 8, D), 1)
    place = lax.broadcasted_iota(jnp.int32, (4, 8, 8, D), 2)
    lane4 = lax.broadcasted_iota(jnp.int32, (4, 8, 8, D), 3)
    chosen = jnp.where((lane4 // 96 == second) & (place == 0), wide, 0.0)
    inner_rows = jnp.sum(chosen, axis=1)
    for i in range(4):
        vec_ref[8 + i : 9 + i, :] = inner_rows[i, 0:1, :]
    vec_ref[12:16, :] = jnp.zeros((4, D), F32)

    x = x_ref[...]
    straighten(raw_k, 0, keep(wk_ref))
    k_ref[...] = dot_nt(x, wk_ref[...]).astype(BF16)
    settle(raw_q, sems.at[0])
    straighten(raw_q, 0, keep(wq_ref))
    q_ref[...] = (dot_nt(x, wq_ref[...]) + vec_ref[0:1, :]).astype(BF16)
    settle(raw_v, sems.at[2])
    straighten(raw_v, 0, keep(wv_ref))
    v_ref[...] = (dot_nt(x, wv_ref[...]) + vec_ref[1:2, :]).astype(BF16)


def project(table, core, layer_input, own, other):
    rows = jax.ShapeDtypeStruct((TOKENS, D), BF16)
    square = jax.ShapeDtypeStruct((D, D), BF16)
    return pl.pallas_call(
        project_kernel,
        in_specs=[SMEM, SMEM, VMEM] + [ANY] * 8,
        out_specs=[VMEM] * 7,
        out_shape=(rows, rows, rows, square, square, square, jax.ShapeDtypeStruct((16, D), F32)),
        scratch_shapes=[
            pltpu.VMEM((GROUPS, ROWS, D), BF16),
            pltpu.VMEM((GROUPS, 32, D), BF16),
            pltpu.VMEM((GROUPS, ROWS, D), BF16),
            pltpu.SemaphoreType.DMA((3,)),
        ],
        compiler_params=pltpu.CompilerParams(vmem_limit_bytes=LIMIT),
        cost_estimate=pl.CostEstimate(flops=2 * 10**9, bytes_accessed=12 * 10**6, transcendentals=0),
        name="project",
    )(table, core, layer_input, *own, *other)


def attend_kernel(counts, q_ref, k_ref, v_ref, prior_ref, *refs):
    raw_ref, probs_ref, mixed_ref = refs[-3:]
    query = q_ref[...] * jnp.asarray(HEAD ** (-0.5), BF16)
    key = k_ref[...]
    value = v_ref[...]
    low_lane = lax.broadcasted_iota(jnp.int32, (TOKENS, PAIR), 1) < HEAD
    segments = unit_segments(counts)
    results = []
    for head in range(2):
        chosen = low_lane if head == 0 else ~low_lane
        masked = jnp.where(chosen, query, jnp.zeros_like(query))
        products = dot_nt(masked, key)
        for block in range(DEV_UNITS):
            rows = slice(block * UNIT, (block + 1) * UNIT)
            allowed = allowed_lanes(segments, block)
            scores = products[rows] + prior_ref[head, rows, :].astype(F32)
            raw_ref[head, rows, :] = jnp.where(allowed, scores, 0.0).astype(BF16)
            scores = jnp.where(allowed, scores, -1e30)
            grown = jnp.exp(scores - jnp.max(scores, axis=-1, keepdims=True))
            total = jnp.sum(grown, axis=-1, keepdims=True)
            probs_ref[head, rows, :] = (grown * (1.0 / total)).astype(BF16)
        results.append(dot_nn(probs_ref[head], value))
    mixed_ref[...] = jnp.where(low_lane, results[0], results[1]).astype(BF16)


def attend(counts, queries, keys, values, prior_logits, first, last, held):
    columns = pl.BlockSpec((TOKENS, PAIR), lambda i, *_: (0, i + first))
    logits = pl.BlockSpec((2, TOKENS, TOKENS), lambda i, *_: (i + first, 0, 0))
    logits_shape = jax.ShapeDtypeStruct((H, TOKENS, TOKENS), BF16)
    pairs = last - first
    return pl.pallas_call(
        attend_kernel,
        grid_spec=pltpu.PrefetchScalarGridSpec(
            num_scalar_prefetch=1,
            grid=(pairs,),
            in_specs=[columns] * 3 + [logits] + [ANY] * len(held),
            out_specs=[logits, logits, columns],
        ),
        out_shape=(logits_shape, logits_shape, jax.ShapeDtypeStruct((TOKENS, D), BF16)),
        input_output_aliases={5 + i: i for i in range(len(held))},
        compiler_params=pltpu.CompilerParams(vmem_limit_bytes=LIMIT),
        cost_estimate=pl.CostEstimate(
            flops=pairs * 10**9, bytes_accessed=pairs * 5 * 10**6, transcendentals=pairs * 2**19
        ),
        name="attend_%d" % first,
    )(counts, queries, keys, values, prior_logits, *held)


def unit_segments(counts):
    start = [counts[0, 0], counts[0, 0] + 2 * counts[0, 1]]
    start.append(start[1] + 3 * counts[0, 2])
    segments = []
    current = jnp.int32(-1)
    for unit in range(DEV_UNITS):
        first = unit < start[0]
        second = (unit >= start[0]) & (unit < start[1]) & ((unit - start[0]) % 2 == 0)
        third = (unit >= start[1]) & (unit < start[2]) & ((unit - start[1]) % 3 == 0)
        fourth = (unit >= start[2]) & ((unit - start[2]) % 4 == 0)
        current = current + jnp.where(first | second | third | fourth, 1, 0)
        segments.append(current)
    return segments


def allowed_lanes(segments, block):
    unit = lax.broadcasted_iota(jnp.int32, (1, TOKENS), 1) // UNIT
    same = jnp.zeros((1, TOKENS), jnp.int32)
    for other in range(DEV_UNITS):
        same = jnp.where(unit == other, jnp.where(segments[other] == segments[block], 1, 0), same)
    return same > 0


def mean_of(values):
    return jnp.sum(values, axis=-1, keepdims=True) * (1.0 / D)


def normalise(values):
    centred = values - mean_of(values)
    scale = lax.rsqrt(mean_of(centred * centred) + EPSILON)
    return centred * scale, scale


def norm_back(slope, normal, scale):
    return scale * (slope - mean_of(slope) - normal * mean_of(slope * normal))


def fold(values):
    return jnp.sum(values.reshape(values.shape[0] // 8, 8, D), axis=0)


HALVES = (slice(0, 256), slice(256, 512))


def middle_kernel(table, core, x_ref, mixed_ref, cot_ref, vec_ref, *refs):
    own_b, other_b = refs[0:2], refs[2:4]
    own, other = refs[4:8], refs[8:12]
    y_ref, first_ref, mixed_low_ref, og_ref, vg_ref = refs[12:17]
    outs = refs[17:21]
    (
        raw_o,
        wo,
        w_in,
        raw_a,
        raw_b,
        w_out,
        active,
        curve,
        normed,
        normal,
        scales,
        total,
        low,
        low_t,
        d_in,
        d_out,
        sems,
    ) = refs[21:38]

    fetch(table, core, (None, None) + own_b, (None, None) + other_b, {(1, 1): (lambda g: raw_o.at[g], 0)}, sems)

    def inner_place(skip):
        return lambda g: w_in.at[pl.ds(pl.multiple_of(g * 96 + skip, 48), 48)]

    targets = {
        (0, 0): (inner_place(0), 1),
        (0, 1): (inner_place(48), 1),
        (1, 0): (lambda g: raw_a.at[g], 2),
        (1, 1): (lambda g: raw_b.at[g], 3),
    }
    fetch(table, core, own, other, targets, sems)

    def keep_wo(i, rows):
        wo[192 * i : 192 * (i + 1), :] = rows

    settle(raw_o, sems.at[0])
    straighten(raw_o, 0, keep_wo)
    for rows in HALVES:
        attended = dot_nt(mixed_ref[rows, :], wo[...]) + vec_ref[2:3, :]
        values, scale = normalise(x_ref[rows, :].astype(F32) + attended)
        normal[rows, :] = values
        scales[rows, :] = scale
        normed[rows, :] = (values * vec_ref[3:4, :] + vec_ref[4:5, :]).astype(BF16)

    def keep_out(part):
        def store(i, rows):
            w_out[192 * i : 192 * (i + 1), part * D : (part + 1) * D] = rows

        return store

    settle(w_in, sems.at[1])
    for j in range(12):
        columns = slice(256 * j, 256 * (j + 1))
        place = slice(256 * (j % 3), 256 * (j % 3 + 1))
        inner = dot_nt(normed[...], w_in[columns, :]) + vec_ref[8 + j // 3 : 9 + j // 3, place]
        bell = 0.5 * (1.0 + lax.erf(inner * (0.5**0.5)))
        active[:, columns] = (inner * bell).astype(BF16)
        slope = bell + inner * jnp.exp(inner * inner * -0.5) * 0.3989422804014327
        curve[:, columns] = slope.astype(BF16)
        if j == 3:
            settle(raw_a, sems.at[2])
            settle(raw_b, sems.at[3])
        if j in (4, 6, 8, 10):
            part = (j - 4) // 2
            straighten(raw_a if part < 2 else raw_b, ROWS * (part % 2), keep_out(part))

    gain_sum, shift_sum = 0.0, 0.0
    for rows in HALVES:
        for j in range(3):
            columns = slice(256 * j, 256 * (j + 1))
            total[rows, columns] = dot_nt(active[rows, :], w_out[columns, :])
        values, scale = normalise(normed[rows, :].astype(F32) + (total[rows, :] + vec_ref[5:6, :]))
        y_ref[rows, :] = (values * vec_ref[6:7, :] + vec_ref[7:8, :]).astype(BF16)
        given = cot_ref[rows, :].astype(F32)
        gain_sum += fold(given * values)
        shift_sum += fold(given)
        slope = norm_back(given * vec_ref[6:7, :], values, scale)
        total[rows, :] = slope
        low[rows, :] = slope.astype(BF16)

    vg_ref[...] = jnp.zeros_like(vg_ref)
    ones = jnp.ones((8, TOKENS), BF16)
    vg_ref[6:7, :] = jnp.sum(gain_sum, axis=0, keepdims=True)
    vg_ref[7:8, :] = jnp.sum(shift_sum, axis=0, keepdims=True)
    vg_ref[5:6, :] = dot_nn(ones, low[...])[0:1]
    low_t[...] = low[...].T

    for j in range(12):
        columns = slice(256 * j, 256 * (j + 1))
        place = slice(256 * (j % 3), 256 * (j % 3 + 1))
        grown = dot_nn(low_t[...], active[:, columns])
        d_out[j // 3, :, :, place] = grown.reshape(GROUPS, ROWS, 256).astype(BF16)
        slope = dot_nn(low[...], w_out[:, columns])
        curve[:, columns] = (slope * curve[:, columns].astype(F32)).astype(BF16)

    for part in range(4):
        columns = slice(part * D, (part + 1) * D)
        grown = dot_tn(curve[:, columns], normed[...])
        d_in[8 * part : 8 * part + 8] = grown.reshape(8, 4, ROWS, D).astype(BF16)
        vg_ref[8 + part : 9 + part, :] = dot_nn(ones, curve[:, columns])[0:1]

    def send(parts, half, row, sem):
        for part in range(2):
            target = parts[part]

            def body(i, carry):
                group = table[row + part, i]
                if half == 0:
                    pltpu.make_async_copy(
                        d_in.at[group, pl.ds(2 * part, 2)], target.at[i], sems.at[sem + part]
                    ).start()
                else:
                    for k in range(2):
                        pltpu.make_async_copy(
                            d_out.at[2 * part + k, group], target.at[i, k], sems.at[sem + part]
                        ).start()
                return carry

            lax.fori_loop(0, GROUPS, body, 0)

    @pl.when(core[0] == 0)
    def _():
        send(outs[0:2], 0, 0, 4)
        send(outs[2:4], 1, 2, 6)

    @pl.when(core[0] != 0)
    def _():
        send(outs[0:2], 1, 0, 4)
        send(outs[2:4], 0, 2, 6)

    gain_sum, shift_sum = 0.0, 0.0
    for rows in HALVES:
        for j in range(3):
            columns = slice(256 * j, 256 * (j + 1))
            total[rows, columns] += dot_nn(curve[rows, :], w_in[:, columns])
        given = total[rows, :]
        values = normal[rows, :]
        gain_sum += fold(given * values)
        shift_sum += fold(given)
        slope = norm_back(given * vec_ref[3:4, :], values, scales[rows, :])
        first_ref[rows, :] = slope
        low[rows, :] = slope.astype(BF16)
        mixed_low_ref[rows, :] = dot_nn(low[rows, :], wo[...]).astype(BF16)
    vg_ref[3:4, :] = jnp.sum(gain_sum, axis=0, keepdims=True)
    vg_ref[4:5, :] = jnp.sum(shift_sum, axis=0, keepdims=True)
    vg_ref[2:3, :] = dot_nn(ones, low[...])[0:1]
    grown = dot_tn(low[...], mixed_ref[...]).reshape(GROUPS, ROWS, D)
    og_ref[...] = jnp.concatenate([grown, jnp.zeros((GROUPS, 8, D), F32)], axis=1).astype(BF16)
    for i in range(4):
        settle(outs[i], sems.at[4 + i])


def middle(table, core, layer_input, mixed, cotangent, vectors, own_b, other_b, own, other):
    part = jax.ShapeDtypeStruct((GROUPS, 2, ROWS, D), BF16)
    return pl.pallas_call(
        middle_kernel,
        in_specs=[SMEM, SMEM, VMEM, VMEM, VMEM, VMEM] + [ANY] * 12,
        out_specs=[VMEM] * 5 + [ANY] * 4,
        out_shape=(
            jax.ShapeDtypeStruct((TOKENS, D), BF16),
            jax.ShapeDtypeStruct((TOKENS, D), F32),
            jax.ShapeDtypeStruct((TOKENS, D), BF16),
            jax.ShapeDtypeStruct((GROUPS, 32, D), BF16),
            jax.ShapeDtypeStruct((16, D), F32),
            part,
            part,
            part,
            part,
        ),
        scratch_shapes=[
            pltpu.VMEM((GROUPS, 32, D), BF16),
            pltpu.VMEM((D, D), BF16),
            pltpu.VMEM((FF, D), BF16),
            pltpu.VMEM((GROUPS, 48, D), BF16),
            pltpu.VMEM((GROUPS, 48, D), BF16),
            pltpu.VMEM((D, FF), BF16),
            pltpu.VMEM((TOKENS, FF), BF16),
            pltpu.VMEM((TOKENS, FF), BF16),
            pltpu.VMEM((TOKENS, D), BF16),
            pltpu.VMEM((TOKENS, D), F32),
            pltpu.VMEM((TOKENS, 1), F32),
            pltpu.VMEM((TOKENS, D), F32),
            pltpu.VMEM((TOKENS, D), BF16),
            pltpu.VMEM((D, TOKENS), BF16),
            pltpu.VMEM((GROUPS, 4, ROWS, D), BF16),
            pltpu.VMEM((4, GROUPS, ROWS, D), BF16),
            pltpu.SemaphoreType.DMA((8,)),
        ],
        compiler_params=pltpu.CompilerParams(vmem_limit_bytes=LIMIT),
        cost_estimate=pl.CostEstimate(flops=16 * 10**9, bytes_accessed=30 * 10**6, transcendentals=3145728),
        name="middle",
    )(table, core, layer_input, mixed, cotangent, vectors, *own_b, *other_b, *own, *other)


def pair_back(counts, q_ref, k_ref, v_ref, mixed_ref, slope_ref, probs_ref, cot_ref, out_ref):
    low_lane = lax.broadcasted_iota(jnp.int32, (TOKENS, PAIR), 1) < HEAD
    segments = unit_segments(counts)
    scale = jnp.asarray(HEAD ** (-0.5), BF16)
    slope = slope_ref[...]
    query = q_ref[...] * scale
    key = k_ref[...] * scale
    value = v_ref[...]
    product = slope.astype(F32) * mixed_ref[...].astype(F32)
    queries, keys, values = [], [], []
    for head in range(2):
        chosen = low_lane if head == 0 else ~low_lane
        masked = jnp.where(chosen, slope, jnp.zeros_like(slope))
        shared = jnp.sum(jnp.where(chosen, product, 0.0), axis=-1, keepdims=True)
        products = dot_nt(masked, value)
        for block in range(DEV_UNITS):
            rows = slice(block * UNIT, (block + 1) * UNIT)
            allowed = allowed_lanes(segments, block)
            grown = probs_ref[head, rows, :].astype(F32) * (products[rows] - shared[rows])
            grown = grown + jnp.where(allowed, cot_ref[head, rows, :].astype(F32), 0.0)
            out_ref[head, rows, :] = grown.astype(BF16)
        logits = out_ref[head]
        heads = slice(head * HEAD, (head + 1) * HEAD)
        queries.append(dot_nn(logits, key))
        keys.append(dot_tn(query[:, heads], logits))
        values.append(dot_tn(slope[:, heads], probs_ref[head]))
    return (
        jnp.where(low_lane, queries[0], queries[1]).astype(BF16),
        jnp.concatenate(keys, axis=0).astype(BF16),
        jnp.concatenate(values, axis=0).astype(BF16),
    )


def attend_back_kernel(counts, *refs):
    dq_ref, dk_ref, dv_ref = refs[8:11]
    dq_ref[...], dk_ref[...], dv_ref[...] = pair_back(counts, *refs[0:8])


FIRST = 2
EARLY = PAIR * FIRST


def attend_back(counts, queries, keys, values, mixed, mixed_low, probs, logits_cotangent):
    columns = pl.BlockSpec((TOKENS, PAIR), lambda i, *_: (0, i))
    turned = pl.BlockSpec((PAIR, TOKENS), lambda i, *_: (i, 0))
    logits = pl.BlockSpec((2, TOKENS, TOKENS), lambda i, *_: (i, 0, 0))
    return pl.pallas_call(
        attend_back_kernel,
        grid_spec=pltpu.PrefetchScalarGridSpec(
            num_scalar_prefetch=1,
            grid=(FIRST,),
            in_specs=[columns] * 5 + [logits] * 2,
            out_specs=[logits, columns, turned, turned],
        ),
        out_shape=(
            jax.ShapeDtypeStruct((H, TOKENS, TOKENS), BF16),
            jax.ShapeDtypeStruct((TOKENS, D), BF16),
            jax.ShapeDtypeStruct((D, TOKENS), BF16),
            jax.ShapeDtypeStruct((D, TOKENS), BF16),
        ),
        compiler_params=pltpu.CompilerParams(vmem_limit_bytes=LIMIT),
        cost_estimate=pl.CostEstimate(flops=2 * 10**9, bytes_accessed=7 * 10**6, transcendentals=0),
        name="attend_back_first",
    )(counts, queries, keys, values, mixed, mixed_low, probs, logits_cotangent)


def rest_kernel(table, core, counts, *refs):
    vg_ref, x_in, og_in, logits_in, dq_in, dk_in, dv_in = refs[7:14]
    out_ref, dq_ref, dk_ref, dv_ref = refs[14:18]
    outs = refs[18:22]
    x_ref, og_ref, dq_all, dk_all, dv_all, d_q, d_k, d_v = refs[22:30]
    sems, in_sems = refs[30:32]
    step = pl.program_id(0)
    ones = jnp.ones((8, TOKENS), BF16)
    brought = (
        (x_in, x_ref),
        (dq_in.at[:, pl.ds(0, EARLY)], dq_all.at[:, pl.ds(0, EARLY)]),
        (dk_in.at[pl.ds(0, EARLY)], dk_all.at[pl.ds(0, EARLY)]),
        (dv_in.at[pl.ds(0, EARLY)], dv_all.at[pl.ds(0, EARLY)]),
        (og_in, og_ref),
    )

    @pl.when(step == 0)
    def _():
        for i, (source, target) in enumerate(brought):
            pltpu.make_async_copy(source, target, in_sems.at[i]).start()

    dq, dk, dv = pair_back(counts, *refs[0:7], out_ref)
    dq_ref[...] = dq
    dk_ref[...] = dk
    dv_ref[...] = dv

    rows = pl.ds(pl.multiple_of((step + FIRST) * PAIR, PAIR), PAIR)
    dq_all[:, rows] = dq
    dk_all[rows, :] = dk
    dv_all[rows, :] = dv

    def send(source, half, part):
        def copies(outs_of, row, sem):
            def body(i, carry):
                pltpu.make_async_copy(
                    source.at[table[row + part, i]], outs_of[part].at[i], sems.at[sem + part]
                ).start()
                return carry

            lax.fori_loop(0, GROUPS, body, 0)

        pl.when(core[0] == half)(lambda: copies(outs[0:2], 0, 0))
        pl.when(core[0] != half)(lambda: copies(outs[2:4], 2, 2))

    @pl.when(step == pl.num_programs(0) - 1)
    def _():
        for i, (source, target) in enumerate(brought):
            pltpu.make_async_copy(source, target, in_sems.at[i]).wait()
        send(og_ref, 1, 1)
        x = x_ref[...]
        d_q[...] = dot_tn(dq_all[...], x).reshape(GROUPS, ROWS, D).astype(BF16)
        send(d_q, 0, 0)
        d_v[...] = dot_nn(dv_all[...], x).reshape(GROUPS, ROWS, D).astype(BF16)
        send(d_v, 1, 0)
        query_sum = dot_nn(ones, dq_all[...])
        value_sum = dot_nt(ones, dv_all[...])
        rows8 = lax.broadcasted_iota(jnp.int32, (8, D), 0)
        offsets = vg_ref[0:8, :]
        offsets = jnp.where(
            rows8 == 0, query_sum[0:1, :], jnp.where(rows8 == 1, value_sum[0:1, :], offsets)
        )
        group = lax.broadcasted_iota(jnp.int32, (32, 8, D), 0)
        lane = lax.broadcasted_iota(jnp.int32, (32, 8, D), 2)
        chosen = jnp.where(lane // ROWS == group, offsets[None], 0.0)
        row = lax.broadcasted_iota(jnp.int32, (D, 128), 0)
        column = lax.broadcasted_iota(jnp.int32, (D, 128), 1)
        narrow = dot_nn(chosen.reshape(256, D).astype(BF16), (row % ROWS == column).astype(BF16))
        wide = jnp.broadcast_to(vg_ref[8:12, :][:, None, :], (4, 8, D))
        second = lax.broadcasted_iota(jnp.int32, (4, 8, D), 1)
        lane = lax.broadcasted_iota(jnp.int32, (4, 8, D), 2)
        chosen = jnp.where(lane // 96 == second, wide, 0.0).reshape(32, D)
        inner = dot_nn(chosen.astype(BF16), (row % 96 == column).astype(BF16))
        place = lax.broadcasted_iota(jnp.int32, (32, 8, 128), 1)
        inner = jnp.where(place == 0, inner[:, None, :], 0.0)
        small = jnp.concatenate(
            [narrow.reshape(32, 8, 128), inner, jnp.zeros((32, 8, D - 256), F32)], axis=2
        )
        d_k[...] = jnp.concatenate(
            [dot_nn(dk_all[...], x).reshape(GROUPS, ROWS, D), small], axis=1
        ).astype(BF16)
        send(d_k, 0, 1)
        for i in range(4):
            settle(outs[i], sems.at[i])


def rest(table, core, counts, queries, keys, values, mixed, mixed_low, probs, logits_cotangent, layer_input, held, og, vg):
    columns = pl.BlockSpec((TOKENS, PAIR), lambda i, *_: (0, i + FIRST))
    turned = pl.BlockSpec((PAIR, TOKENS), lambda i, *_: (i + FIRST, 0))
    logits = pl.BlockSpec((2, TOKENS, TOKENS), lambda i, *_: (i + FIRST, 0, 0))
    part_a = jax.ShapeDtypeStruct((GROUPS, ROWS, D), BF16)
    part_b = jax.ShapeDtypeStruct((GROUPS, 32, D), BF16)
    return pl.pallas_call(
        rest_kernel,
        grid_spec=pltpu.PrefetchScalarGridSpec(
            num_scalar_prefetch=3,
            grid=(H // 2 - FIRST,),
            in_specs=[columns] * 5
            + [logits] * 2
            + [pl.BlockSpec((16, D), lambda i, *_: (0, 0))]
            + [ANY] * 6,
            out_specs=[logits, columns, turned, turned] + [ANY] * 4,
            scratch_shapes=[
                pltpu.VMEM((TOKENS, D), BF16),
                pltpu.VMEM((GROUPS, 32, D), BF16),
                pltpu.VMEM((TOKENS, D), BF16),
                pltpu.VMEM((D, TOKENS), BF16),
                pltpu.VMEM((D, TOKENS), BF16),
                pltpu.VMEM((GROUPS, ROWS, D), BF16),
                pltpu.VMEM((GROUPS, 32, D), BF16),
                pltpu.VMEM((GROUPS, ROWS, D), BF16),
                pltpu.SemaphoreType.DMA((4,)),
                pltpu.SemaphoreType.DMA((5,)),
            ],
        ),
        out_shape=(
            jax.ShapeDtypeStruct((H, TOKENS, TOKENS), BF16),
            jax.ShapeDtypeStruct((TOKENS, D), BF16),
            jax.ShapeDtypeStruct((D, TOKENS), BF16),
            jax.ShapeDtypeStruct((D, TOKENS), BF16),
            part_a,
            part_b,
            part_a,
            part_b,
        ),
        input_output_aliases={13 + i: i for i in range(4)},
        compiler_params=pltpu.CompilerParams(vmem_limit_bytes=LIMIT),
        cost_estimate=pl.CostEstimate(flops=6 * 10**9, bytes_accessed=25 * 10**6, transcendentals=0),
        name="attend_back_rest",
    )(
        table,
        core,
        counts,
        queries,
        keys,
        values,
        mixed,
        mixed_low,
        probs,
        logits_cotangent,
        vg,
        layer_input,
        og,
        *held,
    )


def pack_kernel(core, *refs):
    query, key, value, output, inner, outer = refs[0:6]
    small = refs[6:15]
    mine_ref, other_ref, first, second = refs[15:19]
    first[...] = jnp.zeros_like(first)
    second[...] = jnp.zeros_like(second)
    first[0:6, :] = query[...].astype(F32)
    first[6:12, :] = key[...].astype(F32)
    first[12:36, :] = inner[...].astype(F32)
    for i, ref in enumerate(small):
        row, lane = 36 + i // 6, 128 * (i % 6)
        first[row : row + 1, lane : lane + ref.shape[1]] = ref[...].astype(F32)
    second[0:6, :] = value[...].astype(F32)
    second[6:12, :] = output[...].astype(F32)
    for i in range(4):
        second[12 + 6 * i : 18 + 6 * i, :] = outer[:, D * i : D * (i + 1)].astype(F32)

    @pl.when(core[0] == 0)
    def _():
        mine_ref[...] = first[...].astype(BF16)
        other_ref[...] = second[...].astype(BF16)

    @pl.when(core[0] != 0)
    def _():
        mine_ref[...] = second[...].astype(BF16)
        other_ref[...] = first[...].astype(BF16)


def pack(core, kernels, small):
    half = jax.ShapeDtypeStruct((40, D), BF16)
    return pl.pallas_call(
        pack_kernel,
        in_specs=[SMEM] + [VMEM] * 15,
        out_specs=[VMEM] * 2,
        out_shape=(half, half),
        scratch_shapes=[pltpu.VMEM((40, D), F32)] * 2,
        name="pack",
    )(core, *(kernel.T for kernel in kernels), *(v.reshape(1, -1) for v in small))


def finish_kernel(place, ff_own, ff_other, tail_own, tail_other, query, key, value, output, inner, outer, *small):
    def write(mine, ff_first, ff_second, tail_first, tail_second):
        rows = slice(6 * mine, 6 * mine + 6)
        for ref, part, skip in (
            (query, tail_first, 0),
            (key, tail_first, 24),
            (value, tail_second, 0),
            (output, tail_second, 24),
        ):
            ref[...] = part[skip + rows.start : skip + rows.stop, :]
        inner[...] = ff_first[24 * mine : 24 * mine + 24, :]
        for i in range(4):
            outer[:, D * i : D * (i + 1)] = ff_second[24 * i + rows.start : 24 * i + rows.stop, :]
        for i in range(8):
            small[i][...] = tail_first[48 + i : 49 + i, rows]
        small[8][...] = tail_first[48:49, 128 + 24 * mine : 152 + 24 * mine]

    for mine in range(4):

        @pl.when(place[0] == mine)
        def _():
            if mine < 2:
                write(mine, ff_own, ff_other, tail_own, tail_other)
            else:
                write(mine, ff_other, ff_own, tail_other, tail_own)


def finish(mine, ff_own, ff_other, tail_own, tail_other):
    narrow = jax.ShapeDtypeStruct((6, D), F32)
    outs = pl.pallas_call(
        finish_kernel,
        in_specs=[SMEM] + [VMEM] * 4,
        out_specs=[VMEM] * 15,
        out_shape=(
            narrow,
            narrow,
            narrow,
            narrow,
            jax.ShapeDtypeStruct((24, D), F32),
            jax.ShapeDtypeStruct((6, FF), F32),
        )
        + (jax.ShapeDtypeStruct((1, 6), F32),) * 8
        + (jax.ShapeDtypeStruct((1, 24), F32),),
        name="finish",
    )(mine.astype(jnp.int32).reshape(1), ff_own, ff_other, tail_own, tail_other)
    return tuple(out.T for out in outs[:6]) + tuple(out.reshape(-1) for out in outs[6:])


def gather_weights(core_table, kernels, vectors, inner_offset):
    core, low_x = lax.axis_index("c"), lax.axis_index("xl")
    mine = core * 2 + low_x
    own, other = pack(core_table, kernels, (*vectors, inner_offset))
    pieces = jnp.stack(
        [
            own,
            swap(own, "xl"),
            swap(other, "c"),
            lax.ppermute(other, ("c", "xl"), [(i, 3 - i) for i in range(4)]),
        ]
    )
    natural = jnp.concatenate(
        [lax.dynamic_slice_in_dim(pieces, mine ^ i, 1, axis=0) for i in range(4)], axis=0
    )
    first = core == 0
    near_a = natural[:, 0:6].reshape(ROWS, D)
    near_b = natural[:, 6:12].reshape(ROWS, D)
    inner = natural[:, 12:36].reshape(96, D)
    outer = natural[:, 12:36].reshape(4, 4, 6, D).transpose(1, 0, 2, 3).reshape(96, D)
    offsets = natural[:, 36:38].reshape(4, 12, 128)[:, 0:8, 0:6].transpose(1, 0, 2).reshape(8, ROWS)
    offsets = jnp.pad(offsets, ((0, 0), (0, 128 - ROWS)))
    wide_offset = jnp.pad(natural[:, 37, 256:280].reshape(1, 96), ((0, 7), (0, 32)))
    small = jnp.concatenate([offsets, wide_offset, jnp.zeros((8, D - 256), BF16)], axis=1)
    wide = jnp.where(first, inner, outer)
    block = jnp.concatenate([near_a, wide[0:48], near_b, small, wide[48:96]], axis=0)
    both = jnp.stack([block, exchange(block, STEPS_A[0])])
    part_a, part_b = both[:, 0:72], both[:, 72:152]
    for i in (1, 2):
        arrived_a, arrived_b = after((exchange(part_a, STEPS_A[i]), exchange(part_b, STEPS_B[i])))
        part_a = jnp.concatenate([part_a, arrived_a], axis=0)
        part_b = jnp.concatenate([part_b, arrived_b], axis=0)
    arrived_a, arrived_b = after((exchange(part_a, STEPS_A[3]), exchange(part_b, STEPS_B[3])))
    near_a = jnp.concatenate([part_a[:, 0:24], arrived_a[:, 0:24]], axis=0)
    near_b = jnp.concatenate([part_b[:, 0:32], arrived_b[:, 0:32]], axis=0)
    far_a = jnp.concatenate([part_a[:, 24:72], arrived_a[:, 24:72]], axis=0)
    far_b = jnp.concatenate([part_b[:, 32:80], arrived_b[:, 32:80]], axis=0)
    last_a, last_b = exchange(near_a, STEPS_A[4]), exchange(near_b, STEPS_B[4])
    far_a, far_b, last_a, last_b = after((far_a, far_b, last_a, last_b))
    near = (near_a, last_a, near_b, last_b)
    return near, tuple(swap(part, "c") for part in near), (far_a, far_b)


def after(values, *others):
    return lax.optimization_barrier((values, others))[0] if others else lax.optimization_barrier(values)


def add(first, second):
    return (first.astype(F32) + second.astype(F32)).astype(BF16)


def add3(first, second, third):
    return (first.astype(F32) + second.astype(F32) + third.astype(F32)).astype(BF16)


def add_kernel(first_a, second_a, first_b, second_b, sum_a, sum_b):
    sum_a[...] = (first_a[...].astype(F32) + second_a[...].astype(F32)).astype(BF16)
    sum_b[...] = (first_b[...].astype(F32) + second_b[...].astype(F32)).astype(BF16)


def add_later(*arrays):
    block = (4, 2, ROWS, D)
    part = jax.ShapeDtypeStruct((16, 2, ROWS, D), BF16)
    return pl.pallas_call(
        add_kernel,
        grid=(4,),
        in_specs=[pl.BlockSpec(block, lambda i: (i + 4, 0, 0, 0))] * 4,
        out_specs=[pl.BlockSpec(block, lambda i: (i, 0, 0, 0))] * 2,
        out_shape=(part, part),
        cost_estimate=pl.CostEstimate(flops=10**6, bytes_accessed=7 * 10**6, transcendentals=0),
        name="add_later",
    )(*arrays)


def split(*arrays):
    half = arrays[0].shape[0] // 2
    combine = add if len(arrays) == 2 else add3
    return combine(*(a[:half] for a in arrays)), combine(*(a[half:] for a in arrays))


def halve(total, step):
    return split(total[0], exchange(total[1], step))


def reduce_end(total_a, total_b):
    kept, sent = (
        jnp.concatenate([total_a[i].reshape(-1, D), total_b[i].reshape(-1, D)], axis=0) for i in range(2)
    )
    total = add(kept, exchange(sent, STEPS_A[0]))
    own = total.astype(F32) + swap(total, "xl").astype(F32)
    return own, swap(own, "c")


def body(
    layer_input,
    prior_logits,
    bucket_counts,
    output_cotangent,
    logits_cotangent,
    query_kernel,
    query_offset,
    key_kernel,
    value_kernel,
    value_offset,
    output_kernel,
    output_offset,
    first_gain,
    first_shift,
    inner_kernel,
    inner_offset,
    outer_kernel,
    outer_offset,
    second_gain,
    second_shift,
):
    core, low_x = lax.axis_index("c"), lax.axis_index("xl")
    mine = core * 2 + low_x
    table = jnp.stack(
        [
            position_groups(STEPS_A, core),
            position_groups(STEPS_B, core),
            position_groups(STEPS_A, 1 - core),
            position_groups(STEPS_B, 1 - core),
        ]
    )
    core_table = core.astype(jnp.int32).reshape(1)
    near, near_other, far = gather_weights(
        core_table,
        (query_kernel, key_kernel, value_kernel, output_kernel, inner_kernel, outer_kernel),
        (
            query_offset,
            value_offset,
            output_offset,
            first_gain,
            first_shift,
            outer_offset,
            second_gain,
            second_shift,
        ),
        inner_offset,
    )
    far_last = (exchange(far[0], STEPS_A[4]), exchange(far[1], STEPS_B[4]))
    far_other = [swap(far[0], "c"), None, swap(far[1], "c"), None]
    queries, keys, values, query_matrix, key_matrix, value_matrix, vectors = project(
        table, core_table, layer_input, near, near_other
    )
    raw_logits, probs, mixed = attend(bucket_counts, queries, keys, values, prior_logits, 0, 6, ())
    far_last, mixed = after((far_last, mixed))
    far_other[1], far_other[3] = swap(far_last[0], "c"), swap(far_last[1], "c")
    layer_output, first_slope, mixed_low, output_slope, vector_slopes, *ff = middle(
        table,
        core_table,
        layer_input,
        mixed,
        output_cotangent,
        vectors,
        near[2:4],
        near_other[2:4],
        (far[0], far_last[0], far[1], far_last[1]),
        far_other,
    )

    moved = [swap(ff[2], "c"), swap(ff[3], "c")]
    heads = (queries, keys, values, mixed, mixed_low, probs, logits_cotangent)
    held = attend_back(bucket_counts, *heads)
    moved, held = after((moved, held))
    half = GROUPS // 2
    sent_a, sent_b = add_later(ff[0], moved[0], ff[1], moved[1])
    held, sent_a, sent_b = after((held, sent_a, sent_b))
    logits_slope, dq, dk, dv, *tail = rest(
        table, core_table, bucket_counts, *heads, layer_input, held, output_slope, vector_slopes
    )
    arrived_a, arrived_b = exchange(sent_a, STEPS_A[4]), exchange(sent_b, STEPS_B[4])
    arrived_a, arrived_b, tail = after((arrived_a, arrived_b, tuple(tail)))
    tail_moved = [swap(tail[2], "c"), swap(tail[3], "c")]
    tail_sent = [add(tail[i][half:], tail_moved[i][half:]) for i in range(2)]
    arrived_a, arrived_b, tail_sent = after((arrived_a, arrived_b, tail_sent))
    ff_a = split(ff[0][:half], moved[0][:half], arrived_a)
    ff_b = split(ff[1][:half], moved[1][:half], arrived_b)
    input_slope = (
        first_slope + dot_nn(dq, query_matrix) + dot_tn(dk, key_matrix) + dot_tn(dv, value_matrix)
    ).astype(BF16)
    tail_arrived = after(
        (exchange(tail_sent[0], STEPS_A[4]), exchange(tail_sent[1], STEPS_B[4])), input_slope
    )
    tail_a = split(tail[0][:half], tail_moved[0][:half], tail_arrived[0])
    tail_b = split(tail[1][:half], tail_moved[1][:half], tail_arrived[1])
    for i in (3, 2, 1):
        arrived_a, arrived_b = after((exchange(tail_a[1], STEPS_A[i]), exchange(tail_b[1], STEPS_B[i])))
        tail_a, tail_b = split(tail_a[0], arrived_a), split(tail_b[0], arrived_b)
        ff_a, ff_b = halve(ff_a, STEPS_A[i]), halve(ff_b, STEPS_B[i])
    ff_sums = reduce_end(ff_a, ff_b)
    tail_sums = reduce_end(tail_a, tail_b)
    query_owned, key_owned, value_owned, output_owned, inner_owned, outer_owned, *small = finish(
        mine, *ff_sums, *tail_sums
    )

    return (
        layer_output,
        raw_logits,
        input_slope,
        logits_slope,
        query_owned,
        small[0],
        key_owned,
        value_owned,
        small[1],
        output_owned,
        small[2],
        small[3],
        small[4],
        inner_owned,
        small[8],
        outer_owned,
        small[5],
        small[6],
        small[7],
    )


def solution(mesh):
    fine = Mesh(mesh.devices.reshape(SIZES), AXES)
    rows = P(AXES, None)
    logits = P(None, AXES, None)
    columns = P(None, AXES)
    vector = P(AXES)
    return jax.shard_map(
        body,
        mesh=fine,
        in_specs=(
            rows,
            logits,
            rows,
            rows,
            logits,
            columns,
            vector,
            columns,
            columns,
            vector,
            columns,
            vector,
            vector,
            vector,
            columns,
            vector,
            columns,
            vector,
            vector,
            vector,
        ),
        out_specs=(
            rows,
            logits,
            rows,
            logits,
            columns,
            vector,
            columns,
            columns,
            vector,
            columns,
            vector,
            vector,
            vector,
            columns,
            vector,
            columns,
            vector,
            vector,
            vector,
        ),
        check_vma=False,
    )
```

```python
import jax
import jax.numpy as jnp
from jax import lax
from jax.experimental import pallas as pl
from jax.experimental.pallas import tpu as pltpu
from jax.sharding import Mesh
from jax.sharding import PartitionSpec as P

D = 768
H = 12
HEAD = 64
FF = 3072
UNIT = 128
DEV_UNITS = 4
EPSILON = 1e-12

AXES = ("xh", "z", "y", "c", "xl")
SIZES = (2, 4, 4, 2, 2)
GROUPS = 32
ROWS = 24
MASKS = ((1, 3), (3, 1))
STEPS_A = (("x", 0), ("z", 0), ("z", 1), ("y", 0), ("y", 1))
STEPS_B = (("x", 0), ("y", 0), ("y", 1), ("z", 0), ("z", 1))
BF16 = jnp.bfloat16
F32 = jnp.float32


def exchange(values, step):
    axis, turn = step
    if axis == "x":
        return lax.ppermute(values, ("xh", "xl"), [(i, 3 - i) for i in range(4)])
    pairs = []
    for i in range(4):
        for core in range(2):
            pairs.append((i * 2 + core, (i ^ MASKS[core][turn]) * 2 + core))
    return lax.ppermute(values, (axis, "c"), pairs)


def swap(values, axis):
    return lax.ppermute(values, axis, [(0, 1), (1, 0)])


def position_groups(steps, core):
    position = jnp.arange(GROUPS, dtype=jnp.int32)
    place = {
        "x": jnp.full((GROUPS,), lax.axis_index("xh"), jnp.int32),
        "y": jnp.full((GROUPS,), lax.axis_index("y"), jnp.int32),
        "z": jnp.full((GROUPS,), lax.axis_index("z"), jnp.int32),
    }
    for bit, (axis, turn) in enumerate(steps):
        if axis == "x":
            mask = 1
        else:
            mask = jnp.where(core == 0, MASKS[0][turn], MASKS[1][turn])
        place[axis] = place[axis] ^ (((position >> bit) & 1) * mask)
    return (place["x"] * 4 + place["z"]) * 4 + place["y"]


ANY = pl.BlockSpec(memory_space=pl.ANY)
VMEM = pl.BlockSpec(memory_space=pltpu.VMEM)
SMEM = pl.BlockSpec(memory_space=pltpu.SMEM)
TOKENS = 512
PAIR = 2 * HEAD
LIMIT = 58 * 1024 * 1024


def dot_nt(rows, matrix):
    return lax.dot_general(rows, matrix, (((1,), (1,)), ((), ())), preferred_element_type=F32)


def dot_nn(rows, matrix):
    return lax.dot_general(rows, matrix, (((1,), (0,)), ((), ())), preferred_element_type=F32)


def dot_tn(rows, matrix):
    return lax.dot_general(rows, matrix, (((0,), (0,)), ((), ())), preferred_element_type=F32)


def fetch(table, core, own, other, targets, sems):
    def place(parts, half, row):
        for part in range(2):
            if (half, part) not in targets:
                continue
            where, sem = targets[half, part]
            for second in range(2):
                source = parts[2 * part + second]

                def body(i, carry):
                    group = table[row + part, i + 16 * second]
                    pltpu.make_async_copy(source.at[i], where(group), sems.at[sem]).start()
                    return carry

                lax.fori_loop(0, 16, body, 0)

    @pl.when(core[0] == 0)
    def _():
        place(own, 0, 0)
        place(other, 1, 2)

    @pl.when(core[0] != 0)
    def _():
        place(own, 1, 0)
        place(other, 0, 2)


def settle(ref, sem):
    pltpu.make_async_copy(ref, ref, sem).wait()


def straighten(raw, skip, store):
    for i in range(4):
        block = raw[8 * i : 8 * i + 8].astype(F32)[:, skip : skip + ROWS]
        store(i, block.reshape(8 * ROWS, D).astype(BF16))


def project_kernel(table, core, x_ref, *refs):
    own, other = refs[0:4], refs[4:8]
    q_ref, k_ref, v_ref, wq_ref, wk_ref, wv_ref, vec_ref = refs[8:15]
    raw_q, raw_k, raw_v, sems = refs[15:19]
    targets = {
        (0, 0): (lambda g: raw_q.at[g], 0),
        (0, 1): (lambda g: raw_k.at[g], 1),
        (1, 0): (lambda g: raw_v.at[g], 2),
    }
    fetch(table, core, own, other, targets, sems)

    def keep(ref):
        def store(i, rows):
            ref[192 * i : 192 * (i + 1), :] = rows

        return store

    settle(raw_k, sems.at[1])
    small = raw_k[...].astype(F32)[:, ROWS : ROWS + 8, 0:256]
    row = lax.broadcasted_iota(jnp.int32, (128, D), 0)
    lane = lax.broadcasted_iota(jnp.int32, (128, D), 1)
    spread = (lane % ROWS == row).astype(BF16)
    wide = dot_nn(small[:, :, 0:128].reshape(256, 128).astype(BF16), spread).reshape(32, 8, D)
    group = lax.broadcasted_iota(jnp.int32, (32, 8, D), 0)
    lane3 = lax.broadcasted_iota(jnp.int32, (32, 8, D), 2)
    vec_ref[0:8, :] = jnp.sum(jnp.where(lane3 // ROWS == group, wide, 0.0), axis=0)
    spread = ((lane % 96 == row) & (row < 96)).astype(BF16)
    wide = dot_nn(small[:, :, 128:256].reshape(256, 128).astype(BF16), spread).reshape(4, 8, 8, D)
    second = lax.broadcasted_iota(jnp.int32, (4, 8, 8, D), 1)
    place = lax.broadcasted_iota(jnp.int32, (4, 8, 8, D), 2)
    lane4 = lax.broadcasted_iota(jnp.int32, (4, 8, 8, D), 3)
    chosen = jnp.where((lane4 // 96 == second) & (place == 0), wide, 0.0)
    inner_rows = jnp.sum(chosen, axis=1)
    for i in range(4):
        vec_ref[8 + i : 9 + i, :] = inner_rows[i, 0:1, :]
    vec_ref[12:16, :] = jnp.zeros((4, D), F32)

    x = x_ref[...]
    straighten(raw_k, 0, keep(wk_ref))
    k_ref[...] = dot_nt(x, wk_ref[...]).astype(BF16)
    settle(raw_q, sems.at[0])
    straighten(raw_q, 0, keep(wq_ref))
    q_ref[...] = (dot_nt(x, wq_ref[...]) + vec_ref[0:1, :]).astype(BF16)
    settle(raw_v, sems.at[2])
    straighten(raw_v, 0, keep(wv_ref))
    v_ref[...] = (dot_nt(x, wv_ref[...]) + vec_ref[1:2, :]).astype(BF16)


def project(table, core, layer_input, own, other):
    rows = jax.ShapeDtypeStruct((TOKENS, D), BF16)
    square = jax.ShapeDtypeStruct((D, D), BF16)
    return pl.pallas_call(
        project_kernel,
        in_specs=[SMEM, SMEM, VMEM] + [ANY] * 8,
        out_specs=[VMEM] * 7,
        out_shape=(rows, rows, rows, square, square, square, jax.ShapeDtypeStruct((16, D), F32)),
        scratch_shapes=[
            pltpu.VMEM((GROUPS, ROWS, D), BF16),
            pltpu.VMEM((GROUPS, 32, D), BF16),
            pltpu.VMEM((GROUPS, ROWS, D), BF16),
            pltpu.SemaphoreType.DMA((3,)),
        ],
        compiler_params=pltpu.CompilerParams(vmem_limit_bytes=LIMIT),
        cost_estimate=pl.CostEstimate(flops=2 * 10**9, bytes_accessed=12 * 10**6, transcendentals=0),
        name="project",
    )(table, core, layer_input, *own, *other)


def attend_kernel(counts, q_ref, k_ref, v_ref, prior_ref, *refs):
    raw_ref, probs_ref, mixed_ref = refs[-3:]
    query = q_ref[...] * jnp.asarray(HEAD ** (-0.5), BF16)
    key = k_ref[...]
    value = v_ref[...]
    low_lane = lax.broadcasted_iota(jnp.int32, (TOKENS, PAIR), 1) < HEAD
    segments = unit_segments(counts)
    results = []
    for head in range(2):
        chosen = low_lane if head == 0 else ~low_lane
        masked = jnp.where(chosen, query, jnp.zeros_like(query))
        products = dot_nt(masked, key)
        for block in range(DEV_UNITS):
            rows = slice(block * UNIT, (block + 1) * UNIT)
            allowed = allowed_lanes(segments, block)
            scores = products[rows] + prior_ref[head, rows, :].astype(F32)
            raw_ref[head, rows, :] = jnp.where(allowed, scores, 0.0).astype(BF16)
            scores = jnp.where(allowed, scores, -1e30)
            grown = jnp.exp(scores - jnp.max(scores, axis=-1, keepdims=True))
            total = jnp.sum(grown, axis=-1, keepdims=True)
            probs_ref[head, rows, :] = (grown * (1.0 / total)).astype(BF16)
        results.append(dot_nn(probs_ref[head], value))
    mixed_ref[...] = jnp.where(low_lane, results[0], results[1]).astype(BF16)


def attend(counts, queries, keys, values, prior_logits, first, last, held):
    columns = pl.BlockSpec((TOKENS, PAIR), lambda i, *_: (0, i + first))
    logits = pl.BlockSpec((2, TOKENS, TOKENS), lambda i, *_: (i + first, 0, 0))
    logits_shape = jax.ShapeDtypeStruct((H, TOKENS, TOKENS), BF16)
    pairs = last - first
    return pl.pallas_call(
        attend_kernel,
        grid_spec=pltpu.PrefetchScalarGridSpec(
            num_scalar_prefetch=1,
            grid=(pairs,),
            in_specs=[columns] * 3 + [logits] + [ANY] * len(held),
            out_specs=[logits, logits, columns],
        ),
        out_shape=(logits_shape, logits_shape, jax.ShapeDtypeStruct((TOKENS, D), BF16)),
        input_output_aliases={5 + i: i for i in range(len(held))},
        compiler_params=pltpu.CompilerParams(vmem_limit_bytes=LIMIT),
        cost_estimate=pl.CostEstimate(
            flops=pairs * 10**9, bytes_accessed=pairs * 5 * 10**6, transcendentals=pairs * 2**19
        ),
        name="attend_%d" % first,
    )(counts, queries, keys, values, prior_logits, *held)


def unit_segments(counts):
    start = [counts[0, 0], counts[0, 0] + 2 * counts[0, 1]]
    start.append(start[1] + 3 * counts[0, 2])
    segments = []
    current = jnp.int32(-1)
    for unit in range(DEV_UNITS):
        first = unit < start[0]
        second = (unit >= start[0]) & (unit < start[1]) & ((unit - start[0]) % 2 == 0)
        third = (unit >= start[1]) & (unit < start[2]) & ((unit - start[1]) % 3 == 0)
        fourth = (unit >= start[2]) & ((unit - start[2]) % 4 == 0)
        current = current + jnp.where(first | second | third | fourth, 1, 0)
        segments.append(current)
    return segments


def allowed_lanes(segments, block):
    unit = lax.broadcasted_iota(jnp.int32, (1, TOKENS), 1) // UNIT
    same = jnp.zeros((1, TOKENS), jnp.int32)
    for other in range(DEV_UNITS):
        same = jnp.where(unit == other, jnp.where(segments[other] == segments[block], 1, 0), same)
    return same > 0


def mean_of(values):
    return jnp.sum(values, axis=-1, keepdims=True) * (1.0 / D)


def normalise(values):
    centred = values - mean_of(values)
    scale = lax.rsqrt(mean_of(centred * centred) + EPSILON)
    return centred * scale, scale


def norm_back(slope, normal, scale):
    return scale * (slope - mean_of(slope) - normal * mean_of(slope * normal))


def fold(values):
    return jnp.sum(values.reshape(values.shape[0] // 8, 8, D), axis=0)


HALVES = (slice(0, 256), slice(256, 512))


def middle_kernel(table, core, x_ref, mixed_ref, cot_ref, vec_ref, *refs):
    own_b, other_b = refs[0:2], refs[2:4]
    own, other = refs[4:8], refs[8:12]
    y_ref, first_ref, mixed_low_ref, og_ref, vg_ref = refs[12:17]
    outs = refs[17:23]
    (
        raw_o,
        wo,
        w_in,
        raw_a,
        raw_b,
        w_out,
        active,
        curve,
        normed,
        normal,
        scales,
        total,
        low,
        low_t,
        d_in,
        d_out,
        sems,
    ) = refs[23:40]

    fetch(table, core, (None, None) + own_b, (None, None) + other_b, {(1, 1): (lambda g: raw_o.at[g], 0)}, sems)

    def inner_place(skip):
        return lambda g: w_in.at[pl.ds(pl.multiple_of(g * 96 + skip, 48), 48)]

    targets = {
        (0, 0): (inner_place(0), 1),
        (0, 1): (inner_place(48), 1),
        (1, 0): (lambda g: raw_a.at[g], 2),
        (1, 1): (lambda g: raw_b.at[g], 3),
    }
    fetch(table, core, own, other, targets, sems)

    def keep_wo(i, rows):
        wo[192 * i : 192 * (i + 1), :] = rows

    settle(raw_o, sems.at[0])
    straighten(raw_o, 0, keep_wo)
    for rows in HALVES:
        attended = dot_nt(mixed_ref[rows, :], wo[...]) + vec_ref[2:3, :]
        values, scale = normalise(x_ref[rows, :].astype(F32) + attended)
        normal[rows, :] = values
        scales[rows, :] = scale
        normed[rows, :] = (values * vec_ref[3:4, :] + vec_ref[4:5, :]).astype(BF16)

    def keep_out(part):
        def store(i, rows):
            w_out[192 * i : 192 * (i + 1), part * D : (part + 1) * D] = rows

        return store

    settle(w_in, sems.at[1])
    for j in range(12):
        columns = slice(256 * j, 256 * (j + 1))
        place = slice(256 * (j % 3), 256 * (j % 3 + 1))
        inner = dot_nt(normed[...], w_in[columns, :]) + vec_ref[8 + j // 3 : 9 + j // 3, place]
        bell = 0.5 * (1.0 + lax.erf(inner * (0.5**0.5)))
        active[:, columns] = (inner * bell).astype(BF16)
        slope = bell + inner * jnp.exp(inner * inner * -0.5) * 0.3989422804014327
        curve[:, columns] = slope.astype(BF16)
        if j == 3:
            settle(raw_a, sems.at[2])
            settle(raw_b, sems.at[3])
        if j in (4, 6, 8, 10):
            part = (j - 4) // 2
            straighten(raw_a if part < 2 else raw_b, ROWS * (part % 2), keep_out(part))

    gain_sum, shift_sum = 0.0, 0.0
    for rows in HALVES:
        for j in range(3):
            columns = slice(256 * j, 256 * (j + 1))
            total[rows, columns] = dot_nt(active[rows, :], w_out[columns, :])
        values, scale = normalise(normed[rows, :].astype(F32) + (total[rows, :] + vec_ref[5:6, :]))
        y_ref[rows, :] = (values * vec_ref[6:7, :] + vec_ref[7:8, :]).astype(BF16)
        given = cot_ref[rows, :].astype(F32)
        gain_sum += fold(given * values)
        shift_sum += fold(given)
        slope = norm_back(given * vec_ref[6:7, :], values, scale)
        total[rows, :] = slope
        low[rows, :] = slope.astype(BF16)

    vg_ref[...] = jnp.zeros_like(vg_ref)
    ones = jnp.ones((8, TOKENS), BF16)
    vg_ref[6:7, :] = jnp.sum(gain_sum, axis=0, keepdims=True)
    vg_ref[7:8, :] = jnp.sum(shift_sum, axis=0, keepdims=True)
    vg_ref[5:6, :] = dot_nn(ones, low[...])[0:1]
    low_t[...] = low[...].T

    for j in range(12):
        columns = slice(256 * j, 256 * (j + 1))
        place = slice(256 * (j % 3), 256 * (j % 3 + 1))
        grown = dot_nn(low_t[...], active[:, columns])
        d_out[j // 3, :, :, place] = grown.reshape(GROUPS, ROWS, 256).astype(BF16)
        slope = dot_nn(low[...], w_out[:, columns])
        curve[:, columns] = (slope * curve[:, columns].astype(F32)).astype(BF16)

    for part in range(4):
        columns = slice(part * D, (part + 1) * D)
        grown = dot_tn(curve[:, columns], normed[...])
        d_in[8 * part : 8 * part + 8] = grown.reshape(8, 4, ROWS, D).astype(BF16)
        vg_ref[8 + part : 9 + part, :] = dot_nn(ones, curve[:, columns])[0:1]

    def send(own, half, row):
        for place in (2, 3, 0, 1):
            second, part = place // 2, place % 2
            target = outs[place] if own else outs[4 + second].at[part]
            sem = sems.at[4 + place] if own else sems.at[8 + second]

            def body(i, carry):
                group = table[row + part, i + 16 * second]
                if half == 0:
                    pltpu.make_async_copy(d_in.at[group, pl.ds(2 * part, 2)], target.at[i], sem).start()
                else:
                    for k in range(2):
                        pltpu.make_async_copy(d_out.at[2 * part + k, group], target.at[i, k], sem).start()
                return carry

            lax.fori_loop(0, GROUPS // 2, body, 0)

    @pl.when(core[0] == 0)
    def _():
        send(False, 1, 2)
        send(True, 0, 0)

    @pl.when(core[0] != 0)
    def _():
        send(False, 0, 2)
        send(True, 1, 0)

    gain_sum, shift_sum = 0.0, 0.0
    for rows in HALVES:
        for j in range(3):
            columns = slice(256 * j, 256 * (j + 1))
            total[rows, columns] += dot_nn(curve[rows, :], w_in[:, columns])
        given = total[rows, :]
        values = normal[rows, :]
        gain_sum += fold(given * values)
        shift_sum += fold(given)
        slope = norm_back(given * vec_ref[3:4, :], values, scales[rows, :])
        first_ref[rows, :] = slope
        low[rows, :] = slope.astype(BF16)
        mixed_low_ref[rows, :] = dot_nn(low[rows, :], wo[...]).astype(BF16)
    vg_ref[3:4, :] = jnp.sum(gain_sum, axis=0, keepdims=True)
    vg_ref[4:5, :] = jnp.sum(shift_sum, axis=0, keepdims=True)
    vg_ref[2:3, :] = dot_nn(ones, low[...])[0:1]
    grown = dot_tn(low[...], mixed_ref[...]).reshape(GROUPS, ROWS, D)
    og_ref[...] = jnp.concatenate([grown, jnp.zeros((GROUPS, 8, D), F32)], axis=1).astype(BF16)
    for i in range(6):
        settle(outs[i], sems.at[4 + i])


def middle(table, core, layer_input, mixed, cotangent, vectors, own_b, other_b, own, other):
    part = jax.ShapeDtypeStruct((GROUPS // 2, 2, ROWS, D), BF16)
    return pl.pallas_call(
        middle_kernel,
        in_specs=[SMEM, SMEM, VMEM, VMEM, VMEM, VMEM] + [ANY] * 12,
        out_specs=[VMEM] * 5 + [ANY] * 6,
        out_shape=(
            jax.ShapeDtypeStruct((TOKENS, D), BF16),
            jax.ShapeDtypeStruct((TOKENS, D), F32),
            jax.ShapeDtypeStruct((TOKENS, D), BF16),
            jax.ShapeDtypeStruct((GROUPS, 32, D), BF16),
            jax.ShapeDtypeStruct((16, D), F32),
        )
        + (part,) * 4
        + (jax.ShapeDtypeStruct((2, GROUPS // 2, 2, ROWS, D), BF16),) * 2,
        scratch_shapes=[
            pltpu.VMEM((GROUPS, 32, D), BF16),
            pltpu.VMEM((D, D), BF16),
            pltpu.VMEM((FF, D), BF16),
            pltpu.VMEM((GROUPS, 48, D), BF16),
            pltpu.VMEM((GROUPS, 48, D), BF16),
            pltpu.VMEM((D, FF), BF16),
            pltpu.VMEM((TOKENS, FF), BF16),
            pltpu.VMEM((TOKENS, FF), BF16),
            pltpu.VMEM((TOKENS, D), BF16),
            pltpu.VMEM((TOKENS, D), F32),
            pltpu.VMEM((TOKENS, 1), F32),
            pltpu.VMEM((TOKENS, D), F32),
            pltpu.VMEM((TOKENS, D), BF16),
            pltpu.VMEM((D, TOKENS), BF16),
            pltpu.VMEM((GROUPS, 4, ROWS, D), BF16),
            pltpu.VMEM((4, GROUPS, ROWS, D), BF16),
            pltpu.SemaphoreType.DMA((10,)),
        ],
        compiler_params=pltpu.CompilerParams(vmem_limit_bytes=LIMIT),
        cost_estimate=pl.CostEstimate(flops=16 * 10**9, bytes_accessed=30 * 10**6, transcendentals=3145728),
        name="middle",
    )(table, core, layer_input, mixed, cotangent, vectors, *own_b, *other_b, *own, *other)


def pair_back(counts, q_ref, k_ref, v_ref, mixed_ref, slope_ref, probs_ref, cot_ref, out_ref):
    low_lane = lax.broadcasted_iota(jnp.int32, (TOKENS, PAIR), 1) < HEAD
    segments = unit_segments(counts)
    scale = jnp.asarray(HEAD ** (-0.5), BF16)
    slope = slope_ref[...]
    query = q_ref[...] * scale
    key = k_ref[...] * scale
    value = v_ref[...]
    product = slope.astype(F32) * mixed_ref[...].astype(F32)
    queries, keys, values = [], [], []
    for head in range(2):
        chosen = low_lane if head == 0 else ~low_lane
        masked = jnp.where(chosen, slope, jnp.zeros_like(slope))
        shared = jnp.sum(jnp.where(chosen, product, 0.0), axis=-1, keepdims=True)
        products = dot_nt(masked, value)
        for block in range(DEV_UNITS):
            rows = slice(block * UNIT, (block + 1) * UNIT)
            allowed = allowed_lanes(segments, block)
            grown = probs_ref[head, rows, :].astype(F32) * (products[rows] - shared[rows])
            grown = grown + jnp.where(allowed, cot_ref[head, rows, :].astype(F32), 0.0)
            out_ref[head, rows, :] = grown.astype(BF16)
        logits = out_ref[head]
        heads = slice(head * HEAD, (head + 1) * HEAD)
        queries.append(dot_nn(logits, key))
        keys.append(dot_tn(query[:, heads], logits))
        values.append(dot_tn(slope[:, heads], probs_ref[head]))
    return (
        jnp.where(low_lane, queries[0], queries[1]).astype(BF16),
        jnp.concatenate(keys, axis=0).astype(BF16),
        jnp.concatenate(values, axis=0).astype(BF16),
    )


def attend_back_kernel(counts, *refs):
    dq_ref, dk_ref, dv_ref = refs[8:11]
    dq_ref[...], dk_ref[...], dv_ref[...] = pair_back(counts, *refs[0:8])


FIRST = 2
EARLY = PAIR * FIRST


def attend_back(counts, queries, keys, values, mixed, mixed_low, probs, logits_cotangent):
    columns = pl.BlockSpec((TOKENS, PAIR), lambda i, *_: (0, i))
    turned = pl.BlockSpec((PAIR, TOKENS), lambda i, *_: (i, 0))
    logits = pl.BlockSpec((2, TOKENS, TOKENS), lambda i, *_: (i, 0, 0))
    return pl.pallas_call(
        attend_back_kernel,
        grid_spec=pltpu.PrefetchScalarGridSpec(
            num_scalar_prefetch=1,
            grid=(FIRST,),
            in_specs=[columns] * 5 + [logits] * 2,
            out_specs=[logits, columns, turned, turned],
        ),
        out_shape=(
            jax.ShapeDtypeStruct((H, TOKENS, TOKENS), BF16),
            jax.ShapeDtypeStruct((TOKENS, D), BF16),
            jax.ShapeDtypeStruct((D, TOKENS), BF16),
            jax.ShapeDtypeStruct((D, TOKENS), BF16),
        ),
        compiler_params=pltpu.CompilerParams(vmem_limit_bytes=LIMIT),
        cost_estimate=pl.CostEstimate(flops=2 * 10**9, bytes_accessed=7 * 10**6, transcendentals=0),
        name="attend_back_first",
    )(counts, queries, keys, values, mixed, mixed_low, probs, logits_cotangent)


def rest_kernel(table, core, counts, *refs):
    vg_ref, x_in, og_in, logits_in, dq_in, dk_in, dv_in = refs[7:14]
    out_ref, dq_ref, dk_ref, dv_ref = refs[14:18]
    outs = refs[18:24]
    x_ref, og_ref, dq_all, dk_all, dv_all, d_q, d_k, d_v = refs[24:32]
    sems, in_sems = refs[32:34]
    step = pl.program_id(0)
    ones = jnp.ones((8, TOKENS), BF16)
    brought = (
        (x_in, x_ref),
        (dq_in.at[:, pl.ds(0, EARLY)], dq_all.at[:, pl.ds(0, EARLY)]),
        (dk_in.at[pl.ds(0, EARLY)], dk_all.at[pl.ds(0, EARLY)]),
        (dv_in.at[pl.ds(0, EARLY)], dv_all.at[pl.ds(0, EARLY)]),
        (og_in, og_ref),
    )

    @pl.when(step == 0)
    def _():
        for i, (source, target) in enumerate(brought):
            pltpu.make_async_copy(source, target, in_sems.at[i]).start()

    dq, dk, dv = pair_back(counts, *refs[0:7], out_ref)
    dq_ref[...] = dq
    dk_ref[...] = dk
    dv_ref[...] = dv

    rows = pl.ds(pl.multiple_of((step + FIRST) * PAIR, PAIR), PAIR)
    dq_all[:, rows] = dq
    dk_all[rows, :] = dk
    dv_all[rows, :] = dv

    def send(source, half, part):
        def copies(own):
            row = part if own else 2 + part
            for second in (1, 0):
                target = outs[2 * second + part] if own else outs[4 + second].at[part]
                sem = sems.at[2 * second + part] if own else sems.at[4 + second]

                def body(i, carry):
                    pltpu.make_async_copy(
                        source.at[table[row, i + 16 * second]], target.at[i], sem
                    ).start()
                    return carry

                lax.fori_loop(0, GROUPS // 2, body, 0)

        pl.when(core[0] == half)(lambda: copies(True))
        pl.when(core[0] != half)(lambda: copies(False))

    def padded(values):
        rows = values.reshape(GROUPS, ROWS, D)
        return jnp.concatenate([rows, jnp.zeros((GROUPS, 8, D), F32)], axis=1).astype(BF16)

    @pl.when(step == pl.num_programs(0) - 1)
    def _():
        for i, (source, target) in enumerate(brought):
            pltpu.make_async_copy(source, target, in_sems.at[i]).wait()
        send(og_ref, 1, 1)
        x = x_ref[...]
        d_q[...] = padded(dot_tn(dq_all[...], x))
        send(d_q, 0, 0)
        d_v[...] = padded(dot_nn(dv_all[...], x))
        send(d_v, 1, 0)
        query_sum = dot_nn(ones, dq_all[...])
        value_sum = dot_nt(ones, dv_all[...])
        rows8 = lax.broadcasted_iota(jnp.int32, (8, D), 0)
        offsets = vg_ref[0:8, :]
        offsets = jnp.where(
            rows8 == 0, query_sum[0:1, :], jnp.where(rows8 == 1, value_sum[0:1, :], offsets)
        )
        group = lax.broadcasted_iota(jnp.int32, (32, 8, D), 0)
        lane = lax.broadcasted_iota(jnp.int32, (32, 8, D), 2)
        chosen = jnp.where(lane // ROWS == group, offsets[None], 0.0)
        row = lax.broadcasted_iota(jnp.int32, (D, 128), 0)
        column = lax.broadcasted_iota(jnp.int32, (D, 128), 1)
        narrow = dot_nn(chosen.reshape(256, D).astype(BF16), (row % ROWS == column).astype(BF16))
        wide = jnp.broadcast_to(vg_ref[8:12, :][:, None, :], (4, 8, D))
        second = lax.broadcasted_iota(jnp.int32, (4, 8, D), 1)
        lane = lax.broadcasted_iota(jnp.int32, (4, 8, D), 2)
        chosen = jnp.where(lane // 96 == second, wide, 0.0).reshape(32, D)
        inner = dot_nn(chosen.astype(BF16), (row % 96 == column).astype(BF16))
        place = lax.broadcasted_iota(jnp.int32, (32, 8, 128), 1)
        inner = jnp.where(place == 0, inner[:, None, :], 0.0)
        small = jnp.concatenate(
            [narrow.reshape(32, 8, 128), inner, jnp.zeros((32, 8, D - 256), F32)], axis=2
        )
        d_k[...] = jnp.concatenate(
            [dot_nn(dk_all[...], x).reshape(GROUPS, ROWS, D), small], axis=1
        ).astype(BF16)
        send(d_k, 0, 1)
        for i in range(6):
            settle(outs[i], sems.at[i])


def rest(table, core, counts, queries, keys, values, mixed, mixed_low, probs, logits_cotangent, layer_input, held, og, vg):
    columns = pl.BlockSpec((TOKENS, PAIR), lambda i, *_: (0, i + FIRST))
    turned = pl.BlockSpec((PAIR, TOKENS), lambda i, *_: (i + FIRST, 0))
    logits = pl.BlockSpec((2, TOKENS, TOKENS), lambda i, *_: (i + FIRST, 0, 0))
    kept = jax.ShapeDtypeStruct((GROUPS // 2, 32, D), BF16)
    sent = jax.ShapeDtypeStruct((2, GROUPS // 2, 32, D), BF16)
    return pl.pallas_call(
        rest_kernel,
        grid_spec=pltpu.PrefetchScalarGridSpec(
            num_scalar_prefetch=3,
            grid=(H // 2 - FIRST,),
            in_specs=[columns] * 5
            + [logits] * 2
            + [pl.BlockSpec((16, D), lambda i, *_: (0, 0))]
            + [ANY] * 6,
            out_specs=[logits, columns, turned, turned] + [ANY] * 6,
            scratch_shapes=[
                pltpu.VMEM((TOKENS, D), BF16),
                pltpu.VMEM((GROUPS, 32, D), BF16),
                pltpu.VMEM((TOKENS, D), BF16),
                pltpu.VMEM((D, TOKENS), BF16),
                pltpu.VMEM((D, TOKENS), BF16),
                pltpu.VMEM((GROUPS, 32, D), BF16),
                pltpu.VMEM((GROUPS, 32, D), BF16),
                pltpu.VMEM((GROUPS, 32, D), BF16),
                pltpu.SemaphoreType.DMA((6,)),
                pltpu.SemaphoreType.DMA((5,)),
            ],
        ),
        out_shape=(
            jax.ShapeDtypeStruct((H, TOKENS, TOKENS), BF16),
            jax.ShapeDtypeStruct((TOKENS, D), BF16),
            jax.ShapeDtypeStruct((D, TOKENS), BF16),
            jax.ShapeDtypeStruct((D, TOKENS), BF16),
            kept,
            kept,
            kept,
            kept,
            sent,
            sent,
        ),
        input_output_aliases={13 + i: i for i in range(4)},
        compiler_params=pltpu.CompilerParams(vmem_limit_bytes=LIMIT),
        cost_estimate=pl.CostEstimate(flops=6 * 10**9, bytes_accessed=25 * 10**6, transcendentals=0),
        name="attend_back_rest",
    )(
        table,
        core,
        counts,
        queries,
        keys,
        values,
        mixed,
        mixed_low,
        probs,
        logits_cotangent,
        vg,
        layer_input,
        og,
        *held,
    )


def pack_kernel(core, *refs):
    query, key, value, output, inner, outer = refs[0:6]
    small = refs[6:15]
    mine_ref, other_ref, first, second = refs[15:19]
    first[...] = jnp.zeros_like(first)
    second[...] = jnp.zeros_like(second)
    first[0:6, :] = query[...].astype(F32)
    first[6:12, :] = key[...].astype(F32)
    first[12:36, :] = inner[...].astype(F32)
    for i, ref in enumerate(small):
        row, lane = 36 + i // 6, 128 * (i % 6)
        first[row : row + 1, lane : lane + ref.shape[1]] = ref[...].astype(F32)
    second[0:6, :] = value[...].astype(F32)
    second[6:12, :] = output[...].astype(F32)
    for i in range(4):
        second[12 + 6 * i : 18 + 6 * i, :] = outer[:, D * i : D * (i + 1)].astype(F32)

    @pl.when(core[0] == 0)
    def _():
        mine_ref[...] = first[...].astype(BF16)
        other_ref[...] = second[...].astype(BF16)

    @pl.when(core[0] != 0)
    def _():
        mine_ref[...] = second[...].astype(BF16)
        other_ref[...] = first[...].astype(BF16)


def pack(core, kernels, small):
    half = jax.ShapeDtypeStruct((40, D), BF16)
    return pl.pallas_call(
        pack_kernel,
        in_specs=[SMEM] + [VMEM] * 15,
        out_specs=[VMEM] * 2,
        out_shape=(half, half),
        scratch_shapes=[pltpu.VMEM((40, D), F32)] * 2,
        name="pack",
    )(core, *(kernel.T for kernel in kernels), *(v.reshape(1, -1) for v in small))


def finish_kernel(place, ff_own, ff_other, tail_own, tail_other, query, key, value, output, inner, outer, *small):
    def write(mine, ff_first, ff_second, tail_first, tail_second):
        rows = slice(6 * mine, 6 * mine + 6)
        for ref, part, skip in (
            (query, tail_first, 0),
            (key, tail_first, 24),
            (value, tail_second, 0),
            (output, tail_second, 24),
        ):
            ref[...] = part[skip + rows.start : skip + rows.stop, :]
        inner[...] = ff_first[24 * mine : 24 * mine + 24, :]
        for i in range(4):
            outer[:, D * i : D * (i + 1)] = ff_second[24 * i + rows.start : 24 * i + rows.stop, :]
        for i in range(8):
            small[i][...] = tail_first[48 + i : 49 + i, rows]
        small[8][...] = tail_first[48:49, 128 + 24 * mine : 152 + 24 * mine]

    for mine in range(4):

        @pl.when(place[0] == mine)
        def _():
            if mine < 2:
                write(mine, ff_own, ff_other, tail_own, tail_other)
            else:
                write(mine, ff_other, ff_own, tail_other, tail_own)


def finish(mine, ff_own, ff_other, tail_own, tail_other):
    narrow = jax.ShapeDtypeStruct((6, D), F32)
    outs = pl.pallas_call(
        finish_kernel,
        in_specs=[SMEM] + [VMEM] * 4,
        out_specs=[VMEM] * 15,
        out_shape=(
            narrow,
            narrow,
            narrow,
            narrow,
            jax.ShapeDtypeStruct((24, D), F32),
            jax.ShapeDtypeStruct((6, FF), F32),
        )
        + (jax.ShapeDtypeStruct((1, 6), F32),) * 8
        + (jax.ShapeDtypeStruct((1, 24), F32),),
        name="finish",
    )(mine.astype(jnp.int32).reshape(1), ff_own, ff_other, tail_own, tail_other)
    return tuple(out.T for out in outs[:6]) + tuple(out.reshape(-1) for out in outs[6:])


def gather_weights(core_table, kernels, vectors, inner_offset):
    core, low_x = lax.axis_index("c"), lax.axis_index("xl")
    mine = core * 2 + low_x
    own, other = pack(core_table, kernels, (*vectors, inner_offset))
    pieces = jnp.stack(
        [
            own,
            swap(own, "xl"),
            swap(other, "c"),
            lax.ppermute(other, ("c", "xl"), [(i, 3 - i) for i in range(4)]),
        ]
    )
    natural = jnp.concatenate(
        [lax.dynamic_slice_in_dim(pieces, mine ^ i, 1, axis=0) for i in range(4)], axis=0
    )
    first = core == 0
    near_a = natural[:, 0:6].reshape(ROWS, D)
    near_b = natural[:, 6:12].reshape(ROWS, D)
    inner = natural[:, 12:36].reshape(96, D)
    outer = natural[:, 12:36].reshape(4, 4, 6, D).transpose(1, 0, 2, 3).reshape(96, D)
    offsets = natural[:, 36:38].reshape(4, 12, 128)[:, 0:8, 0:6].transpose(1, 0, 2).reshape(8, ROWS)
    offsets = jnp.pad(offsets, ((0, 0), (0, 128 - ROWS)))
    wide_offset = jnp.pad(natural[:, 37, 256:280].reshape(1, 96), ((0, 7), (0, 32)))
    small = jnp.concatenate([offsets, wide_offset, jnp.zeros((8, D - 256), BF16)], axis=1)
    wide = jnp.where(first, inner, outer)
    block = jnp.concatenate([near_a, wide[0:48], near_b, small, wide[48:96]], axis=0)
    both = jnp.stack([block, exchange(block, STEPS_A[0])])
    part_a, part_b = both[:, 0:72], both[:, 72:152]
    for i in (1, 2):
        arrived_a, arrived_b = after((exchange(part_a, STEPS_A[i]), exchange(part_b, STEPS_B[i])))
        part_a = jnp.concatenate([part_a, arrived_a], axis=0)
        part_b = jnp.concatenate([part_b, arrived_b], axis=0)
    arrived_a, arrived_b = after((exchange(part_a, STEPS_A[3]), exchange(part_b, STEPS_B[3])))
    near_a = jnp.concatenate([part_a[:, 0:24], arrived_a[:, 0:24]], axis=0)
    near_b = jnp.concatenate([part_b[:, 0:32], arrived_b[:, 0:32]], axis=0)
    far_a = jnp.concatenate([part_a[:, 24:72], arrived_a[:, 24:72]], axis=0)
    far_b = jnp.concatenate([part_b[:, 32:80], arrived_b[:, 32:80]], axis=0)
    last_a, last_b = exchange(near_a, STEPS_A[4]), exchange(near_b, STEPS_B[4])
    far_a, far_b, last_a, last_b = after((far_a, far_b, last_a, last_b))
    near = (near_a, last_a, near_b, last_b)
    return near, tuple(swap(part, "c") for part in near), (far_a, far_b)


def after(values, *others):
    return lax.optimization_barrier((values, others))[0] if others else lax.optimization_barrier(values)


def add(first, second):
    return (first.astype(F32) + second.astype(F32)).astype(BF16)


def add3(first, second, third):
    return (first.astype(F32) + second.astype(F32) + third.astype(F32)).astype(BF16)


def split(*arrays):
    half = arrays[0].shape[0] // 2
    combine = add if len(arrays) == 2 else add3
    return combine(*(a[:half] for a in arrays)), combine(*(a[half:] for a in arrays))


def halve(total, step):
    return split(total[0], exchange(total[1], step))


def reduce_end(total_a, total_b):
    kept, sent = (
        jnp.concatenate([total_a[i].reshape(-1, D), total_b[i].reshape(-1, D)], axis=0) for i in range(2)
    )
    total = add(kept, exchange(sent, STEPS_A[0]))
    own = total.astype(F32) + swap(total, "xl").astype(F32)
    return own, swap(own, "c")


def body(
    layer_input,
    prior_logits,
    bucket_counts,
    output_cotangent,
    logits_cotangent,
    query_kernel,
    query_offset,
    key_kernel,
    value_kernel,
    value_offset,
    output_kernel,
    output_offset,
    first_gain,
    first_shift,
    inner_kernel,
    inner_offset,
    outer_kernel,
    outer_offset,
    second_gain,
    second_shift,
):
    core, low_x = lax.axis_index("c"), lax.axis_index("xl")
    mine = core * 2 + low_x
    table = jnp.stack(
        [
            position_groups(STEPS_A, core),
            position_groups(STEPS_B, core),
            position_groups(STEPS_A, 1 - core),
            position_groups(STEPS_B, 1 - core),
        ]
    )
    core_table = core.astype(jnp.int32).reshape(1)
    near, near_other, far = gather_weights(
        core_table,
        (query_kernel, key_kernel, value_kernel, output_kernel, inner_kernel, outer_kernel),
        (
            query_offset,
            value_offset,
            output_offset,
            first_gain,
            first_shift,
            outer_offset,
            second_gain,
            second_shift,
        ),
        inner_offset,
    )
    far_last = (exchange(far[0], STEPS_A[4]), exchange(far[1], STEPS_B[4]))
    far_other = [swap(far[0], "c"), None, swap(far[1], "c"), None]
    queries, keys, values, query_matrix, key_matrix, value_matrix, vectors = project(
        table, core_table, layer_input, near, near_other
    )
    raw_logits, probs, mixed = attend(bucket_counts, queries, keys, values, prior_logits, 0, 6, ())
    far_last, mixed = after((far_last, mixed))
    far_other[1], far_other[3] = swap(far_last[0], "c"), swap(far_last[1], "c")
    layer_output, first_slope, mixed_low, output_slope, vector_slopes, *ff = middle(
        table,
        core_table,
        layer_input,
        mixed,
        output_cotangent,
        vectors,
        near[2:4],
        near_other[2:4],
        (far[0], far_last[0], far[1], far_last[1]),
        far_other,
    )

    moved = swap(ff[5], "c")
    heads = (queries, keys, values, mixed, mixed_low, probs, logits_cotangent)
    held = attend_back(bucket_counts, *heads)
    moved, held = after((moved, held))
    moved_late = swap(ff[4], "c")
    sent_a, sent_b = add(ff[2], moved[0]), add(ff[3], moved[1])
    held, sent_a, sent_b = after((held, sent_a, sent_b))
    logits_slope, dq, dk, dv, *tail = rest(
        table, core_table, bucket_counts, *heads, layer_input, held, output_slope, vector_slopes
    )
    arrived_a, arrived_b = exchange(sent_a, STEPS_A[4]), exchange(sent_b, STEPS_B[4])
    arrived_a, arrived_b, tail = after((arrived_a, arrived_b, tuple(tail)))
    tail_moved = swap(tail[5], "c")
    ff_a = split(ff[0], moved_late[0], arrived_a)
    ff_b = split(ff[1], moved_late[1], arrived_b)
    tail_moved, ff_a, ff_b = after((tail_moved, ff_a, ff_b))
    late = swap(tail[4], "c")
    tail_sent = [
        add(tail[2][:, :ROWS], tail_moved[0][:, :ROWS]),
        add(tail[3], tail_moved[1]),
    ]
    (dq, dk, dv), tail_sent = after(((dq, dk, dv), tail_sent))
    input_slope = (
        first_slope + dot_nn(dq, query_matrix) + dot_tn(dk, key_matrix) + dot_tn(dv, value_matrix)
    ).astype(BF16)
    tail_arrived = after(
        (exchange(tail_sent[0], STEPS_A[4]), exchange(tail_sent[1], STEPS_B[4])), input_slope
    )
    tail_a = split(tail[0][:, :ROWS], late[0][:, :ROWS], tail_arrived[0])
    tail_b = split(tail[1], late[1], tail_arrived[1])
    for i in (3, 2, 1):
        arrived_a, arrived_b = after((exchange(tail_a[1], STEPS_A[i]), exchange(tail_b[1], STEPS_B[i])))
        tail_a, tail_b = split(tail_a[0], arrived_a), split(tail_b[0], arrived_b)
        ff_a, ff_b = halve(ff_a, STEPS_A[i]), halve(ff_b, STEPS_B[i])
    ff_sums = reduce_end(ff_a, ff_b)
    tail_sums = reduce_end(tail_a, tail_b)
    query_owned, key_owned, value_owned, output_owned, inner_owned, outer_owned, *small = finish(
        mine, *ff_sums, *tail_sums
    )

    return (
        layer_output,
        raw_logits,
        input_slope,
        logits_slope,
        query_owned,
        small[0],
        key_owned,
        value_owned,
        small[1],
        output_owned,
        small[2],
        small[3],
        small[4],
        inner_owned,
        small[8],
        outer_owned,
        small[5],
        small[6],
        small[7],
    )


def solution(mesh):
    fine = Mesh(mesh.devices.reshape(SIZES), AXES)
    rows = P(AXES, None)
    logits = P(None, AXES, None)
    columns = P(None, AXES)
    vector = P(AXES)
    return jax.shard_map(
        body,
        mesh=fine,
        in_specs=(
            rows,
            logits,
            rows,
            rows,
            logits,
            columns,
            vector,
            columns,
            columns,
            vector,
            columns,
            vector,
            vector,
            vector,
            columns,
            vector,
            columns,
            vector,
            vector,
            vector,
        ),
        out_specs=(
            rows,
            logits,
            rows,
            logits,
            columns,
            vector,
            columns,
            columns,
            vector,
            columns,
            vector,
            vector,
            vector,
            columns,
            vector,
            columns,
            vector,
            vector,
            vector,
        ),
        check_vma=False,
    )
```

```python
import jax
import jax.numpy as jnp
from jax import lax
from jax.experimental import pallas as pl
from jax.experimental.pallas import tpu as pltpu
from jax.sharding import Mesh
from jax.sharding import PartitionSpec as P

D = 768
H = 12
HEAD = 64
FF = 3072
UNIT = 128
DEV_UNITS = 4
EPSILON = 1e-12

AXES = ("xh", "z", "y", "c", "xl")
SIZES = (2, 4, 4, 2, 2)
GROUPS = 32
ROWS = 24
MASKS = ((1, 3), (3, 1))
STEPS_A = (("x", 0), ("z", 0), ("z", 1), ("y", 0), ("y", 1))
STEPS_B = (("x", 0), ("y", 0), ("y", 1), ("z", 0), ("z", 1))
BF16 = jnp.bfloat16
F32 = jnp.float32


def exchange(values, step):
    axis, turn = step
    if axis == "x":
        return lax.ppermute(values, ("xh", "xl"), [(i, 3 - i) for i in range(4)])
    pairs = []
    for i in range(4):
        for core in range(2):
            pairs.append((i * 2 + core, (i ^ MASKS[core][turn]) * 2 + core))
    return lax.ppermute(values, (axis, "c"), pairs)


def swap(values, axis):
    return lax.ppermute(values, axis, [(0, 1), (1, 0)])


def position_groups(steps, core):
    position = jnp.arange(GROUPS, dtype=jnp.int32)
    place = {
        "x": jnp.full((GROUPS,), lax.axis_index("xh"), jnp.int32),
        "y": jnp.full((GROUPS,), lax.axis_index("y"), jnp.int32),
        "z": jnp.full((GROUPS,), lax.axis_index("z"), jnp.int32),
    }
    for bit, (axis, turn) in enumerate(steps):
        if axis == "x":
            mask = 1
        else:
            mask = jnp.where(core == 0, MASKS[0][turn], MASKS[1][turn])
        place[axis] = place[axis] ^ (((position >> bit) & 1) * mask)
    return (place["x"] * 4 + place["z"]) * 4 + place["y"]


ANY = pl.BlockSpec(memory_space=pl.ANY)
VMEM = pl.BlockSpec(memory_space=pltpu.VMEM)
SMEM = pl.BlockSpec(memory_space=pltpu.SMEM)
TOKENS = 512
PAIR = 2 * HEAD
LIMIT = 58 * 1024 * 1024


def dot_nt(rows, matrix):
    return lax.dot_general(rows, matrix, (((1,), (1,)), ((), ())), preferred_element_type=F32)


def dot_nn(rows, matrix):
    return lax.dot_general(rows, matrix, (((1,), (0,)), ((), ())), preferred_element_type=F32)


def dot_tn(rows, matrix):
    return lax.dot_general(rows, matrix, (((0,), (0,)), ((), ())), preferred_element_type=F32)


def fetch(table, core, own, other, targets, sems):
    def place(parts, half, row):
        for part in range(2):
            if (half, part) not in targets:
                continue
            where, sem = targets[half, part]
            for second in range(2):
                source = parts[2 * part + second]

                def body(i, carry):
                    group = table[row + part, i + 16 * second]
                    pltpu.make_async_copy(source.at[i], where(group), sems.at[sem]).start()
                    return carry

                lax.fori_loop(0, 16, body, 0)

    @pl.when(core[0] == 0)
    def _():
        place(own, 0, 0)
        place(other, 1, 2)

    @pl.when(core[0] != 0)
    def _():
        place(own, 1, 0)
        place(other, 0, 2)


def settle(ref, sem):
    pltpu.make_async_copy(ref, ref, sem).wait()


def straighten(raw, skip, store):
    for i in range(4):
        block = raw[8 * i : 8 * i + 8].astype(F32)[:, skip : skip + ROWS]
        store(i, block.reshape(8 * ROWS, D).astype(BF16))


def project_kernel(table, core, x_ref, *refs):
    own, other = refs[0:4], refs[4:8]
    q_ref, k_ref, v_ref, wq_ref, wk_ref, wv_ref, vec_ref = refs[8:15]
    raw_q, raw_k, raw_v, sems = refs[15:19]
    targets = {
        (0, 0): (lambda g: raw_q.at[g], 0),
        (0, 1): (lambda g: raw_k.at[g], 1),
        (1, 0): (lambda g: raw_v.at[g], 2),
    }
    fetch(table, core, own, other, targets, sems)

    def keep(ref):
        def store(i, rows):
            ref[192 * i : 192 * (i + 1), :] = rows

        return store

    settle(raw_k, sems.at[1])
    small = raw_k[...].astype(F32)[:, ROWS : ROWS + 8, 0:256]
    row = lax.broadcasted_iota(jnp.int32, (128, D), 0)
    lane = lax.broadcasted_iota(jnp.int32, (128, D), 1)
    spread = (lane % ROWS == row).astype(BF16)
    wide = dot_nn(small[:, :, 0:128].reshape(256, 128).astype(BF16), spread).reshape(32, 8, D)
    group = lax.broadcasted_iota(jnp.int32, (32, 8, D), 0)
    lane3 = lax.broadcasted_iota(jnp.int32, (32, 8, D), 2)
    vec_ref[0:8, :] = jnp.sum(jnp.where(lane3 // ROWS == group, wide, 0.0), axis=0)
    spread = ((lane % 96 == row) & (row < 96)).astype(BF16)
    wide = dot_nn(small[:, :, 128:256].reshape(256, 128).astype(BF16), spread).reshape(4, 8, 8, D)
    second = lax.broadcasted_iota(jnp.int32, (4, 8, 8, D), 1)
    place = lax.broadcasted_iota(jnp.int32, (4, 8, 8, D), 2)
    lane4 = lax.broadcasted_iota(jnp.int32, (4, 8, 8, D), 3)
    chosen = jnp.where((lane4 // 96 == second) & (place == 0), wide, 0.0)
    inner_rows = jnp.sum(chosen, axis=1)
    for i in range(4):
        vec_ref[8 + i : 9 + i, :] = inner_rows[i, 0:1, :]
    vec_ref[12:16, :] = jnp.zeros((4, D), F32)

    x = x_ref[...]
    straighten(raw_k, 0, keep(wk_ref))
    k_ref[...] = dot_nt(x, wk_ref[...]).astype(BF16)
    settle(raw_q, sems.at[0])
    straighten(raw_q, 0, keep(wq_ref))
    q_ref[...] = (dot_nt(x, wq_ref[...]) + vec_ref[0:1, :]).astype(BF16)
    settle(raw_v, sems.at[2])
    straighten(raw_v, 0, keep(wv_ref))
    v_ref[...] = (dot_nt(x, wv_ref[...]) + vec_ref[1:2, :]).astype(BF16)


def project(table, core, layer_input, own, other):
    rows = jax.ShapeDtypeStruct((TOKENS, D), BF16)
    square = jax.ShapeDtypeStruct((D, D), BF16)
    return pl.pallas_call(
        project_kernel,
        in_specs=[SMEM, SMEM, VMEM] + [ANY] * 8,
        out_specs=[VMEM] * 7,
        out_shape=(rows, rows, rows, square, square, square, jax.ShapeDtypeStruct((16, D), F32)),
        scratch_shapes=[
            pltpu.VMEM((GROUPS, ROWS, D), BF16),
            pltpu.VMEM((GROUPS, 32, D), BF16),
            pltpu.VMEM((GROUPS, ROWS, D), BF16),
            pltpu.SemaphoreType.DMA((3,)),
        ],
        compiler_params=pltpu.CompilerParams(vmem_limit_bytes=LIMIT),
        cost_estimate=pl.CostEstimate(flops=2 * 10**9, bytes_accessed=12 * 10**6, transcendentals=0),
        name="project",
    )(table, core, layer_input, *own, *other)


def attend_kernel(counts, q_ref, k_ref, v_ref, prior_ref, *refs):
    raw_ref, probs_ref, mixed_ref = refs[-3:]
    query = q_ref[...] * jnp.asarray(HEAD ** (-0.5), BF16)
    key = k_ref[...]
    value = v_ref[...]
    low_lane = lax.broadcasted_iota(jnp.int32, (TOKENS, PAIR), 1) < HEAD
    segments = unit_segments(counts)
    extended = jnp.concatenate([value, jnp.ones_like(value)], axis=1)
    results = []
    for head in range(2):
        chosen = low_lane if head == 0 else ~low_lane
        masked = jnp.where(chosen, query, jnp.zeros_like(query))
        products = dot_nt(masked, key)
        parts = []
        for block in range(DEV_UNITS):
            rows = slice(block * UNIT, (block + 1) * UNIT)
            allowed = allowed_lanes(segments, block)
            scores = products[rows] + prior_ref[head, rows, :].astype(F32)
            raw_ref[head, rows, :] = jnp.where(allowed, scores, 0.0).astype(BF16)
            scores = jnp.where(allowed, scores, -1e30)
            grown = jnp.exp(scores - jnp.max(scores, axis=-1, keepdims=True))
            summed = dot_nn(grown.astype(BF16), extended)
            inverse = 1.0 / summed[:, PAIR:]
            probs_ref[head, rows, :] = (grown * jnp.concatenate([inverse] * 4, axis=1)).astype(BF16)
            parts.append(summed[:, :PAIR] * inverse)
        results.append(jnp.concatenate(parts, axis=0))
    mixed_ref[...] = jnp.where(low_lane, results[0], results[1]).astype(BF16)


def attend(counts, queries, keys, values, prior_logits, first, last, held):
    columns = pl.BlockSpec((TOKENS, PAIR), lambda i, *_: (0, i + first))
    logits = pl.BlockSpec((2, TOKENS, TOKENS), lambda i, *_: (i + first, 0, 0))
    logits_shape = jax.ShapeDtypeStruct((H, TOKENS, TOKENS), BF16)
    pairs = last - first
    return pl.pallas_call(
        attend_kernel,
        grid_spec=pltpu.PrefetchScalarGridSpec(
            num_scalar_prefetch=1,
            grid=(pairs,),
            in_specs=[columns] * 3 + [logits] + [ANY] * len(held),
            out_specs=[logits, logits, columns],
        ),
        out_shape=(logits_shape, logits_shape, jax.ShapeDtypeStruct((TOKENS, D), BF16)),
        input_output_aliases={5 + i: i for i in range(len(held))},
        compiler_params=pltpu.CompilerParams(vmem_limit_bytes=LIMIT),
        cost_estimate=pl.CostEstimate(
            flops=pairs * 10**9, bytes_accessed=pairs * 5 * 10**6, transcendentals=pairs * 2**19
        ),
        name="attend_%d" % first,
    )(counts, queries, keys, values, prior_logits, *held)


def unit_segments(counts):
    start = [counts[0, 0], counts[0, 0] + 2 * counts[0, 1]]
    start.append(start[1] + 3 * counts[0, 2])
    segments = []
    current = jnp.int32(-1)
    for unit in range(DEV_UNITS):
        first = unit < start[0]
        second = (unit >= start[0]) & (unit < start[1]) & ((unit - start[0]) % 2 == 0)
        third = (unit >= start[1]) & (unit < start[2]) & ((unit - start[1]) % 3 == 0)
        fourth = (unit >= start[2]) & ((unit - start[2]) % 4 == 0)
        current = current + jnp.where(first | second | third | fourth, 1, 0)
        segments.append(current)
    return segments


def allowed_lanes(segments, block):
    unit = lax.broadcasted_iota(jnp.int32, (1, TOKENS), 1) // UNIT
    same = jnp.zeros((1, TOKENS), jnp.int32)
    for other in range(DEV_UNITS):
        same = jnp.where(unit == other, jnp.where(segments[other] == segments[block], 1, 0), same)
    return same > 0


def mean_of(values):
    return jnp.sum(values, axis=-1, keepdims=True) * (1.0 / D)


def normalise(values):
    centred = values - mean_of(values)
    scale = lax.rsqrt(mean_of(centred * centred) + EPSILON)
    return centred * scale, scale


def norm_back(slope, normal, scale):
    return scale * (slope - mean_of(slope) - normal * mean_of(slope * normal))


def fold(values):
    return jnp.sum(values.reshape(values.shape[0] // 8, 8, D), axis=0)


HALVES = (slice(0, 256), slice(256, 512))


def middle_kernel(table, core, x_ref, mixed_ref, cot_ref, vec_ref, *refs):
    own_b, other_b = refs[0:2], refs[2:4]
    own, other = refs[4:8], refs[8:12]
    y_ref, first_ref, mixed_low_ref, og_ref, vg_ref = refs[12:17]
    outs = refs[17:23]
    (
        raw_o,
        wo,
        w_in,
        raw_a,
        raw_b,
        w_out,
        active,
        curve,
        normed,
        normal,
        scales,
        total,
        low,
        low_t,
        d_in,
        d_out,
        sems,
    ) = refs[23:40]

    fetch(table, core, (None, None) + own_b, (None, None) + other_b, {(1, 1): (lambda g: raw_o.at[g], 0)}, sems)

    def inner_place(skip):
        return lambda g: w_in.at[pl.ds(pl.multiple_of(g * 96 + skip, 48), 48)]

    targets = {
        (0, 0): (inner_place(0), 1),
        (0, 1): (inner_place(48), 1),
        (1, 0): (lambda g: raw_a.at[g], 2),
        (1, 1): (lambda g: raw_b.at[g], 3),
    }
    fetch(table, core, own, other, targets, sems)

    def keep_wo(i, rows):
        wo[192 * i : 192 * (i + 1), :] = rows

    settle(raw_o, sems.at[0])
    straighten(raw_o, 0, keep_wo)
    for rows in HALVES:
        attended = dot_nt(mixed_ref[rows, :], wo[...]) + vec_ref[2:3, :]
        values, scale = normalise(x_ref[rows, :].astype(F32) + attended)
        normal[rows, :] = values
        scales[rows, :] = scale
        normed[rows, :] = (values * vec_ref[3:4, :] + vec_ref[4:5, :]).astype(BF16)

    def keep_out(part):
        def store(i, rows):
            w_out[192 * i : 192 * (i + 1), part * D : (part + 1) * D] = rows

        return store

    settle(w_in, sems.at[1])
    for j in range(12):
        columns = slice(256 * j, 256 * (j + 1))
        place = slice(256 * (j % 3), 256 * (j % 3 + 1))
        inner = dot_nt(normed[...], w_in[columns, :]) + vec_ref[8 + j // 3 : 9 + j // 3, place]
        bell = 0.5 * (1.0 + lax.erf(inner * (0.5**0.5)))
        active[:, columns] = (inner * bell).astype(BF16)
        slope = bell + inner * jnp.exp(inner * inner * -0.5) * 0.3989422804014327
        curve[:, columns] = slope.astype(BF16)
        if j == 3:
            settle(raw_a, sems.at[2])
            settle(raw_b, sems.at[3])
        if j in (4, 6, 8, 10):
            part = (j - 4) // 2
            straighten(raw_a if part < 2 else raw_b, ROWS * (part % 2), keep_out(part))

    gain_sum, shift_sum = 0.0, 0.0
    for rows in HALVES:
        for j in range(3):
            columns = slice(256 * j, 256 * (j + 1))
            total[rows, columns] = dot_nt(active[rows, :], w_out[columns, :])
        values, scale = normalise(normed[rows, :].astype(F32) + (total[rows, :] + vec_ref[5:6, :]))
        y_ref[rows, :] = (values * vec_ref[6:7, :] + vec_ref[7:8, :]).astype(BF16)
        given = cot_ref[rows, :].astype(F32)
        gain_sum += fold(given * values)
        shift_sum += fold(given)
        slope = norm_back(given * vec_ref[6:7, :], values, scale)
        total[rows, :] = slope
        low[rows, :] = slope.astype(BF16)

    vg_ref[...] = jnp.zeros_like(vg_ref)
    ones = jnp.ones((8, TOKENS), BF16)
    vg_ref[6:7, :] = jnp.sum(gain_sum, axis=0, keepdims=True)
    vg_ref[7:8, :] = jnp.sum(shift_sum, axis=0, keepdims=True)
    vg_ref[5:6, :] = dot_nn(ones, low[...])[0:1]
    low_t[...] = low[...].T

    for j in range(12):
        columns = slice(256 * j, 256 * (j + 1))
        place = slice(256 * (j % 3), 256 * (j % 3 + 1))
        grown = dot_nn(low_t[...], active[:, columns])
        d_out[j // 3, :, :, place] = grown.reshape(GROUPS, ROWS, 256).astype(BF16)
        slope = dot_nn(low[...], w_out[:, columns])
        curve[:, columns] = (slope * curve[:, columns].astype(F32)).astype(BF16)

    for part in range(4):
        columns = slice(part * D, (part + 1) * D)
        grown = dot_tn(curve[:, columns], normed[...])
        d_in[8 * part : 8 * part + 8] = grown.reshape(8, 4, ROWS, D).astype(BF16)
        vg_ref[8 + part : 9 + part, :] = dot_nn(ones, curve[:, columns])[0:1]

    def send(own, half, row):
        for place in (2, 3, 0, 1):
            second, part = place // 2, place % 2
            target = outs[place] if own else outs[4 + second].at[part]
            sem = sems.at[4 + place] if own else sems.at[8 + second]

            def body(i, carry):
                group = table[row + part, i + 16 * second]
                if half == 0:
                    pltpu.make_async_copy(d_in.at[group, pl.ds(2 * part, 2)], target.at[i], sem).start()
                else:
                    for k in range(2):
                        pltpu.make_async_copy(d_out.at[2 * part + k, group], target.at[i, k], sem).start()
                return carry

            lax.fori_loop(0, GROUPS // 2, body, 0)

    @pl.when(core[0] == 0)
    def _():
        send(False, 1, 2)
        send(True, 0, 0)

    @pl.when(core[0] != 0)
    def _():
        send(False, 0, 2)
        send(True, 1, 0)

    gain_sum, shift_sum = 0.0, 0.0
    for rows in HALVES:
        for j in range(3):
            columns = slice(256 * j, 256 * (j + 1))
            total[rows, columns] += dot_nn(curve[rows, :], w_in[:, columns])
        given = total[rows, :]
        values = normal[rows, :]
        gain_sum += fold(given * values)
        shift_sum += fold(given)
        slope = norm_back(given * vec_ref[3:4, :], values, scales[rows, :])
        first_ref[rows, :] = slope
        low[rows, :] = slope.astype(BF16)
        mixed_low_ref[rows, :] = dot_nn(low[rows, :], wo[...]).astype(BF16)
    vg_ref[3:4, :] = jnp.sum(gain_sum, axis=0, keepdims=True)
    vg_ref[4:5, :] = jnp.sum(shift_sum, axis=0, keepdims=True)
    vg_ref[2:3, :] = dot_nn(ones, low[...])[0:1]
    grown = dot_tn(low[...], mixed_ref[...]).reshape(GROUPS, ROWS, D)
    og_ref[...] = jnp.concatenate([grown, jnp.zeros((GROUPS, 8, D), F32)], axis=1).astype(BF16)
    for i in range(6):
        settle(outs[i], sems.at[4 + i])


def middle(table, core, layer_input, mixed, cotangent, vectors, own_b, other_b, own, other):
    part = jax.ShapeDtypeStruct((GROUPS // 2, 2, ROWS, D), BF16)
    return pl.pallas_call(
        middle_kernel,
        in_specs=[SMEM, SMEM, VMEM, VMEM, VMEM, VMEM] + [ANY] * 12,
        out_specs=[VMEM] * 5 + [ANY] * 6,
        out_shape=(
            jax.ShapeDtypeStruct((TOKENS, D), BF16),
            jax.ShapeDtypeStruct((TOKENS, D), F32),
            jax.ShapeDtypeStruct((TOKENS, D), BF16),
            jax.ShapeDtypeStruct((GROUPS, 32, D), BF16),
            jax.ShapeDtypeStruct((16, D), F32),
        )
        + (part,) * 4
        + (jax.ShapeDtypeStruct((2, GROUPS // 2, 2, ROWS, D), BF16),) * 2,
        scratch_shapes=[
            pltpu.VMEM((GROUPS, 32, D), BF16),
            pltpu.VMEM((D, D), BF16),
            pltpu.VMEM((FF, D), BF16),
            pltpu.VMEM((GROUPS, 48, D), BF16),
            pltpu.VMEM((GROUPS, 48, D), BF16),
            pltpu.VMEM((D, FF), BF16),
            pltpu.VMEM((TOKENS, FF), BF16),
            pltpu.VMEM((TOKENS, FF), BF16),
            pltpu.VMEM((TOKENS, D), BF16),
            pltpu.VMEM((TOKENS, D), F32),
            pltpu.VMEM((TOKENS, 1), F32),
            pltpu.VMEM((TOKENS, D), F32),
            pltpu.VMEM((TOKENS, D), BF16),
            pltpu.VMEM((D, TOKENS), BF16),
            pltpu.VMEM((GROUPS, 4, ROWS, D), BF16),
            pltpu.VMEM((4, GROUPS, ROWS, D), BF16),
            pltpu.SemaphoreType.DMA((10,)),
        ],
        compiler_params=pltpu.CompilerParams(vmem_limit_bytes=LIMIT),
        cost_estimate=pl.CostEstimate(flops=16 * 10**9, bytes_accessed=30 * 10**6, transcendentals=3145728),
        name="middle",
    )(table, core, layer_input, mixed, cotangent, vectors, *own_b, *other_b, *own, *other)


def pair_back(counts, q_ref, k_ref, v_ref, mixed_ref, slope_ref, probs_ref, cot_ref, out_ref):
    low_lane = lax.broadcasted_iota(jnp.int32, (TOKENS, PAIR), 1) < HEAD
    segments = unit_segments(counts)
    scale = jnp.asarray(HEAD ** (-0.5), BF16)
    slope = slope_ref[...]
    query = q_ref[...] * scale
    key = k_ref[...] * scale
    value = v_ref[...]
    product = slope.astype(F32) * mixed_ref[...].astype(F32)
    queries, keys, values = [], [], []
    for head in range(2):
        chosen = low_lane if head == 0 else ~low_lane
        masked = jnp.where(chosen, slope, jnp.zeros_like(slope))
        shared = jnp.sum(jnp.where(chosen, product, 0.0), axis=-1, keepdims=True)
        products = dot_nt(masked, value)
        for block in range(DEV_UNITS):
            rows = slice(block * UNIT, (block + 1) * UNIT)
            allowed = allowed_lanes(segments, block)
            grown = probs_ref[head, rows, :].astype(F32) * (products[rows] - shared[rows])
            grown = grown + jnp.where(allowed, cot_ref[head, rows, :].astype(F32), 0.0)
            out_ref[head, rows, :] = grown.astype(BF16)
        logits = out_ref[head]
        heads = slice(head * HEAD, (head + 1) * HEAD)
        queries.append(dot_nn(logits, key))
        keys.append(dot_tn(query[:, heads], logits))
        values.append(dot_tn(slope[:, heads], probs_ref[head]))
    return (
        jnp.where(low_lane, queries[0], queries[1]).astype(BF16),
        jnp.concatenate(keys, axis=0).astype(BF16),
        jnp.concatenate(values, axis=0).astype(BF16),
    )


def attend_back_kernel(counts, *refs):
    dq_ref, dk_ref, dv_ref = refs[8:11]
    dq_ref[...], dk_ref[...], dv_ref[...] = pair_back(counts, *refs[0:8])


FIRST = 2
EARLY = PAIR * FIRST


def attend_back(counts, queries, keys, values, mixed, mixed_low, probs, logits_cotangent):
    columns = pl.BlockSpec((TOKENS, PAIR), lambda i, *_: (0, i))
    turned = pl.BlockSpec((PAIR, TOKENS), lambda i, *_: (i, 0))
    logits = pl.BlockSpec((2, TOKENS, TOKENS), lambda i, *_: (i, 0, 0))
    return pl.pallas_call(
        attend_back_kernel,
        grid_spec=pltpu.PrefetchScalarGridSpec(
            num_scalar_prefetch=1,
            grid=(FIRST,),
            in_specs=[columns] * 5 + [logits] * 2,
            out_specs=[logits, columns, turned, turned],
        ),
        out_shape=(
            jax.ShapeDtypeStruct((H, TOKENS, TOKENS), BF16),
            jax.ShapeDtypeStruct((TOKENS, D), BF16),
            jax.ShapeDtypeStruct((D, TOKENS), BF16),
            jax.ShapeDtypeStruct((D, TOKENS), BF16),
        ),
        compiler_params=pltpu.CompilerParams(vmem_limit_bytes=LIMIT),
        cost_estimate=pl.CostEstimate(flops=2 * 10**9, bytes_accessed=7 * 10**6, transcendentals=0),
        name="attend_back_first",
    )(counts, queries, keys, values, mixed, mixed_low, probs, logits_cotangent)


def rest_kernel(table, core, counts, *refs):
    vg_ref, x_in, og_in, logits_in, dq_in, dk_in, dv_in = refs[7:14]
    out_ref, dq_ref, dk_ref, dv_ref = refs[14:18]
    outs = refs[18:24]
    x_ref, og_ref, dq_all, dk_all, dv_all, d_q, d_k, d_v = refs[24:32]
    sems, in_sems = refs[32:34]
    step = pl.program_id(0)
    ones = jnp.ones((8, TOKENS), BF16)
    brought = (
        (x_in, x_ref),
        (dq_in.at[:, pl.ds(0, EARLY)], dq_all.at[:, pl.ds(0, EARLY)]),
        (dk_in.at[pl.ds(0, EARLY)], dk_all.at[pl.ds(0, EARLY)]),
        (dv_in.at[pl.ds(0, EARLY)], dv_all.at[pl.ds(0, EARLY)]),
        (og_in, og_ref),
    )

    @pl.when(step == 0)
    def _():
        for i, (source, target) in enumerate(brought):
            pltpu.make_async_copy(source, target, in_sems.at[i]).start()

    dq, dk, dv = pair_back(counts, *refs[0:7], out_ref)
    dq_ref[...] = dq
    dk_ref[...] = dk
    dv_ref[...] = dv

    rows = pl.ds(pl.multiple_of((step + FIRST) * PAIR, PAIR), PAIR)
    dq_all[:, rows] = dq
    dk_all[rows, :] = dk
    dv_all[rows, :] = dv

    def send(source, half, part):
        def copies(own):
            row = part if own else 2 + part
            for second in (1, 0):
                target = outs[2 * second + part] if own else outs[4 + second].at[part]
                sem = sems.at[2 * second + part] if own else sems.at[4 + second]

                def body(i, carry):
                    pltpu.make_async_copy(
                        source.at[table[row, i + 16 * second]], target.at[i], sem
                    ).start()
                    return carry

                lax.fori_loop(0, GROUPS // 2, body, 0)

        pl.when(core[0] == half)(lambda: copies(True))
        pl.when(core[0] != half)(lambda: copies(False))

    def padded(values):
        rows = values.reshape(GROUPS, ROWS, D)
        return jnp.concatenate([rows, jnp.zeros((GROUPS, 8, D), F32)], axis=1).astype(BF16)

    @pl.when(step == pl.num_programs(0) - 1)
    def _():
        for i, (source, target) in enumerate(brought):
            pltpu.make_async_copy(source, target, in_sems.at[i]).wait()
        send(og_ref, 1, 1)
        x = x_ref[...]
        d_q[...] = padded(dot_tn(dq_all[...], x))
        send(d_q, 0, 0)
        d_v[...] = padded(dot_nn(dv_all[...], x))
        send(d_v, 1, 0)
        query_sum = dot_nn(ones, dq_all[...])
        value_sum = dot_nt(ones, dv_all[...])
        rows8 = lax.broadcasted_iota(jnp.int32, (8, D), 0)
        offsets = vg_ref[0:8, :]
        offsets = jnp.where(
            rows8 == 0, query_sum[0:1, :], jnp.where(rows8 == 1, value_sum[0:1, :], offsets)
        )
        group = lax.broadcasted_iota(jnp.int32, (32, 8, D), 0)
        lane = lax.broadcasted_iota(jnp.int32, (32, 8, D), 2)
        chosen = jnp.where(lane // ROWS == group, offsets[None], 0.0)
        row = lax.broadcasted_iota(jnp.int32, (D, 128), 0)
        column = lax.broadcasted_iota(jnp.int32, (D, 128), 1)
        narrow = dot_nn(chosen.reshape(256, D).astype(BF16), (row % ROWS == column).astype(BF16))
        wide = jnp.broadcast_to(vg_ref[8:12, :][:, None, :], (4, 8, D))
        second = lax.broadcasted_iota(jnp.int32, (4, 8, D), 1)
        lane = lax.broadcasted_iota(jnp.int32, (4, 8, D), 2)
        chosen = jnp.where(lane // 96 == second, wide, 0.0).reshape(32, D)
        inner = dot_nn(chosen.astype(BF16), (row % 96 == column).astype(BF16))
        place = lax.broadcasted_iota(jnp.int32, (32, 8, 128), 1)
        inner = jnp.where(place == 0, inner[:, None, :], 0.0)
        small = jnp.concatenate(
            [narrow.reshape(32, 8, 128), inner, jnp.zeros((32, 8, D - 256), F32)], axis=2
        )
        d_k[...] = jnp.concatenate(
            [dot_nn(dk_all[...], x).reshape(GROUPS, ROWS, D), small], axis=1
        ).astype(BF16)
        send(d_k, 0, 1)
        for i in range(6):
            settle(outs[i], sems.at[i])


def rest(table, core, counts, queries, keys, values, mixed, mixed_low, probs, logits_cotangent, layer_input, held, og, vg):
    columns = pl.BlockSpec((TOKENS, PAIR), lambda i, *_: (0, i + FIRST))
    turned = pl.BlockSpec((PAIR, TOKENS), lambda i, *_: (i + FIRST, 0))
    logits = pl.BlockSpec((2, TOKENS, TOKENS), lambda i, *_: (i + FIRST, 0, 0))
    kept = jax.ShapeDtypeStruct((GROUPS // 2, 32, D), BF16)
    sent = jax.ShapeDtypeStruct((2, GROUPS // 2, 32, D), BF16)
    return pl.pallas_call(
        rest_kernel,
        grid_spec=pltpu.PrefetchScalarGridSpec(
            num_scalar_prefetch=3,
            grid=(H // 2 - FIRST,),
            in_specs=[columns] * 5
            + [logits] * 2
            + [pl.BlockSpec((16, D), lambda i, *_: (0, 0))]
            + [ANY] * 6,
            out_specs=[logits, columns, turned, turned] + [ANY] * 6,
            scratch_shapes=[
                pltpu.VMEM((TOKENS, D), BF16),
                pltpu.VMEM((GROUPS, 32, D), BF16),
                pltpu.VMEM((TOKENS, D), BF16),
                pltpu.VMEM((D, TOKENS), BF16),
                pltpu.VMEM((D, TOKENS), BF16),
                pltpu.VMEM((GROUPS, 32, D), BF16),
                pltpu.VMEM((GROUPS, 32, D), BF16),
                pltpu.VMEM((GROUPS, 32, D), BF16),
                pltpu.SemaphoreType.DMA((6,)),
                pltpu.SemaphoreType.DMA((5,)),
            ],
        ),
        out_shape=(
            jax.ShapeDtypeStruct((H, TOKENS, TOKENS), BF16),
            jax.ShapeDtypeStruct((TOKENS, D), BF16),
            jax.ShapeDtypeStruct((D, TOKENS), BF16),
            jax.ShapeDtypeStruct((D, TOKENS), BF16),
            kept,
            kept,
            kept,
            kept,
            sent,
            sent,
        ),
        input_output_aliases={13 + i: i for i in range(4)},
        compiler_params=pltpu.CompilerParams(vmem_limit_bytes=LIMIT),
        cost_estimate=pl.CostEstimate(flops=6 * 10**9, bytes_accessed=25 * 10**6, transcendentals=0),
        name="attend_back_rest",
    )(
        table,
        core,
        counts,
        queries,
        keys,
        values,
        mixed,
        mixed_low,
        probs,
        logits_cotangent,
        vg,
        layer_input,
        og,
        *held,
    )


def pack_kernel(core, *refs):
    query, key, value, output, inner, outer = refs[0:6]
    small = refs[6:15]
    mine_ref, other_ref, first, second = refs[15:19]
    first[...] = jnp.zeros_like(first)
    second[...] = jnp.zeros_like(second)
    first[0:6, :] = query[...].astype(F32)
    first[6:12, :] = key[...].astype(F32)
    first[12:36, :] = inner[...].astype(F32)
    for i, ref in enumerate(small):
        row, lane = 36 + i // 6, 128 * (i % 6)
        first[row : row + 1, lane : lane + ref.shape[1]] = ref[...].astype(F32)
    second[0:6, :] = value[...].astype(F32)
    second[6:12, :] = output[...].astype(F32)
    for i in range(4):
        second[12 + 6 * i : 18 + 6 * i, :] = outer[:, D * i : D * (i + 1)].astype(F32)

    @pl.when(core[0] == 0)
    def _():
        mine_ref[...] = first[...].astype(BF16)
        other_ref[...] = second[...].astype(BF16)

    @pl.when(core[0] != 0)
    def _():
        mine_ref[...] = second[...].astype(BF16)
        other_ref[...] = first[...].astype(BF16)


def pack(core, kernels, small):
    half = jax.ShapeDtypeStruct((40, D), BF16)
    return pl.pallas_call(
        pack_kernel,
        in_specs=[SMEM] + [VMEM] * 15,
        out_specs=[VMEM] * 2,
        out_shape=(half, half),
        scratch_shapes=[pltpu.VMEM((40, D), F32)] * 2,
        name="pack",
    )(core, *(kernel.T for kernel in kernels), *(v.reshape(1, -1) for v in small))


def finish_kernel(place, ff_own, ff_other, tail_own, tail_other, query, key, value, output, inner, outer, *small):
    def write(mine, ff_first, ff_second, tail_first, tail_second):
        rows = slice(6 * mine, 6 * mine + 6)
        for ref, part, skip in (
            (query, tail_first, 0),
            (key, tail_first, 24),
            (value, tail_second, 0),
            (output, tail_second, 24),
        ):
            ref[...] = part[skip + rows.start : skip + rows.stop, :]
        inner[...] = ff_first[24 * mine : 24 * mine + 24, :]
        for i in range(4):
            outer[:, D * i : D * (i + 1)] = ff_second[24 * i + rows.start : 24 * i + rows.stop, :]
        for i in range(8):
            small[i][...] = tail_first[48 + i : 49 + i, rows]
        small[8][...] = tail_first[48:49, 128 + 24 * mine : 152 + 24 * mine]

    for mine in range(4):

        @pl.when(place[0] == mine)
        def _():
            if mine < 2:
                write(mine, ff_own, ff_other, tail_own, tail_other)
            else:
                write(mine, ff_other, ff_own, tail_other, tail_own)


def finish(mine, ff_own, ff_other, tail_own, tail_other):
    narrow = jax.ShapeDtypeStruct((6, D), F32)
    outs = pl.pallas_call(
        finish_kernel,
        in_specs=[SMEM] + [VMEM] * 4,
        out_specs=[VMEM] * 15,
        out_shape=(
            narrow,
            narrow,
            narrow,
            narrow,
            jax.ShapeDtypeStruct((24, D), F32),
            jax.ShapeDtypeStruct((6, FF), F32),
        )
        + (jax.ShapeDtypeStruct((1, 6), F32),) * 8
        + (jax.ShapeDtypeStruct((1, 24), F32),),
        name="finish",
    )(mine.astype(jnp.int32).reshape(1), ff_own, ff_other, tail_own, tail_other)
    return tuple(out.T for out in outs[:6]) + tuple(out.reshape(-1) for out in outs[6:])


def gather_weights(core_table, kernels, vectors, inner_offset):
    core, low_x = lax.axis_index("c"), lax.axis_index("xl")
    mine = core * 2 + low_x
    own, other = pack(core_table, kernels, (*vectors, inner_offset))
    pieces = jnp.stack(
        [
            own,
            swap(own, "xl"),
            swap(other, "c"),
            lax.ppermute(other, ("c", "xl"), [(i, 3 - i) for i in range(4)]),
        ]
    )
    natural = jnp.concatenate(
        [lax.dynamic_slice_in_dim(pieces, mine ^ i, 1, axis=0) for i in range(4)], axis=0
    )
    first = core == 0
    near_a = natural[:, 0:6].reshape(ROWS, D)
    near_b = natural[:, 6:12].reshape(ROWS, D)
    inner = natural[:, 12:36].reshape(96, D)
    outer = natural[:, 12:36].reshape(4, 4, 6, D).transpose(1, 0, 2, 3).reshape(96, D)
    offsets = natural[:, 36:38].reshape(4, 12, 128)[:, 0:8, 0:6].transpose(1, 0, 2).reshape(8, ROWS)
    offsets = jnp.pad(offsets, ((0, 0), (0, 128 - ROWS)))
    wide_offset = jnp.pad(natural[:, 37, 256:280].reshape(1, 96), ((0, 7), (0, 32)))
    small = jnp.concatenate([offsets, wide_offset, jnp.zeros((8, D - 256), BF16)], axis=1)
    wide = jnp.where(first, inner, outer)
    block = jnp.concatenate([near_a, wide[0:48], near_b, small, wide[48:96]], axis=0)
    both = jnp.stack([block, exchange(block, STEPS_A[0])])
    part_a, part_b = both[:, 0:72], both[:, 72:152]
    for i in (1, 2):
        arrived_a, arrived_b = after((exchange(part_a, STEPS_A[i]), exchange(part_b, STEPS_B[i])))
        part_a = jnp.concatenate([part_a, arrived_a], axis=0)
        part_b = jnp.concatenate([part_b, arrived_b], axis=0)
    arrived_a, arrived_b = after((exchange(part_a, STEPS_A[3]), exchange(part_b, STEPS_B[3])))
    near_a = jnp.concatenate([part_a[:, 0:24], arrived_a[:, 0:24]], axis=0)
    near_b = jnp.concatenate([part_b[:, 0:32], arrived_b[:, 0:32]], axis=0)
    far_a = jnp.concatenate([part_a[:, 24:72], arrived_a[:, 24:72]], axis=0)
    far_b = jnp.concatenate([part_b[:, 32:80], arrived_b[:, 32:80]], axis=0)
    last_a, last_b = exchange(near_a, STEPS_A[4]), exchange(near_b, STEPS_B[4])
    far_a, far_b, last_a, last_b = after((far_a, far_b, last_a, last_b))
    near = (near_a, last_a, near_b, last_b)
    return near, tuple(swap(part, "c") for part in near), (far_a, far_b)


def after(values, *others):
    return lax.optimization_barrier((values, others))[0] if others else lax.optimization_barrier(values)


def add(first, second):
    return (first.astype(F32) + second.astype(F32)).astype(BF16)


def add3(first, second, third):
    return (first.astype(F32) + second.astype(F32) + third.astype(F32)).astype(BF16)


def split(*arrays):
    half = arrays[0].shape[0] // 2
    combine = add if len(arrays) == 2 else add3
    return combine(*(a[:half] for a in arrays)), combine(*(a[half:] for a in arrays))


def halve(total, step):
    return split(total[0], exchange(total[1], step))


def reduce_end(total_a, total_b):
    kept, sent = (
        jnp.concatenate([total_a[i].reshape(-1, D), total_b[i].reshape(-1, D)], axis=0) for i in range(2)
    )
    total = add(kept, exchange(sent, STEPS_A[0]))
    own = total.astype(F32) + swap(total, "xl").astype(F32)
    return own, swap(own, "c")


def body(
    layer_input,
    prior_logits,
    bucket_counts,
    output_cotangent,
    logits_cotangent,
    query_kernel,
    query_offset,
    key_kernel,
    value_kernel,
    value_offset,
    output_kernel,
    output_offset,
    first_gain,
    first_shift,
    inner_kernel,
    inner_offset,
    outer_kernel,
    outer_offset,
    second_gain,
    second_shift,
):
    core, low_x = lax.axis_index("c"), lax.axis_index("xl")
    mine = core * 2 + low_x
    table = jnp.stack(
        [
            position_groups(STEPS_A, core),
            position_groups(STEPS_B, core),
            position_groups(STEPS_A, 1 - core),
            position_groups(STEPS_B, 1 - core),
        ]
    )
    core_table = core.astype(jnp.int32).reshape(1)
    near, near_other, far = gather_weights(
        core_table,
        (query_kernel, key_kernel, value_kernel, output_kernel, inner_kernel, outer_kernel),
        (
            query_offset,
            value_offset,
            output_offset,
            first_gain,
            first_shift,
            outer_offset,
            second_gain,
            second_shift,
        ),
        inner_offset,
    )
    far_last = (exchange(far[0], STEPS_A[4]), exchange(far[1], STEPS_B[4]))
    far_other = [swap(far[0], "c"), None, swap(far[1], "c"), None]
    queries, keys, values, query_matrix, key_matrix, value_matrix, vectors = project(
        table, core_table, layer_input, near, near_other
    )
    raw_logits, probs, mixed = attend(bucket_counts, queries, keys, values, prior_logits, 0, 6, ())
    far_last, mixed = after((far_last, mixed))
    far_other[1], far_other[3] = swap(far_last[0], "c"), swap(far_last[1], "c")
    layer_output, first_slope, mixed_low, output_slope, vector_slopes, *ff = middle(
        table,
        core_table,
        layer_input,
        mixed,
        output_cotangent,
        vectors,
        near[2:4],
        near_other[2:4],
        (far[0], far_last[0], far[1], far_last[1]),
        far_other,
    )

    moved = swap(ff[5], "c")
    heads = (queries, keys, values, mixed, mixed_low, probs, logits_cotangent)
    held = attend_back(bucket_counts, *heads)
    moved, held = after((moved, held))
    moved_late = swap(ff[4], "c")
    sent_a, sent_b = add(ff[2], moved[0]), add(ff[3], moved[1])
    held, sent_a, sent_b = after((held, sent_a, sent_b))
    logits_slope, dq, dk, dv, *tail = rest(
        table, core_table, bucket_counts, *heads, layer_input, held, output_slope, vector_slopes
    )
    arrived_a, arrived_b = exchange(sent_a, STEPS_A[4]), exchange(sent_b, STEPS_B[4])
    arrived_a, arrived_b, tail = after((arrived_a, arrived_b, tuple(tail)))
    tail_moved = swap(tail[5], "c")
    ff_a = split(ff[0], moved_late[0], arrived_a)
    ff_b = split(ff[1], moved_late[1], arrived_b)
    tail_moved, ff_a, ff_b = after((tail_moved, ff_a, ff_b))
    late = swap(tail[4], "c")
    tail_sent = [
        add(tail[2][:, :ROWS], tail_moved[0][:, :ROWS]),
        add(tail[3], tail_moved[1]),
    ]
    (dq, dk, dv), tail_sent = after(((dq, dk, dv), tail_sent))
    input_slope = (
        first_slope + dot_nn(dq, query_matrix) + dot_tn(dk, key_matrix) + dot_tn(dv, value_matrix)
    ).astype(BF16)
    tail_arrived = after(
        (exchange(tail_sent[0], STEPS_A[4]), exchange(tail_sent[1], STEPS_B[4])), input_slope
    )
    tail_a = split(tail[0][:, :ROWS], late[0][:, :ROWS], tail_arrived[0])
    tail_b = split(tail[1], late[1], tail_arrived[1])
    for i in (3, 2, 1):
        arrived_a, arrived_b = after((exchange(tail_a[1], STEPS_A[i]), exchange(tail_b[1], STEPS_B[i])))
        tail_a, tail_b = split(tail_a[0], arrived_a), split(tail_b[0], arrived_b)
        ff_a, ff_b = halve(ff_a, STEPS_A[i]), halve(ff_b, STEPS_B[i])
    ff_sums = reduce_end(ff_a, ff_b)
    tail_sums = reduce_end(tail_a, tail_b)
    query_owned, key_owned, value_owned, output_owned, inner_owned, outer_owned, *small = finish(
        mine, *ff_sums, *tail_sums
    )

    return (
        layer_output,
        raw_logits,
        input_slope,
        logits_slope,
        query_owned,
        small[0],
        key_owned,
        value_owned,
        small[1],
        output_owned,
        small[2],
        small[3],
        small[4],
        inner_owned,
        small[8],
        outer_owned,
        small[5],
        small[6],
        small[7],
    )


def solution(mesh):
    fine = Mesh(mesh.devices.reshape(SIZES), AXES)
    rows = P(AXES, None)
    logits = P(None, AXES, None)
    columns = P(None, AXES)
    vector = P(AXES)
    return jax.shard_map(
        body,
        mesh=fine,
        in_specs=(
            rows,
            logits,
            rows,
            rows,
            logits,
            columns,
            vector,
            columns,
            columns,
            vector,
            columns,
            vector,
            vector,
            vector,
            columns,
            vector,
            columns,
            vector,
            vector,
            vector,
        ),
        out_specs=(
            rows,
            logits,
            rows,
            logits,
            columns,
            vector,
            columns,
            columns,
            vector,
            columns,
            vector,
            vector,
            vector,
            columns,
            vector,
            columns,
            vector,
            vector,
            vector,
        ),
        check_vma=False,
    )
```
